256 devices in a mesh: tile: 64 (over z, y_hi, x), copy: 4 (over y_lo, core).
Axes of the slice: x: 4, y: 4 (y_hi: 2, y_lo: 2; y = y_hi * 2 + y_lo), z: 8, core: 2. Of those that a mesh axis runs over, the one named last changes fastest.
Arguments:
- pair_rep: bfloat16 [1536, 1536, 128], P('tile', 'copy'), may hold values from -6 to 6
- single: bfloat16 [1536, 384], P('tile'), may hold values from -6 to 6
- atom_feat: bfloat16 [12288, 128], P('tile'), may hold values from -6 to 6
- coords: float32 [8, 3, 12288], P('copy', None, 'tile'), may hold values from -96 to 96
- levels: int32 [8], P('copy'), may hold values from 0 to 199
- window_offset: int32 [384], P('tile'), may hold values from 0 to 32
- atom_token: int32 [12288], P('tile'), may hold values from 0 to 1535, as said below
- trans_in: bfloat16 [128, 1024], replicated, may hold values from -0.5 to 0.5
- trans_out: bfloat16 [512, 128], replicated, may hold values from -0.25 to 0.25
- bias_weight: bfloat16 [128, 16], replicated, may hold values from -0.5 to 0.5
- single_weight: bfloat16 [384, 768], replicated, may hold values from -0.3125 to 0.3125
- coord_weight: float32 [3, 128], replicated, may hold values from -3.5 to 3.5
- atom_weight: bfloat16 [128, 384], replicated, as said below
- agg_weight: bfloat16 [128, 768], replicated, may hold values from -0.5 to 0.5
- token_weight: bfloat16 [768, 2304], replicated, as said below
- noise_weight: float32 [768], replicated, may hold values from -6 to 6
- cotangent: bfloat16 [8, 1536, 768], P('copy', 'tile'), may hold values from -6 to 6
Outputs:
- token_update: bfloat16 [8, 1536, 768], P('copy', 'tile')
- grad_pair: bfloat16 [1536, 1536, 128], P('tile', 'copy')
The draws below stay inside these ranges and needn't reach their ends.
Inputs may be any that keep to these rules, and one draw needn't show every extreme that they name: atom_token never falls; atoms k * 192 to (k + 1) * 192 - 1 belong to tokens k * 24 to (k + 1) * 24 - 1, and every token has one atom or more. `atom_weight`: columns are queries, keys and values in this order. `token_weight`: columns are queries, keys and values in this order.
All inputs are finite; a program needn't handle non-finite values.
Results may differ from the reference program's by a relative error of at most 0.007.
The reference program's roundings to bfloat16 on the way count: a program that leaves them out, or rounds other values in their place, can miss the bound.
Values may be sent and summed in bfloat16 or wider, within the bound.
No kernel may reach another device: no remote copies, remote signals or barrier semaphores. Data moves between devices by JAX's collectives and lax.ppermute only.
A program may use at most 128 MiB of HBM per device.

```python
import math
import jax
import jax.numpy as jnp
from jax import lax

TOK_DEV = 24
CP = 128
CS = 384
H = 16
HEAD = 48
A_HEADS = 4
A_HEAD = 32
Q_BLOCK = 32
K_WIN = 128
LEVELS = 200
CT = 768
CA = 128
FF_PAIR = 512
TOKENS = 1536
ATOM_DEV = 192
ATOMS = 12288
COPIES = 8


def draw_atom_token(key, part):
    key = jax.random.fold_in(key, 11)
    groups = TOKENS // TOK_DEV
    extra = jax.random.randint(key, (groups, ATOM_DEV - TOK_DEV), 0, TOK_DEV).astype(jnp.int32)
    base = jnp.broadcast_to(jnp.arange(TOK_DEV, dtype=jnp.int32)[None, :], (groups, TOK_DEV))
    local = jnp.sort(jnp.concatenate([base, extra], axis=1), axis=1)
    offsets = TOK_DEV * jnp.arange(groups, dtype=jnp.int32)[:, None]
    return (local + offsets).reshape(-1)


def draw_atom_weight(key, part):
    key = jax.random.fold_in(key, 23)
    return (jax.random.normal(key, (CA, 3 * CA), jnp.float32) * CA ** (-0.5)).astype(jnp.bfloat16)


def draw_token_weight(key, part):
    key = jax.random.fold_in(key, 37)
    return (jax.random.normal(key, (CT, 3 * CT), jnp.float32) * CT ** (-0.5)).astype(jnp.bfloat16)


def place_ends(entries, own_key, smallest, high):
    longest = entries.shape.index(max(entries.shape))
    spots = []
    for shift in (0, 1):
        where = [jax.random.randint(jax.random.fold_in(own_key, axis), (), 0, length) for axis, length in enumerate(entries.shape)]
        where[longest] = (where[longest] + shift) % entries.shape[longest]
        spots.append(tuple(where))
    return entries.at[spots[0]].set(smallest).at[spots[1]].set(high)


def shard_levels(key, extent, shards, low, high):
    def one(axis_at, blocks):
        heights = jax.random.uniform(jax.random.fold_in(jax.random.fold_in(key, 6), axis_at), (blocks,), jnp.float32, low / len(shards), high / len(shards))
        return jnp.repeat(jnp.exp(heights), extent[axis_at] // blocks).reshape((-1,) + (1,) * (len(extent) - axis_at - 1))

    level = one(*shards[0])
    for cut in shards[1:]:
        level = level * one(*cut)
    return level


def scatter_about(own_key, shape, scale, bound, cuts=(), kind=jnp.bfloat16):
    gain = shard_levels(own_key, shape, cuts, -0.22, 0.18) if cuts else 1.0
    array = jax.random.normal(own_key, shape, jnp.float32) * scale * gain
    return jnp.minimum(jnp.maximum(array, -bound), bound).astype(kind)


def setup_inputs(seed: int = 0) -> dict:
    seeds = jax.random.split(jax.random.key(seed), 18)
    pair_rep = scatter_about(seeds[0], (TOKENS, TOKENS, CP), 1.0, 6.0, ((0, 64), (1, 4)))
    single = scatter_about(seeds[1], (TOKENS, CS), 1.0, 6.0, ((0, 64),))
    atom_feat = scatter_about(seeds[2], (ATOMS, CA), 1.0, 6.0, ((0, 64),))
    coords = scatter_about(seeds[3], (COPIES, 3, ATOMS), 16.0, 96.0, ((0, 4), (2, 64)), jnp.float32)
    levels = place_ends(jax.random.randint(seeds[4], (COPIES,), 0, LEVELS), jax.random.fold_in(seeds[4], 1), 0, LEVELS - 1).astype(jnp.int32)
    window_offset = place_ends(jax.random.randint(seeds[5], (ATOMS // Q_BLOCK,), 0, Q_BLOCK + 1), jax.random.fold_in(seeds[5], 1), 0, Q_BLOCK).astype(jnp.int32)
    atom_token = draw_atom_token(jax.random.fold_in(seeds[17], 71), 0)
    trans_in = scatter_about(seeds[7], (CP, 2 * FF_PAIR), CP ** -0.5, 0.5)
    trans_out = scatter_about(seeds[8], (FF_PAIR, CP), FF_PAIR ** -0.5, 0.25)
    bias_weight = scatter_about(seeds[9], (CP, H), CP ** -0.5, 0.5)
    single_weight = scatter_about(seeds[10], (CS, CT), CS ** -0.5, 0.3125)
    coord_weight = scatter_about(seeds[11], (3, CA), 3 ** -0.5, 3.5, (), jnp.float32)
    atom_weight = draw_atom_weight(jax.random.fold_in(seeds[17], 71), 0)
    agg_weight = scatter_about(seeds[13], (CA, CT), CA ** -0.5, 0.5)
    token_weight = draw_token_weight(jax.random.fold_in(seeds[17], 71), 0)
    noise_weight = scatter_about(seeds[15], (CT,), 1.0, 6.0, (), jnp.float32)
    cotangent = scatter_about(seeds[16], (COPIES, TOKENS, CT), 1.0, 6.0, ((0, 4), (1, 64)))
    return dict(pair_rep=pair_rep, single=single, atom_feat=atom_feat, coords=coords, levels=levels, window_offset=window_offset, atom_token=atom_token, trans_in=trans_in, trans_out=trans_out, bias_weight=bias_weight, single_weight=single_weight, coord_weight=coord_weight, atom_weight=atom_weight, agg_weight=agg_weight, token_weight=token_weight, noise_weight=noise_weight, cotangent=cotangent)


epsilon = 1e-05
sigma_data = 16.0
sigma_top = 160.0
sigma_low = 0.0004
rho_power = 7.0
excluded = -1e+30
highest_precision = lax.Precision.HIGHEST

def norm_parts(value):
    average = lax.optimization_barrier(jnp.mean(value, axis=-1, keepdims=True))
    centred = value - average
    spread = lax.optimization_barrier(jnp.mean(centred * centred, axis=-1, keepdims=True))
    scale = lax.rsqrt(spread + epsilon)
    return (centred * scale, scale)

def noise_scales(levels):
    fraction = levels.astype(jnp.float32) / LEVELS
    highest = sigma_top ** (1.0 / rho_power)
    lowest = sigma_low ** (1.0 / rho_power)
    sigma = sigma_data * (highest + fraction * (lowest - highest)) ** rho_power
    input_scale = lax.rsqrt(sigma * sigma + sigma_data * sigma_data)
    noise_code = 0.25 * jnp.log(sigma / sigma_data)
    return (input_scale, noise_code)

def soft_weights(scores):
    highest = lax.optimization_barrier(jnp.max(scores, axis=-1, keepdims=True))
    spread = jnp.exp(scores - highest)
    return spread / lax.optimization_barrier(jnp.sum(spread, axis=-1, keepdims=True))

def condition_pair(row_block, trans_in, trans_out):
    normal, _ = norm_parts(row_block.astype(jnp.float32))
    normed = normal.astype(jnp.bfloat16)
    gate_up = jnp.einsum('ijc,cf->ijf', normed.astype(jnp.float32), trans_in.astype(jnp.float32))
    inner = trans_out.shape[0]
    hidden = (jax.nn.silu(gate_up[..., :inner]) * gate_up[..., inner:]).astype(jnp.bfloat16)
    pair_delta = jnp.einsum('ijf,fc->ijc', hidden.astype(jnp.float32), trans_out.astype(jnp.float32))
    return (row_block.astype(jnp.float32) + pair_delta).astype(jnp.bfloat16)

def copy_tokens(coords_one, input_scale, noise_code, atom_feat, coord_weight, atom_weight, window_offset, atom_token, agg_weight, single_term, noise_weight, token_weight):
    scaled = coords_one * input_scale
    atoms = atom_feat.astype(jnp.float32)
    for axis_index in range(3):
        atoms = atoms + scaled[axis_index][:, None] * coord_weight[axis_index][None, :]
    atom_normal, _ = norm_parts(atoms)
    atom_proj = jnp.dot(atom_normal.astype(jnp.bfloat16), atom_weight, preferred_element_type=jnp.float32)
    width = A_HEADS * A_HEAD
    rim_width = K_WIN // 2
    blocks = ATOMS // Q_BLOCK
    queries = atom_proj[:, :width].reshape(blocks, Q_BLOCK, A_HEADS, A_HEAD)
    padded = jnp.pad(atom_proj[:, width:], ((rim_width, rim_width), (0, 0)))
    window_index = Q_BLOCK * jnp.arange(blocks, dtype=jnp.int32)[:, None] + window_offset[:, None] + jnp.arange(K_WIN, dtype=jnp.int32)[None, :]
    position = window_index - rim_width
    inside = (position >= 0) & (position < ATOMS)
    window = padded[window_index]
    window_keys = window[..., :width].reshape(blocks, K_WIN, A_HEADS, A_HEAD)
    values = window[..., width:].reshape(blocks, K_WIN, A_HEADS, A_HEAD)
    scores = jnp.einsum('bqhd,bkhd->bhqk', queries, window_keys, precision=highest_precision) / math.sqrt(A_HEAD)
    scores = jnp.where(inside[:, None, None, :], scores, excluded)
    soft_probs = soft_weights(scores).astype(jnp.bfloat16)
    attended = jnp.einsum('bhqk,bkhd->bqhd', soft_probs.astype(jnp.float32), values, precision=highest_precision).reshape(ATOMS, width)
    atom_out = (atoms + attended).astype(jnp.bfloat16)
    hidden = jax.nn.relu(jnp.dot(atom_out, agg_weight, preferred_element_type=jnp.float32))
    token_sums = jax.ops.segment_sum(hidden, atom_token, num_segments=TOKENS)
    counts = jax.ops.segment_sum(jnp.ones((ATOMS,), jnp.float32), atom_token, num_segments=TOKENS)
    token_feat = token_sums / counts[:, None]
    token_normal, _ = norm_parts(token_feat)
    token_in = token_normal + single_term + noise_code * noise_weight[None, :]
    return jnp.dot(token_in, token_weight.astype(jnp.float32), precision=highest_precision)

def reference(pair_rep, single, atom_feat, coords, levels, window_offset, atom_token, trans_in, trans_out, bias_weight, single_weight, coord_weight, atom_weight, agg_weight, token_weight, noise_weight, cotangent):
    width = H * HEAD
    input_scale, noise_code = noise_scales(levels)
    single_term = jnp.dot(single, single_weight, preferred_element_type=jnp.float32)

    def one_copy(item):
        return copy_tokens(item[0], item[1], item[2], atom_feat, coord_weight, atom_weight, window_offset, atom_token, agg_weight, single_term, noise_weight, token_weight)
    token_proj = lax.map(one_copy, (coords, input_scale, noise_code))
    key_heads = token_proj[..., width:2 * width].reshape(COPIES, TOKENS, H, HEAD)
    value_heads = token_proj[..., 2 * width:].reshape(COPIES, TOKENS, H, HEAD)
    blocks = TOKENS // TOK_DEV
    pair_blocks = pair_rep.reshape(blocks, TOK_DEV, TOKENS, CP)
    query_blocks = token_proj[..., :width].reshape(COPIES, blocks, TOK_DEV, width).transpose(1, 0, 2, 3)
    grad_blocks = cotangent.reshape(COPIES, blocks, TOK_DEV, width).transpose(1, 0, 2, 3)
    bias_float = bias_weight.astype(jnp.float32)

    def row_pass(item):
        pair_rows, query_rows, grad_rows = item
        pair_cond = condition_pair(pair_rows, trans_in, trans_out)
        cond_normal, cond_scale = norm_parts(pair_cond.astype(jnp.float32))
        cond_normed = cond_normal.astype(jnp.bfloat16)
        head_bias = jnp.einsum('ijc,ch->hij', cond_normed.astype(jnp.float32), bias_float, precision=highest_precision)
        query_heads = query_rows.reshape(COPIES, TOK_DEV, H, HEAD)
        scores = jnp.einsum('nihd,njhd->nhij', query_heads, key_heads, precision=highest_precision) / math.sqrt(HEAD)
        scores = scores + head_bias[None]
        exact = soft_weights(scores)
        soft_probs = exact.astype(jnp.bfloat16)
        update = jnp.einsum('nhij,njhd->nihd', soft_probs.astype(jnp.float32), value_heads, precision=highest_precision)
        update = update.reshape(COPIES, TOK_DEV, width).astype(jnp.bfloat16)
        cot_heads = grad_rows.reshape(COPIES, TOK_DEV, H, HEAD).astype(jnp.float32)
        prob_grad = jnp.einsum('nihd,njhd->nhij', cot_heads, value_heads, precision=highest_precision)
        inner = lax.optimization_barrier(jnp.sum(exact * prob_grad, axis=-1, keepdims=True))
        bias_grad = lax.optimization_barrier(jnp.sum(exact * (prob_grad - inner), axis=0))
        grad_normal = jnp.einsum('hij,ch->ijc', bias_grad, bias_float, precision=highest_precision)
        gradient = grad_normal - lax.optimization_barrier(jnp.mean(grad_normal, axis=-1, keepdims=True)) - cond_normal * lax.optimization_barrier(jnp.mean(grad_normal * cond_normal, axis=-1, keepdims=True))
        return (update, (gradient * cond_scale).astype(jnp.bfloat16))
    updates, gradients = lax.map(row_pass, (pair_blocks, query_blocks, grad_blocks))
    token_update = updates.transpose(1, 0, 2, 3).reshape(COPIES, TOKENS, width)
    grad_pair = gradients.reshape(TOKENS, TOKENS, CP)
    return (token_update, grad_pair)
```

```python
import math

import jax
import jax.numpy as jnp
from jax import lax
from jax.experimental import pallas as pl
from jax.experimental.pallas import tpu as pltpu
from jax.sharding import Mesh, PartitionSpec as P

A_HEAD = 32
A_HEADS = 4
Q_BLOCK = 32
K_WIN = 128
LEVELS = 200
HEAD = 48
H = 16

epsilon = 1e-05
sigma_data = 16.0
sigma_top = 160.0
sigma_low = 0.0004
rho_power = 7.0
excluded = -1e30
TILE = ("z", "g")
COPY = ("ylo", "core")
PLANE = ("g", "ylo")
BF = jnp.bfloat16
F32 = jnp.float32
NT = (((1,), (1,)), ((), ()))
NN = (((1,), (0,)), ((), ()))
TN = (((0,), (0,)), ((), ()))


def norm_parts(value):
    average = jnp.mean(value, axis=-1, keepdims=True)
    centred = value - average
    spread = jnp.mean(centred * centred, axis=-1, keepdims=True)
    scale = lax.rsqrt(spread + epsilon)
    return (centred * scale, scale)


def noise_scales(levels):
    fraction = levels.astype(F32) / LEVELS
    highest = sigma_top ** (1.0 / rho_power)
    lowest = sigma_low ** (1.0 / rho_power)
    sigma = sigma_data * (highest + fraction * (lowest - highest)) ** rho_power
    input_scale = lax.rsqrt(sigma * sigma + sigma_data * sigma_data)
    noise_code = 0.25 * jnp.log(sigma / sigma_data)
    return (input_scale, noise_code)


def dot(a, b, dims=NN):
    return lax.dot_general(a, b, dims, preferred_element_type=F32)


def two_parts(value):
    high = value.astype(BF)
    low = (value - high.astype(F32)).astype(BF)
    return high, low


def three_parts(value):
    high = value.astype(BF)
    rest = value - high.astype(F32)
    middle = rest.astype(BF)
    low = (rest - middle.astype(F32)).astype(BF)
    return high, middle, low


def atom_kernel(
    place, offsets, noise, low, high, normed, atoms, atom_weight, agg_weight, local_token,
    single, single_weight, noise_weight, token_weight, cotangent, out
):
    tile = place[0]
    copies, rows, width = normed.shape
    blocks = rows // Q_BLOCK
    span = K_WIN + Q_BLOCK
    rim = K_WIN // 2
    total = 64 * rows
    tok_rows = single.shape[0]
    head_of = lax.broadcasted_iota(jnp.int32, (Q_BLOCK, width), 1) // A_HEAD
    reach = lax.broadcasted_iota(jnp.int32, (1, span), 1)
    member = (
        lax.broadcasted_iota(jnp.int32, (tok_rows, rows), 0) == local_token[...]
    ).astype(F32)
    counts = jnp.sum(member, axis=1, keepdims=True)
    member = member.astype(BF)
    single_term = dot(single[...], single_weight[...])
    token_in = []
    for n in range(copies):
        ext = jnp.concatenate([low[n], normed[n], high[n]], axis=0)
        proj = dot(ext, atom_weight[...])
        queries = proj[rim : rim + rows, :width] * (1.0 / math.sqrt(A_HEAD))
        key_high, key_low = two_parts(proj[:, width : 2 * width])
        val_high, val_low = two_parts(proj[:, 2 * width :])
        keys = jnp.concatenate([key_high, key_low], axis=1)
        vals = jnp.concatenate([val_high, val_low], axis=1)
        parts = []
        for b in range(blocks):
            first = b * Q_BLOCK
            block = queries[first : first + Q_BLOCK]
            spread = jnp.concatenate(
                [jnp.where(head_of == h, block, 0.0) for h in range(A_HEADS)], axis=0
            )
            q_high, q_low = two_parts(spread)
            scores = dot(
                jnp.concatenate([q_high, q_high], axis=1), keys[first : first + span], NT
            ) + dot(q_low, key_high[first : first + span], NT)
            offset = offsets[b]
            position = tile * rows + first - rim + reach
            inside = (
                (reach >= offset)
                & (reach < offset + K_WIN)
                & (position >= 0)
                & (position < total)
            )
            scores = jnp.where(inside, scores, excluded)
            top = jnp.max(scores, axis=-1, keepdims=True)
            weights = jnp.exp(scores - top)
            weights = weights / jnp.sum(weights, axis=-1, keepdims=True)
            mixed = dot(weights.astype(BF), vals[first : first + span])
            mixed = mixed[:, :width] + mixed[:, width:]
            gathered = jnp.where(head_of == 0, mixed[:Q_BLOCK], 0.0)
            for h in range(1, A_HEADS):
                gathered += jnp.where(
                    head_of == h, mixed[h * Q_BLOCK : (h + 1) * Q_BLOCK], 0.0
                )
            parts.append(gathered)
        atom_out = (atoms[n] + jnp.concatenate(parts, axis=0)).astype(BF)
        hidden = jnp.maximum(dot(atom_out, agg_weight[...]), 0.0)
        sums = 0.0
        for part in three_parts(hidden):
            sums = sums + dot(member, part)
        token_normal, _ = norm_parts(sums / counts)
        token_in.append(token_normal + single_term + noise[n] * noise_weight[...])
    token_in = jnp.concatenate(token_in, axis=0)
    count = token_in.shape[0]
    stacked = jnp.concatenate(three_parts(token_in), axis=0)
    proj = dot(stacked, token_weight[...])
    proj = proj[:count] + proj[count : 2 * count] + proj[2 * count :]
    wide = H * HEAD
    cot = jnp.concatenate([cotangent[n].astype(F32) for n in range(copies)], axis=0)
    blank = jnp.zeros((count, 128 - 2 * HEAD), F32)
    for h in range(H):
        at = h * HEAD
        out[h, :, :128] = jnp.concatenate(
            [proj[:, at : at + HEAD] * (1.0 / math.sqrt(HEAD)), cot[:, at : at + HEAD], blank], axis=1
        )
        out[h, :, 128:] = jnp.concatenate(
            [
                proj[:, wide + at : wide + at + HEAD],
                proj[:, 2 * wide + at : 2 * wide + at + HEAD],
                blank,
            ],
            axis=1,
        )


def pair_kernel(pair, trans_in, trans_out, bias_weight_t, cond_out, bias_out):
    inner = trans_out.shape[0]
    for i in range(pair.shape[0]):
        row = pair[i].astype(F32)
        normal, _ = norm_parts(row)
        gate_up = dot(normal.astype(BF), trans_in[...])
        gate = gate_up[:, :inner]
        half = 0.5 * gate
        hidden = ((half + half * jnp.tanh(half)) * gate_up[:, inner:]).astype(BF)
        cond = (row + dot(hidden, trans_out[...])).astype(BF)
        cond_out[i] = cond
        normal, _ = norm_parts(cond.astype(F32))
        bias_out[:, i, :] = dot(bias_weight_t[...], normal.astype(BF), NT)


def attend_kernel(place, queries, kv, bias_mine, bias_other, update, grad_mine, grad_other):
    core = place[0]
    blocks = [core, 2 + core, 1 - core, 3 - core]
    rows = 192
    cols = 384
    tok = 24
    lane = lax.broadcasted_iota(jnp.int32, (1, 128), 1)
    is_key = lane < HEAD
    is_value = (lane >= HEAD) & (lane < 2 * HEAD)
    bias = jnp.concatenate(
        [
            jnp.concatenate(
                [
                    (bias_mine if c < 2 else bias_other)[2 * g + c % 2]
                    for c in range(4)
                ],
                axis=1,
            )
            for g in range(8)
        ],
        axis=0,
    )
    grad = None
    for y in range(2):
        for p in range(2):
            query = jnp.concatenate(
                [queries[2 * g + y, p * tok : (p + 1) * tok, :128] for g in range(8)], axis=0
            )
            q_high, q_low = two_parts(jnp.where(is_key, query, 0.0))
            cot = jnp.where(is_value, query, 0.0).astype(BF)
            tokens = []
            for c in blocks:
                for z in range(2):
                    for g in range(8):
                        tokens.append(kv[2 * c + z, 2 * g + y, p * tok : (p + 1) * tok, :])
            high, low = two_parts(jnp.concatenate(tokens, axis=0))
            both = jnp.concatenate([high, low], axis=1)
            scores = (
                dot(jnp.concatenate([q_high, q_high], axis=1), both, NT)
                + dot(q_low, high, NT)
                + bias
            )
            top = jnp.max(scores, axis=-1, keepdims=True)
            weights = jnp.exp(scores - top)
            weights = weights * (1.0 / jnp.sum(weights, axis=-1, keepdims=True))
            mixed = dot(weights.astype(BF), both)
            mixed = mixed[:, :128] + mixed[:, 128:]
            for g in range(8):
                update[2 * g + y, p * tok : (p + 1) * tok, :] = mixed[g * tok : (g + 1) * tok]
            term = weights * dot(jnp.concatenate([cot, cot], axis=1), both, NT)
            term = term - weights * jnp.sum(term, axis=-1, keepdims=True)
            grad = term if grad is None else grad + term
    for g in range(8):
        for c in range(4):
            (grad_mine if c < 2 else grad_other)[2 * g + c % 2] = grad[
                g * tok : (g + 1) * tok, c * cols : (c + 1) * cols
            ]


def grad_kernel(grad, cond, weight_parts, out):
    for i in range(cond.shape[0]):
        high, middle, low = three_parts(grad[:, i, :])
        stacked = jnp.concatenate([high, middle, low, high, middle], axis=0)
        grad_normal = dot(stacked, weight_parts[...], TN)
        normal, scale = norm_parts(cond[i].astype(F32))
        shared = jnp.mean(grad_normal * normal, axis=-1, keepdims=True)
        out[i] = ((grad_normal - normal * shared) * scale).astype(BF)


def params(**more):
    return pltpu.CompilerParams(vmem_limit_bytes=56 * 1024 * 1024, **more)


VMEM = pl.BlockSpec(memory_space=pltpu.VMEM)
SMEM = pl.BlockSpec(memory_space=pltpu.SMEM)


def on_device(
    pair_rep,
    single,
    atom_feat,
    coords,
    levels,
    window_offset,
    atom_token,
    trans_in,
    trans_out,
    bias_weight,
    single_weight,
    coord_weight,
    atom_weight,
    agg_weight,
    token_weight,
    noise_weight,
    cotangent,
):
    tile_index = lax.axis_index(TILE).astype(jnp.int32)
    core_index = lax.axis_index("core").astype(jnp.int32)
    copies, tok_rows, width = cotangent.shape
    atom_rows, atom_width = atom_feat.shape
    cols = pair_rep.shape[1]
    rim = K_WIN // 2
    input_scale, noise_code = noise_scales(levels)
    scaled = coords * input_scale[:, None, None]
    atoms = atom_feat.astype(F32)[None]
    for axis_index in range(3):
        atoms = atoms + scaled[:, axis_index, :, None] * coord_weight[axis_index][None, None, :]
    atom_normal, _ = norm_parts(atoms)
    normed = atom_normal.astype(BF)
    forward = [(i, i + 1) for i in range(63)]
    backward = [(i + 1, i) for i in range(63)]
    low = lax.ppermute(normed[:, atom_rows - rim :], TILE, forward)
    high = lax.ppermute(normed[:, :rim], TILE, backward)
    local_token = (atom_token - tile_index * tok_rows)[None, :]
    packed = pl.pallas_call(
        atom_kernel,
        out_shape=jax.ShapeDtypeStruct((H, copies * tok_rows, 256), F32),
        in_specs=[SMEM] * 3 + [VMEM] * 12,
        out_specs=VMEM,
        compiler_params=params(),
        cost_estimate=pl.CostEstimate(flops=3_000_000_000, bytes_accessed=6_000_000, transcendentals=0),
        name="atom_stage",
    )(
        tile_index[None], window_offset, noise_code, low, high, normed, atoms, atom_weight, agg_weight,
        local_token, single, single_weight, noise_weight[None, :], token_weight, cotangent,
    )
    packed = lax.all_to_all(packed, PLANE, 0, 0, tiled=True)
    kv = lax.all_gather(packed[:, :, 128:], "z", axis=0)

    step = 8
    bias_t = bias_weight.T
    cond, bias = pl.pallas_call(
        pair_kernel,
        grid=(tok_rows // step,),
        out_shape=(
            jax.ShapeDtypeStruct(pair_rep.shape, BF),
            jax.ShapeDtypeStruct((H, tok_rows, cols), F32),
        ),
        in_specs=[
            pl.BlockSpec((step, cols, 128), lambda i: (i, 0, 0)),
            pl.BlockSpec(trans_in.shape, lambda i: (0, 0)),
            pl.BlockSpec(trans_out.shape, lambda i: (0, 0)),
            pl.BlockSpec(bias_t.shape, lambda i: (0, 0)),
        ],
        out_specs=(
            pl.BlockSpec((step, cols, 128), lambda i: (i, 0, 0)),
            pl.BlockSpec((H, step, cols), lambda i: (0, i, 0)),
        ),
        compiler_params=params(),
        cost_estimate=pl.CostEstimate(flops=4_000_000_000, bytes_accessed=6_000_000, transcendentals=5_000_000),
        name="pair_transition",
    )(pair_rep, trans_in, trans_out, bias_t)
    bias_mine = lax.all_to_all(bias, PLANE, 0, 0, tiled=True)
    swap = [(0, 1), (1, 0)]
    bias_other = lax.ppermute(bias_mine, "core", swap)

    update, grad_mine, grad_other = pl.pallas_call(
        attend_kernel,
        out_shape=(
            jax.ShapeDtypeStruct((H, copies * tok_rows, 128), F32),
            jax.ShapeDtypeStruct((H, tok_rows, cols), F32),
            jax.ShapeDtypeStruct((H, tok_rows, cols), F32),
        ),
        in_specs=[SMEM] + [VMEM] * 4,
        out_specs=(VMEM, VMEM, VMEM),
        compiler_params=params(),
        cost_estimate=pl.CostEstimate(flops=4_000_000_000, bytes_accessed=8_000_000, transcendentals=1_200_000),
        name="token_attention",
    )(core_index[None], packed, kv, bias_mine, bias_other)
    grad = grad_mine + lax.ppermute(grad_other, "core", swap)
    grad = lax.all_to_all(grad, PLANE, 0, 0, tiled=True)
    update = update[:, :, HEAD : 2 * HEAD].astype(BF)
    update = lax.all_to_all(update, PLANE, 0, 0, tiled=True)
    update = update.reshape(H, copies, tok_rows, HEAD).transpose(1, 2, 0, 3)
    update = update.reshape(copies, tok_rows, width)

    weight = bias_weight.astype(F32)
    weight = (weight - jnp.mean(weight, axis=0, keepdims=True)).T
    w_high, w_low = two_parts(weight)
    weight_parts = jnp.concatenate([w_high, w_high, w_high, w_low, w_low], axis=0)
    gradient = pl.pallas_call(
        grad_kernel,
        grid=(tok_rows // step,),
        out_shape=jax.ShapeDtypeStruct(pair_rep.shape, BF),
        in_specs=[
            pl.BlockSpec((H, step, cols), lambda i: (0, i, 0)),
            pl.BlockSpec((step, cols, 128), lambda i: (i, 0, 0)),
            pl.BlockSpec(weight_parts.shape, lambda i: (0, 0)),
        ],
        out_specs=pl.BlockSpec((step, cols, 128), lambda i: (i, 0, 0)),
        compiler_params=params(),
        cost_estimate=pl.CostEstimate(flops=400_000_000, bytes_accessed=6_000_000, transcendentals=0),
        name="pair_gradient",
    )(grad, cond, weight_parts)
    return (update, gradient)


def solution(mesh):
    fine = Mesh(mesh.devices.reshape(8, 8, 2, 2), ("z", "g", "ylo", "core"))
    placed = (
        P(TILE, COPY, None),
        P(TILE, None),
        P(TILE, None),
        P(COPY, None, TILE),
        P(COPY),
        P(TILE),
        P(TILE),
        P(),
        P(),
        P(),
        P(),
        P(),
        P(),
        P(),
        P(),
        P(),
        P(COPY, TILE, None),
    )
    return jax.shard_map(
        on_device,
        mesh=fine,
        in_specs=placed,
        out_specs=(P(COPY, TILE, None), P(TILE, COPY, None)),
        check_vma=False,
    )
```

```python
import math

import jax
import jax.numpy as jnp
from jax import lax
from jax.experimental import pallas as pl
from jax.experimental.pallas import tpu as pltpu
from jax.sharding import Mesh, PartitionSpec as P

A_HEAD = 32
A_HEADS = 4
Q_BLOCK = 32
K_WIN = 128
LEVELS = 200
HEAD = 48
H = 16

epsilon = 1e-05
sigma_data = 16.0
sigma_top = 160.0
sigma_low = 0.0004
rho_power = 7.0
excluded = -1e30
TILE = ("z", "g")
COPY = ("ylo", "core")
PLANE = ("g", "ylo")
BF = jnp.bfloat16
F32 = jnp.float32
NT = (((1,), (1,)), ((), ()))
NN = (((1,), (0,)), ((), ()))
TN = (((0,), (0,)), ((), ()))


def norm_parts(value):
    average = jnp.mean(value, axis=-1, keepdims=True)
    centred = value - average
    spread = jnp.mean(centred * centred, axis=-1, keepdims=True)
    scale = lax.rsqrt(spread + epsilon)
    return (centred * scale, scale)


def noise_parts(level):
    fraction = jnp.full((1, 128), level, jnp.int32).astype(F32) / LEVELS
    highest = sigma_top ** (1.0 / rho_power)
    lowest = sigma_low ** (1.0 / rho_power)
    root = highest + fraction * (lowest - highest)
    square = root * root
    sigma = sigma_data * (square * square * square * root)
    input_scale = lax.rsqrt(sigma * sigma + sigma_data * sigma_data)
    noise_code = 0.25 * jnp.log(sigma / sigma_data)
    return (input_scale, noise_code)


def dot(a, b, dims=NN):
    return lax.dot_general(a, b, dims, preferred_element_type=F32)


def two_parts(value):
    high = value.astype(BF)
    low = (value - high.astype(F32)).astype(BF)
    return high, low


def three_parts(value):
    high = value.astype(BF)
    rest = value - high.astype(F32)
    middle = rest.astype(BF)
    low = (rest - middle.astype(F32)).astype(BF)
    return high, middle, low


def grid_scale(top):
    top = jnp.maximum(top, 1e-30)
    power = jnp.ceil(jnp.log2(top))
    steps = jnp.ceil(top * jnp.exp2(13.0 - power)) + 1.0
    return steps, power


def scale_value(steps, power):
    return steps * jnp.exp2(power - 13.0) * (1.0 / 32767.0)


def whole(value):
    return jnp.round(value).astype(jnp.int32)


def start_kernel(levels, feat, coords, coord_weight, atoms_out, normed_out, first_out, last_out):
    rows = feat.shape[0]
    rim = K_WIN // 2
    for n in range(coords.shape[0]):
        input_scale, _ = noise_parts(levels[n])
        scaled = coords[n] * input_scale[:, :1]
        atoms = feat[...].astype(F32) + lax.dot_general(
            scaled, coord_weight[...], TN, precision=lax.Precision.HIGHEST, preferred_element_type=F32
        )
        normal, _ = norm_parts(atoms)
        normal = normal.astype(BF)
        atoms_out[n] = atoms
        normed_out[n] = normal
        first_out[n] = normal[:rim]
        last_out[n] = normal[rows - rim :]


def atom_kernel(
    place, offsets, levels, low, high, normed, atoms, atom_weight, agg_weight, atom_token,
    single, single_weight, noise_weight, token_weight, cotangent, out
):
    tile = place[0]
    copies, rows, width = normed.shape
    blocks = rows // Q_BLOCK
    span = K_WIN + Q_BLOCK
    rim = K_WIN // 2
    total = 64 * rows
    tok_rows = single.shape[0]
    head_of = lax.broadcasted_iota(jnp.int32, (Q_BLOCK, width), 1) // A_HEAD
    reach = lax.broadcasted_iota(jnp.int32, (1, span), 1)
    local_token = atom_token[...].reshape(1, rows) - tile * tok_rows
    member = (lax.broadcasted_iota(jnp.int32, (tok_rows, rows), 0) == local_token).astype(F32)
    counts = jnp.sum(member, axis=1, keepdims=True)
    member = member.astype(BF)
    single_term = dot(single[...], single_weight[...])
    noise_row = noise_weight[...].reshape(1, noise_weight.shape[0])
    token_in = []
    for n in range(copies):
        ext = jnp.concatenate([low[n], normed[n], high[n]], axis=0)
        proj = dot(ext, atom_weight[...])
        queries = proj[rim : rim + rows, :width] * (1.0 / math.sqrt(A_HEAD))
        key_high, key_low = two_parts(proj[:, width : 2 * width])
        val_high, val_low = two_parts(proj[:, 2 * width :])
        keys = jnp.concatenate([key_high, key_low], axis=1)
        vals = jnp.concatenate([val_high, val_low], axis=1)
        parts = []
        for b in range(blocks):
            first = b * Q_BLOCK
            block = queries[first : first + Q_BLOCK]
            spread = jnp.concatenate(
                [jnp.where(head_of == h, block, 0.0) for h in range(A_HEADS)], axis=0
            )
            q_high, q_low = two_parts(spread)
            stacked = jnp.concatenate(
                [
                    jnp.concatenate([q_high, q_high], axis=1),
                    jnp.concatenate([q_low, jnp.zeros_like(q_low)], axis=1),
                ],
                axis=0,
            )
            scores = dot(stacked, keys[first : first + span], NT)
            scores = scores[: A_HEADS * Q_BLOCK] + scores[A_HEADS * Q_BLOCK :]
            offset = offsets[b]
            position = tile * rows + first - rim + reach
            inside = (
                (reach >= offset)
                & (reach < offset + K_WIN)
                & (position >= 0)
                & (position < total)
            )
            scores = jnp.where(inside, scores, excluded)
            top = jnp.max(scores, axis=-1, keepdims=True)
            weights = jnp.exp(scores - top)
            weights = weights * (1.0 / jnp.sum(weights, axis=-1, keepdims=True))
            mixed = dot(weights.astype(BF), vals[first : first + span])
            mixed = mixed[:, :width] + mixed[:, width:]
            gathered = jnp.where(head_of == 0, mixed[:Q_BLOCK], 0.0)
            for h in range(1, A_HEADS):
                gathered += jnp.where(
                    head_of == h, mixed[h * Q_BLOCK : (h + 1) * Q_BLOCK], 0.0
                )
            parts.append(gathered)
        atom_out = (atoms[n] + jnp.concatenate(parts, axis=0)).astype(BF)
        hidden = jnp.maximum(dot(atom_out, agg_weight[...]), 0.0)
        sums = 0.0
        for part in two_parts(hidden):
            sums = sums + dot(member, part)
        token_normal, _ = norm_parts(sums / counts)
        _, noise_code = noise_parts(levels[n])
        token_in.append(token_normal + single_term + noise_code[:, :1] * noise_row)
    token_in = jnp.concatenate(token_in, axis=0)
    count = token_in.shape[0]
    stacked = jnp.concatenate(two_parts(token_in), axis=0)
    proj = dot(stacked, token_weight[...])
    proj = proj[:count] + proj[count:]
    wide = H * HEAD
    cot = jnp.concatenate([cotangent[n].astype(F32) for n in range(copies)], axis=0)
    lane = lax.broadcasted_iota(jnp.int32, (1, 128 - 2 * HEAD), 1)
    for h in range(H):
        at = h * HEAD
        pieces = [
            proj[:, at : at + HEAD] * (1.0 / math.sqrt(HEAD)),
            cot[:, at : at + HEAD],
            proj[:, wide + at : wide + at + HEAD],
            proj[:, 2 * wide + at : 2 * wide + at + HEAD],
        ]
        for half in range(2):
            row = []
            codes = jnp.zeros((1, 128 - 2 * HEAD), F32)
            for at_piece in range(2):
                piece = pieces[2 * half + at_piece]
                top = jnp.max(jnp.max(jnp.abs(piece), axis=0, keepdims=True), axis=1, keepdims=True)
                steps, power = grid_scale(top)
                codes = jnp.where(lane == 2 * at_piece, steps, codes)
                codes = jnp.where(lane == 2 * at_piece + 1, power, codes)
                row.append(piece * (1.0 / scale_value(steps, power)))
            row.append(jnp.broadcast_to(codes, (count, 128 - 2 * HEAD)))
            out[h, :, half * 128 : (half + 1) * 128] = whole(
                jnp.concatenate(row, axis=1)
            ).astype(jnp.int16)


def pair_kernel(pair, trans_in, trans_out, bias_weight_t, unit, cond_out, bias_out, held):
    inner = trans_out.shape[0]
    cols = pair.shape[1]
    step = pl.program_id(0)
    lanes = 128
    row_at = lax.broadcasted_iota(jnp.int32, (256, 256), 0)
    col_at = lax.broadcasted_iota(jnp.int32, (256, 256), 1)
    same = (row_at // lanes) == (col_at // lanes)
    ones = jnp.where(same, 1.0 / lanes, 0.0).astype(BF)
    centre = jnp.where(
        same, jnp.where(row_at == col_at, 1.0 - 1.0 / lanes, -1.0 / lanes), 0.0
    ).astype(BF)

    def normalise(value):
        half = value.shape[0] // 2
        centred = dot(jnp.concatenate([value[:half], value[half:]], axis=1), centre)
        high, low = two_parts(centred * centred)
        spread = dot(high, ones) + dot(low, ones)
        normal = (centred * lax.rsqrt(spread + epsilon)).astype(BF)
        return jnp.concatenate([normal[:, :lanes], normal[:, lanes:]], axis=0)

    group = 4
    chunk = 256
    for part in range(pair.shape[0] // group):
        value = pair[part * group : (part + 1) * group].reshape(group * cols, lanes)
        normed = normalise(value)
        delta = value.astype(F32)
        hidden = []
        for f in range(inner // chunk):
            half = dot(normed, trans_in[:, f * chunk : (f + 1) * chunk] * 0.5)
            up = dot(normed, trans_in[:, inner + f * chunk : inner + (f + 1) * chunk])
            hidden.append(((half + half * jnp.tanh(half)) * up).astype(BF))
        delta = delta + dot(jnp.concatenate(hidden, axis=1), trans_out[...])
        cond = delta.astype(BF)
        cond_out[part * group : (part + 1) * group] = cond.reshape(group, cols, lanes)
        bias = dot(bias_weight_t[...], normalise(cond), NT) * (1.0 / unit[...])
        for i in range(group):
            held[step, :, part * group + i, :] = bias[:, i * cols : (i + 1) * cols]

    @pl.when(step == pl.num_programs(0) - 1)
    def _():
        for s in range(held.shape[0]):
            rows = held.shape[2]
            bias_out[:, s * rows : (s + 1) * rows, :] = whole(held[s]).astype(jnp.int16)


def attend_kernel(place, unit, queries, kv, bias_mine, bias_other, update_mine, grad_other):
    core = place[0]
    blocks = [core, 2 + core, 1 - core, 3 - core]
    cols = 384
    tok = 24
    rows = 8 * tok
    lane = lax.broadcasted_iota(jnp.int32, (1, 128), 1)
    is_key = lane < HEAD
    is_value = (lane >= HEAD) & (lane < 2 * HEAD)

    def decode(block):
        block = block.astype(jnp.int32).astype(F32)
        codes = block[0:1]
        at = 2 * HEAD
        first = scale_value(codes[:, at : at + 1], codes[:, at + 1 : at + 2])
        second = scale_value(codes[:, at + 2 : at + 3], codes[:, at + 3 : at + 4])
        return block * jnp.where(is_key, first, jnp.where(is_value, second, 0.0))

    bias = jnp.concatenate(
        [
            jnp.concatenate(
                [
                    (bias_mine if c < 2 else bias_other)[2 * g + c % 2].astype(jnp.int32).astype(F32)
                    for c in range(4)
                ],
                axis=1,
            )
            for g in range(8)
        ],
        axis=0,
    ) * unit[0]
    grad = None
    for y in range(2):
        query_blocks = [decode(queries[2 * g + y, :, :128]) for g in range(8)]
        token_blocks = [
            decode(kv[2 * c + z, 2 * g + y]) for c in blocks for z in range(2) for g in range(8)
        ]
        for p in range(2):
            query = jnp.concatenate([b[p * tok : (p + 1) * tok] for b in query_blocks], axis=0)
            q_high, q_low = two_parts(jnp.where(is_key, query, 0.0))
            c_high, c_low = two_parts(jnp.where(is_value, query, 0.0))
            high, low = two_parts(
                jnp.concatenate([b[p * tok : (p + 1) * tok] for b in token_blocks], axis=0)
            )
            both = jnp.concatenate([high, low], axis=1)
            none = jnp.zeros_like(q_low)
            stacked = jnp.concatenate(
                [
                    jnp.concatenate([q_high, q_high], axis=1),
                    jnp.concatenate([q_low, none], axis=1),
                    jnp.concatenate([c_high, c_high], axis=1),
                    jnp.concatenate([c_low, none], axis=1),
                ],
                axis=0,
            )
            products = dot(stacked, both, NT)
            scores = products[:rows] + products[rows : 2 * rows] + bias
            prob_grad = products[2 * rows : 3 * rows] + products[3 * rows :]
            top = jnp.max(scores, axis=-1, keepdims=True)
            weights = jnp.exp(scores - top)
            weights = weights * (1.0 / jnp.sum(weights, axis=-1, keepdims=True))
            mixed = dot(weights.astype(BF), both)
            mixed = mixed[:, :128] + mixed[:, 128:]
            for g in range(8):
                update_mine[2 * g + y, :, cols + p * HEAD : cols + (p + 1) * HEAD] = mixed[
                    g * tok : (g + 1) * tok, HEAD : 2 * HEAD
                ]
            term = weights * prob_grad
            term = term - weights * jnp.sum(term, axis=-1, keepdims=True)
            grad = term if grad is None else grad + term
    for g in range(8):
        for c in range(4):
            (update_mine if c < 2 else grad_other)[2 * g + c % 2, :, :cols] = grad[
                g * tok : (g + 1) * tok, c * cols : (c + 1) * cols
            ]


def merge_kernel(mine, other, out):
    cols = other.shape[2]
    used = 2 * HEAD
    lane = lax.broadcasted_iota(jnp.int32, (1, 128), 1)
    for h in range(mine.shape[0]):
        grad = mine[h, :, :cols] + other[h]
        update = jnp.where(lane < used, mine[h, :, cols:], 0.0)
        codes = update
        scaled = []
        for at, part in ((0, grad), (2, update)):
            steps, power = grid_scale(jnp.max(jnp.abs(part), axis=-1, keepdims=True))
            scaled.append(part * (1.0 / scale_value(steps, power)))
            codes = jnp.where(lane == used + at, steps, codes)
            codes = jnp.where(lane == used + at + 1, power, codes)
        last = jnp.where(lane < used, scaled[1], codes)
        out[h] = jnp.concatenate(
            [
                whole(scaled[0][:, :256]),
                whole(jnp.concatenate([scaled[0][:, 256:], last], axis=1)),
            ],
            axis=0,
        ).astype(jnp.int16)


def grad_kernel(packed, cond, bias_weight, out, update_out, held):
    step = pl.program_id(0)
    lanes = 128
    heads, _, rows, cols = held.shape[1], 0, held.shape[2], held.shape[3]
    tok = packed.shape[1] // 2

    @pl.when(step == 0)
    def _():
        pieces = [[], []]
        for h in range(heads):
            block = packed[h].astype(jnp.int32).astype(F32)
            low, high = block[:tok], block[tok:]
            at = lanes + 2 * HEAD
            grad_scale = scale_value(high[:, at : at + 1], high[:, at + 1 : at + 2])
            update_scale = scale_value(high[:, at + 2 : at + 3], high[:, at + 3 : at + 4])
            grad = jnp.concatenate([low, high[:, :lanes]], axis=1) * grad_scale
            for s in range(held.shape[0]):
                held[s, h] = grad[s * rows : (s + 1) * rows]
            for p in range(2):
                pieces[p].append(
                    high[:, lanes + p * HEAD : lanes + (p + 1) * HEAD] * update_scale
                )
        for p in range(2):
            update_out[p] = jnp.concatenate(pieces[p], axis=1).astype(BF)

    row_at = lax.broadcasted_iota(jnp.int32, (256, 256), 0)
    col_at = lax.broadcasted_iota(jnp.int32, (256, 256), 1)
    same = (row_at // lanes) == (col_at // lanes)
    ones = jnp.where(same, 1.0 / lanes, 0.0).astype(BF)
    centre = jnp.where(
        same, jnp.where(row_at == col_at, 1.0 - 1.0 / lanes, -1.0 / lanes), 0.0
    ).astype(BF)
    weight = bias_weight[...].astype(F32)
    w_high, w_low = two_parts(weight - jnp.mean(weight, axis=-1, keepdims=True))
    parts = jnp.concatenate([w_high, w_high, w_high, w_low, w_low], axis=0)
    group = 4
    count = group * cols
    half = count // 2

    def paired(value):
        return jnp.concatenate([value[:half], value[half:]], axis=1)

    def mean(value):
        high, low = two_parts(value)
        return dot(high, ones) + dot(low, ones)

    for part in range(rows // group):
        normals = []
        for i in range(group):
            high, middle, low = three_parts(held[step, :, part * group + i, :])
            stacked = jnp.concatenate([high, middle, low, high, middle], axis=0)
            normals.append(dot(stacked, parts, TN))
        grad_normal = paired(jnp.concatenate(normals, axis=0))
        value = cond[part * group : (part + 1) * group].reshape(count, lanes)
        centred = dot(paired(value), centre)
        scale = lax.rsqrt(mean(centred * centred) + epsilon)
        normal = centred * scale
        result = ((grad_normal - normal * mean(grad_normal * normal)) * scale).astype(BF)
        result = jnp.concatenate([result[:, :lanes], result[:, lanes:]], axis=0)
        out[part * group : (part + 1) * group] = result.reshape(group, cols, lanes)


def params(**more):
    return pltpu.CompilerParams(vmem_limit_bytes=56 * 1024 * 1024, **more)


VMEM = pl.BlockSpec(memory_space=pltpu.VMEM)
SMEM = pl.BlockSpec(memory_space=pltpu.SMEM)


def on_device(
    pair_rep,
    single,
    atom_feat,
    coords,
    levels,
    window_offset,
    atom_token,
    trans_in,
    trans_out,
    bias_weight,
    single_weight,
    coord_weight,
    atom_weight,
    agg_weight,
    token_weight,
    noise_weight,
    cotangent,
):
    tile_index = lax.axis_index(TILE).astype(jnp.int32)
    core_index = lax.axis_index("core").astype(jnp.int32)
    copies, tok_rows, width = cotangent.shape
    atom_rows, atom_width = atom_feat.shape
    cols = pair_rep.shape[1]
    rim = K_WIN // 2
    atoms, normed, first, last = pl.pallas_call(
        start_kernel,
        out_shape=(
            jax.ShapeDtypeStruct((copies, atom_rows, atom_width), F32),
            jax.ShapeDtypeStruct((copies, atom_rows, atom_width), BF),
            jax.ShapeDtypeStruct((copies, rim, atom_width), BF),
            jax.ShapeDtypeStruct((copies, rim, atom_width), BF),
        ),
        in_specs=[SMEM] + [VMEM] * 3,
        out_specs=(VMEM,) * 4,
        compiler_params=params(),
        cost_estimate=pl.CostEstimate(flops=1_000_000, bytes_accessed=500_000, transcendentals=0),
        name="atom_start",
    )(levels, atom_feat, coords, coord_weight)
    forward = [(i, i + 1) for i in range(63)]
    backward = [(i + 1, i) for i in range(63)]
    low = lax.ppermute(last, TILE, forward)
    high = lax.ppermute(first, TILE, backward)
    packed = pl.pallas_call(
        atom_kernel,
        out_shape=jax.ShapeDtypeStruct((H, copies * tok_rows, 256), jnp.int16),
        in_specs=[SMEM] * 3 + [VMEM] * 12,
        out_specs=VMEM,
        compiler_params=params(),
        cost_estimate=pl.CostEstimate(flops=3_000_000_000, bytes_accessed=6_000_000, transcendentals=0),
        name="atom_stage",
    )(
        tile_index[None], window_offset, levels, low, high, normed, atoms, atom_weight, agg_weight,
        atom_token, single, single_weight, noise_weight, token_weight, cotangent,
    )
    packed = lax.all_to_all(packed, PLANE, 0, 0, tiled=True)
    kv = lax.all_gather(packed[:, :, 128:], "z", axis=0)

    step = 8
    steps = tok_rows // step
    bias_t = bias_weight.T
    reach = jnp.sqrt(jnp.sum(jnp.square(bias_weight.astype(F32)), axis=0))
    unit = (reach * (math.sqrt(128.0) * 1.01 / 32767.0) + 1e-30).astype(F32)
    cond, bias = pl.pallas_call(
        pair_kernel,
        grid=(steps,),
        out_shape=(
            jax.ShapeDtypeStruct(pair_rep.shape, BF),
            jax.ShapeDtypeStruct((H, tok_rows, cols), jnp.int16),
        ),
        in_specs=[
            pl.BlockSpec((step, cols, 128), lambda i: (i, 0, 0)),
            pl.BlockSpec(trans_in.shape, lambda i: (0, 0)),
            pl.BlockSpec(trans_out.shape, lambda i: (0, 0)),
            pl.BlockSpec(bias_t.shape, lambda i: (0, 0)),
            pl.BlockSpec((H, 1), lambda i: (0, 0)),
        ],
        out_specs=(
            pl.BlockSpec((step, cols, 128), lambda i: (i, 0, 0)),
            pl.BlockSpec((H, tok_rows, cols), lambda i: (0, 0, 0)),
        ),
        scratch_shapes=[pltpu.VMEM((steps, H, step, cols), F32)],
        compiler_params=params(),
        cost_estimate=pl.CostEstimate(flops=4_000_000_000, bytes_accessed=6_000_000, transcendentals=5_000_000),
        name="pair_transition",
    )(pair_rep, trans_in, trans_out, bias_t, unit[:, None])
    bias_mine = lax.all_to_all(bias, PLANE, 0, 0, tiled=True)
    swap = [(0, 1), (1, 0)]
    bias_other = lax.ppermute(bias_mine, "core", swap)

    head_index = lax.axis_index(PLANE)
    grad_mine, grad_other = pl.pallas_call(
        attend_kernel,
        out_shape=(
            jax.ShapeDtypeStruct((H, tok_rows, cols + 128), F32),
            jax.ShapeDtypeStruct((H, tok_rows, cols), F32),
        ),
        in_specs=[SMEM] * 2 + [VMEM] * 4,
        out_specs=(VMEM, VMEM),
        compiler_params=params(),
        cost_estimate=pl.CostEstimate(flops=4_000_000_000, bytes_accessed=8_000_000, transcendentals=1_200_000),
        name="token_attention",
    )(core_index[None], lax.dynamic_slice(unit, (head_index,), (1,)), packed, kv, bias_mine, bias_other)
    merged = pl.pallas_call(
        merge_kernel,
        out_shape=jax.ShapeDtypeStruct((H, 2 * tok_rows, 256), jnp.int16),
        in_specs=[VMEM] * 2,
        out_specs=VMEM,
        compiler_params=params(),
        cost_estimate=pl.CostEstimate(flops=2_000_000, bytes_accessed=2_000_000, transcendentals=0),
        name="gradient_merge",
    )(grad_mine, lax.ppermute(grad_other, "core", swap))
    merged = lax.all_to_all(merged, PLANE, 0, 0, tiled=True)
    gradient, update = pl.pallas_call(
        grad_kernel,
        grid=(steps,),
        out_shape=(
            jax.ShapeDtypeStruct(pair_rep.shape, BF),
            jax.ShapeDtypeStruct(cotangent.shape, BF),
        ),
        in_specs=[
            pl.BlockSpec(merged.shape, lambda i: (0, 0, 0)),
            pl.BlockSpec((step, cols, 128), lambda i: (i, 0, 0)),
            pl.BlockSpec(bias_t.shape, lambda i: (0, 0)),
        ],
        out_specs=(
            pl.BlockSpec((step, cols, 128), lambda i: (i, 0, 0)),
            pl.BlockSpec(cotangent.shape, lambda i: (0, 0, 0)),
        ),
        scratch_shapes=[pltpu.VMEM((steps, H, step, cols), F32)],
        compiler_params=params(),
        cost_estimate=pl.CostEstimate(flops=400_000_000, bytes_accessed=6_000_000, transcendentals=0),
        name="pair_gradient",
    )(merged, cond, bias_t)
    return (update, gradient)


def solution(mesh):
    fine = Mesh(mesh.devices.reshape(8, 8, 2, 2), ("z", "g", "ylo", "core"))
    placed = (
        P(TILE, COPY, None),
        P(TILE, None),
        P(TILE, None),
        P(COPY, None, TILE),
        P(COPY),
        P(TILE),
        P(TILE),
        P(),
        P(),
        P(),
        P(),
        P(),
        P(),
        P(),
        P(),
        P(),
        P(COPY, TILE, None),
    )
    return jax.shard_map(
        on_device,
        mesh=fine,
        in_specs=placed,
        out_specs=(P(COPY, TILE, None), P(TILE, COPY, None)),
        check_vma=False,
    )
```

```python
import math

import jax
import jax.numpy as jnp
from jax import lax
from jax.experimental import pallas as pl
from jax.experimental.pallas import tpu as pltpu
from jax.sharding import Mesh, PartitionSpec as P

A_HEAD = 32
A_HEADS = 4
Q_BLOCK = 32
K_WIN = 128
LEVELS = 200
HEAD = 48
H = 16

epsilon = 1e-05
sigma_data = 16.0
sigma_top = 160.0
sigma_low = 0.0004
rho_power = 7.0
excluded = -1e30
TILE = ("z", "g")
COPY = ("ylo", "core")
PLANE = ("g", "ylo")
BF = jnp.bfloat16
F32 = jnp.float32
NT = (((1,), (1,)), ((), ()))
NN = (((1,), (0,)), ((), ()))
TN = (((0,), (0,)), ((), ()))


def norm_parts(value):
    average = jnp.mean(value, axis=-1, keepdims=True)
    centred = value - average
    spread = jnp.mean(centred * centred, axis=-1, keepdims=True)
    scale = lax.rsqrt(spread + epsilon)
    return (centred * scale, scale)


def noise_parts(level):
    fraction = jnp.full((1, 128), level, jnp.int32).astype(F32) / LEVELS
    highest = sigma_top ** (1.0 / rho_power)
    lowest = sigma_low ** (1.0 / rho_power)
    root = highest + fraction * (lowest - highest)
    square = root * root
    sigma = sigma_data * (square * square * square * root)
    input_scale = lax.rsqrt(sigma * sigma + sigma_data * sigma_data)
    noise_code = 0.25 * jnp.log(sigma / sigma_data)
    return (input_scale, noise_code)


def dot(a, b, dims=NN):
    return lax.dot_general(a, b, dims, preferred_element_type=F32)


def two_parts(value):
    high = value.astype(BF)
    low = (value - high.astype(F32)).astype(BF)
    return high, low


def three_parts(value):
    high = value.astype(BF)
    rest = value - high.astype(F32)
    middle = rest.astype(BF)
    low = (rest - middle.astype(F32)).astype(BF)
    return high, middle, low


def grid_scale(top):
    top = jnp.maximum(top, 1e-30)
    power = jnp.ceil(jnp.log2(top))
    steps = jnp.ceil(top * jnp.exp2(13.0 - power)) + 1.0
    return steps, power


def scale_value(steps, power):
    return steps * jnp.exp2(power - 13.0) * (1.0 / 32767.0)


def whole(value):
    return jnp.round(value).astype(jnp.int32)


def start_kernel(levels, feat, coords, coord_weight, atoms_out, normed_out, first_out, last_out):
    rows = feat.shape[0]
    rim = K_WIN // 2
    for n in range(coords.shape[0]):
        input_scale, _ = noise_parts(levels[n])
        scaled = coords[n] * input_scale[:, :1]
        atoms = feat[...].astype(F32) + lax.dot_general(
            scaled, coord_weight[...], TN, precision=lax.Precision.HIGHEST, preferred_element_type=F32
        )
        normal, _ = norm_parts(atoms)
        normal = normal.astype(BF)
        atoms_out[n] = atoms
        normed_out[n] = normal
        first_out[n] = normal[:rim]
        last_out[n] = normal[rows - rim :]


def atom_kernel(
    place, offsets, levels, low, high, normed, atoms, atom_weight, agg_weight, atom_token,
    single, single_weight, noise_weight, token_weight, cotangent, out, weight_held, arrival
):
    tile = place[0]
    fetch = pltpu.make_async_copy(token_weight, weight_held, arrival)
    fetch.start()
    copies, rows, width = normed.shape
    blocks = rows // Q_BLOCK
    span = K_WIN + Q_BLOCK
    rim = K_WIN // 2
    total = 64 * rows
    tok_rows = single.shape[0]
    head_of = lax.broadcasted_iota(jnp.int32, (Q_BLOCK, width), 1) // A_HEAD
    twice_head = lax.broadcasted_iota(jnp.int32, (Q_BLOCK, 2 * width), 1) % width // A_HEAD
    reach = lax.broadcasted_iota(jnp.int32, (1, span), 1)
    local_token = atom_token[...].reshape(1, rows) - tile * tok_rows
    member = (lax.broadcasted_iota(jnp.int32, (tok_rows, rows), 0) == local_token).astype(F32)
    counts = jnp.sum(member, axis=1, keepdims=True)
    member = member.astype(BF)
    single_term = dot(single[...], single_weight[...])
    noise_row = noise_weight[...].reshape(1, noise_weight.shape[0])
    scores = []
    vals = []
    for n in range(copies):
        ext = jnp.concatenate([low[n], normed[n], high[n]], axis=0)
        proj = dot(ext, atom_weight[...])
        queries = proj[rim : rim + rows, :width] * (1.0 / math.sqrt(A_HEAD))
        q_high, q_low = two_parts(queries)
        key_high, key_low = two_parts(proj[:, width : 2 * width])
        keys = jnp.concatenate([key_high, key_low], axis=1)
        vals.append(jnp.concatenate(two_parts(proj[:, 2 * width :]), axis=1))
        twice = jnp.concatenate([q_high, q_high], axis=1)
        once = jnp.concatenate([q_low, jnp.zeros_like(q_low)], axis=1)
        blank = jnp.zeros((Q_BLOCK, 2 * width), BF)
        for b in range(blocks):
            first = b * Q_BLOCK
            stacked = jnp.concatenate(
                [
                    jnp.where(twice_head == h, part[first : first + Q_BLOCK], blank)
                    for part in (twice, once)
                    for h in range(A_HEADS)
                ],
                axis=0,
            )
            both = dot(stacked, keys[first : first + span], NT)
            offset = offsets[b]
            position = tile * rows + first - rim + reach
            inside = (
                (reach >= offset)
                & (reach < offset + K_WIN)
                & (position >= 0)
                & (position < total)
            )
            half = A_HEADS * Q_BLOCK
            scores.append(jnp.where(inside, both[:half] + both[half:], excluded))
    scores = jnp.concatenate(scores, axis=0)
    weights = jnp.exp(scores - jnp.max(scores, axis=-1, keepdims=True))
    weights = weights * (1.0 / jnp.sum(weights, axis=-1, keepdims=True))
    weights = weights.astype(BF)
    token_in = []
    for n in range(copies):
        parts = []
        for b in range(blocks):
            first = b * Q_BLOCK
            at = (n * blocks + b) * A_HEADS * Q_BLOCK
            mixed = dot(weights[at : at + A_HEADS * Q_BLOCK], vals[n][first : first + span])
            mixed = mixed[:, :width] + mixed[:, width:]
            gathered = jnp.where(head_of == 0, mixed[:Q_BLOCK], 0.0)
            for h in range(1, A_HEADS):
                gathered += jnp.where(
                    head_of == h, mixed[h * Q_BLOCK : (h + 1) * Q_BLOCK], 0.0
                )
            parts.append(gathered)
        atom_out = (atoms[n] + jnp.concatenate(parts, axis=0)).astype(BF)
        hidden = jnp.maximum(dot(atom_out, agg_weight[...]), 0.0)
        sums = 0.0
        for part in two_parts(hidden):
            sums = sums + dot(member, part)
        token_normal, _ = norm_parts(sums / counts)
        _, noise_code = noise_parts(levels[n])
        token_in.append(token_normal + single_term + noise_code[:, :1] * noise_row)
    token_in = jnp.concatenate(token_in, axis=0)
    count = token_in.shape[0]
    stacked = jnp.concatenate(two_parts(token_in), axis=0)
    fetch.wait()
    proj = dot(stacked, weight_held[...])
    proj = proj[:count] + proj[count:]
    wide = H * HEAD
    cot = jnp.concatenate([cotangent[n].astype(F32) for n in range(copies)], axis=0)
    head_at = lax.broadcasted_iota(jnp.int32, (H, wide), 1) // HEAD
    mine = head_at == lax.broadcasted_iota(jnp.int32, (H, wide), 0)
    lane = lax.broadcasted_iota(jnp.int32, (H, 128 - 2 * HEAD), 1)
    codes = [jnp.zeros(lane.shape, F32)] * 2
    coded = []
    sources = [
        proj[:, :wide] * (1.0 / math.sqrt(HEAD)), cot, proj[:, wide : 2 * wide], proj[:, 2 * wide :]
    ]
    for index, source in enumerate(sources):
        top = jnp.max(jnp.abs(source), axis=0, keepdims=True)
        steps, power = grid_scale(jnp.max(jnp.where(mine, top, 0.0), axis=1, keepdims=True))
        inverse = 1.0 / scale_value(steps, power)
        inverse = jnp.max(jnp.where(mine, inverse, 0.0), axis=0, keepdims=True)
        coded.append(jnp.round(source * inverse))
        half, at = index // 2, 2 * (index % 2)
        codes[half] = jnp.where(
            lane == at, steps, jnp.where(lane == at + 1, power, codes[half])
        )
    for h in range(H):
        at = h * HEAD
        for half in range(2):
            row = [coded[2 * half + k][:, at : at + HEAD] for k in range(2)]
            row.append(jnp.broadcast_to(codes[half][h : h + 1], (count, 128 - 2 * HEAD)))
            out[h, :, half * 128 : (half + 1) * 128] = (
                jnp.concatenate(row, axis=1).astype(jnp.int32).astype(jnp.int16)
            )


def head_unit(weight):
    weight = weight.astype(F32)
    reach = jnp.sqrt(jnp.sum(weight * weight, axis=-1, keepdims=True))
    return reach * (math.sqrt(128.0) * 1.01 / 32767.0) + 1e-30


def lane_matrices(lanes):
    row_at = lax.broadcasted_iota(jnp.int32, (2 * lanes, 2 * lanes), 0)
    col_at = lax.broadcasted_iota(jnp.int32, (2 * lanes, 2 * lanes), 1)
    same = (row_at // lanes) == (col_at // lanes)
    ones = jnp.where(same, 1.0 / lanes, 0.0).astype(BF)
    centre = jnp.where(
        same, jnp.where(row_at == col_at, 1.0 - 1.0 / lanes, -1.0 / lanes), 0.0
    ).astype(BF)
    return jnp.concatenate([ones, ones], axis=0), centre


def lane_mean(value, ones):
    return dot(jnp.concatenate(two_parts(value), axis=1), ones)


def pair_block(pair, trans_in, trans_out, bias_weight_t, cond_out, store):
    inner = trans_out.shape[0]
    cols = pair.shape[1]
    lanes = 128
    ones, centre = lane_matrices(lanes)
    unit = head_unit(bias_weight_t[...])

    def normalise(value):
        half = value.shape[0] // 2
        centred = dot(jnp.concatenate([value[:half], value[half:]], axis=1), centre)
        normal = (centred * lax.rsqrt(lane_mean(centred * centred, ones) + epsilon)).astype(BF)
        return jnp.concatenate([normal[:, :lanes], normal[:, lanes:]], axis=0)

    group = 4
    chunk = 128
    weights = [
        jnp.concatenate(
            [
                trans_in[:, f : f + chunk] * 0.5,
                trans_in[:, inner + f : inner + f + chunk],
            ],
            axis=1,
        )
        for f in range(0, inner, chunk)
    ]
    for part in range(pair.shape[0] // group):
        value = pair[part * group : (part + 1) * group].reshape(group * cols, lanes)
        normed = normalise(value)
        delta = value.astype(F32)
        hidden = []
        for weight in weights:
            both = dot(normed, weight)
            half = both[:, :chunk]
            hidden.append(((half + half * jnp.tanh(half)) * both[:, chunk:]).astype(BF))
        delta = delta + dot(jnp.concatenate(hidden, axis=1), trans_out[...])
        cond = delta.astype(BF)
        cond_out[part * group : (part + 1) * group] = cond.reshape(group, cols, lanes)
        bias = dot(bias_weight_t[...], normalise(cond), NT) * (1.0 / unit)
        for i in range(group):
            store(part * group + i, bias[:, i * cols : (i + 1) * cols])


def pair_first_kernel(pair, trans_in, trans_out, bias_weight_t, anchor, cond_out, bias_out):
    def store(i, value):
        bias_out[:, i, :] = value

    pair_block(pair, trans_in, trans_out, bias_weight_t, cond_out, store)


def pair_next_kernel(pair, trans_in, trans_out, bias_weight_t, anchor, cond, cond_out, bias_out):
    pair_first_kernel(pair, trans_in, trans_out, bias_weight_t, anchor, cond_out, bias_out)


def pair_last_kernel(
    pair, trans_in, trans_out, bias_weight_t, anchor, cond, first, second, cond_out, bias_out, held
):
    def store(i, value):
        held[:, i, :] = value

    pair_block(pair, trans_in, trans_out, bias_weight_t, cond_out, store)
    for h in range(bias_out.shape[0]):
        parts = [first[h], second[h], held[h]]
        bias_out[h] = whole(jnp.concatenate(parts, axis=0)).astype(jnp.int16)


def pair_call(kernel, index, inputs, extra, anchor, cond, bias_shape, scratch=()):
    pair_rep, trans_in, trans_out, bias_t = inputs
    step, cols = 8, pair_rep.shape[1]
    block = pl.BlockSpec((step, cols, 128), lambda i: (index, 0, 0))
    operands = [pair_rep, trans_in, trans_out, bias_t, anchor]
    if cond is not None:
        operands.append(cond)
    count = len(operands)
    specs = [block] + [pl.BlockSpec(x.shape, lambda i: (0, 0)) for x in operands[1:4]]
    specs += [ANY] * (count - 4)
    specs += [pl.BlockSpec(x.shape, lambda i: (0, 0, 0)) for x in extra]
    return pl.pallas_call(
        kernel,
        grid=(1,),
        out_shape=(jax.ShapeDtypeStruct(pair_rep.shape, BF), bias_shape),
        in_specs=specs,
        out_specs=(block, pl.BlockSpec(bias_shape.shape, lambda i: (0, 0, 0))),
        scratch_shapes=list(scratch),
        input_output_aliases={} if cond is None else {5: 0},
        compiler_params=params(),
        cost_estimate=pl.CostEstimate(
            flops=6_000_000_000, bytes_accessed=8_000_000, transcendentals=0
        ),
        name="pair_part",
    )(*operands, *extra)


def attend_kernel(
    core_at, head_at, z_at, queries, kv0, kv1, kv2, kv3, kv4, kv5, kv6, kv7, bias_mine, bias_other, bias_weight_t,
    update_mine, grad_other, kv
):
    core = core_at[0]
    unit = head_unit(bias_weight_t[...])
    this = lax.broadcasted_iota(jnp.int32, unit.shape, 0) == head_at[0]
    unit = jnp.sum(jnp.where(this, unit, 0.0), axis=0, keepdims=True)
    for back, block in enumerate((kv0, kv1, kv2, kv3, kv4, kv5, kv6, kv7)):
        kv[lax.rem(z_at[0] + 8 - back, 8)] = block[...]
    blocks = [core, 2 + core, 1 - core, 3 - core]
    cols = 384
    tok = 24
    rows = 8 * tok
    lane = lax.broadcasted_iota(jnp.int32, (1, 128), 1)
    is_key = lane < HEAD
    is_value = (lane >= HEAD) & (lane < 2 * HEAD)

    def decode(block):
        block = block.astype(jnp.int32).astype(F32)
        codes = block[0:1]
        at = 2 * HEAD
        first = scale_value(codes[:, at : at + 1], codes[:, at + 1 : at + 2])
        second = scale_value(codes[:, at + 2 : at + 3], codes[:, at + 3 : at + 4])
        return block * jnp.where(is_key, first, jnp.where(is_value, second, 0.0))

    bias = jnp.concatenate(
        [
            jnp.concatenate(
                [
                    (bias_mine if c < 2 else bias_other)[2 * g + c % 2].astype(jnp.int32).astype(F32)
                    for c in range(4)
                ],
                axis=1,
            )
            for g in range(8)
        ],
        axis=0,
    ) * unit
    grad = None
    for y in range(2):
        query_blocks = [decode(queries[2 * g + y, :, :128]) for g in range(8)]
        token_blocks = [
            decode(kv[2 * c + z, 2 * g + y]) for c in blocks for z in range(2) for g in range(8)
        ]
        for p in range(2):
            query = jnp.concatenate([b[p * tok : (p + 1) * tok] for b in query_blocks], axis=0)
            q_high, q_low = two_parts(jnp.where(is_key, query, 0.0))
            c_high, c_low = two_parts(jnp.where(is_value, query, 0.0))
            high, low = two_parts(
                jnp.concatenate([b[p * tok : (p + 1) * tok] for b in token_blocks], axis=0)
            )
            both = jnp.concatenate([high, low], axis=1)
            none = jnp.zeros_like(q_low)
            stacked = jnp.concatenate(
                [
                    jnp.concatenate([q_high, q_high], axis=1),
                    jnp.concatenate([q_low, none], axis=1),
                    jnp.concatenate([c_high, c_high], axis=1),
                    jnp.concatenate([c_low, none], axis=1),
                ],
                axis=0,
            )
            products = dot(stacked, both, NT)
            scores = products[:rows] + products[rows : 2 * rows] + bias
            prob_grad = products[2 * rows : 3 * rows] + products[3 * rows :]
            top = jnp.max(scores, axis=-1, keepdims=True)
            weights = jnp.exp(scores - top)
            weights = weights * (1.0 / jnp.sum(weights, axis=-1, keepdims=True))
            mixed = dot(weights.astype(BF), both)
            mixed = mixed[:, :128] + mixed[:, 128:]
            for g in range(8):
                update_mine[2 * g + y, :, cols + p * HEAD : cols + (p + 1) * HEAD] = mixed[
                    g * tok : (g + 1) * tok, HEAD : 2 * HEAD
                ]
            term = weights * prob_grad
            term = term - weights * jnp.sum(term, axis=-1, keepdims=True)
            grad = term if grad is None else grad + term
    for g in range(8):
        for c in range(4):
            (update_mine if c < 2 else grad_other)[2 * g + c % 2, :, :cols] = grad[
                g * tok : (g + 1) * tok, c * cols : (c + 1) * cols
            ]


def merge_kernel(mine, other, out):
    cols = other.shape[2]
    used = 2 * HEAD
    lane = lax.broadcasted_iota(jnp.int32, (1, 128), 1)
    for h in range(mine.shape[0]):
        grad = mine[h, :, :cols] + other[h]
        update = jnp.where(lane < used, mine[h, :, cols:], 0.0)
        codes = update
        scaled = []
        for at, part in ((0, grad), (2, update)):
            steps, power = grid_scale(jnp.max(jnp.abs(part), axis=-1, keepdims=True))
            scaled.append(part * (1.0 / scale_value(steps, power)))
            codes = jnp.where(lane == used + at, steps, codes)
            codes = jnp.where(lane == used + at + 1, power, codes)
        last = jnp.where(lane < used, scaled[1], codes)
        out[h] = jnp.concatenate(
            [
                whole(scaled[0][:, :256]),
                whole(jnp.concatenate([scaled[0][:, 256:], last], axis=1)),
            ],
            axis=0,
        ).astype(jnp.int16)


def grad_kernel(packed, cond, bias_weight, out, update_out, held):
    step = pl.program_id(0)
    lanes = 128
    heads, _, rows, cols = held.shape[1], 0, held.shape[2], held.shape[3]
    tok = packed.shape[1] // 2

    @pl.when(step == 0)
    def _():
        pieces = [[], []]
        for h in range(heads):
            block = packed[h].astype(jnp.int32).astype(F32)
            low, high = block[:tok], block[tok:]
            at = lanes + 2 * HEAD
            grad_scale = scale_value(high[:, at : at + 1], high[:, at + 1 : at + 2])
            update_scale = scale_value(high[:, at + 2 : at + 3], high[:, at + 3 : at + 4])
            grad = jnp.concatenate([low, high[:, :lanes]], axis=1) * grad_scale
            for s in range(held.shape[0]):
                held[s, h] = grad[s * rows : (s + 1) * rows]
            for p in range(2):
                pieces[p].append(
                    high[:, lanes + p * HEAD : lanes + (p + 1) * HEAD] * update_scale
                )
        for p in range(2):
            update_out[p] = jnp.concatenate(pieces[p], axis=1).astype(BF)

    ones, centre = lane_matrices(lanes)
    weight = bias_weight[...].astype(F32)
    w_high, w_low = two_parts(weight - jnp.mean(weight, axis=-1, keepdims=True))
    parts = jnp.concatenate([w_high, w_high, w_high, w_low, w_low], axis=0)
    group = 4
    count = group * cols
    half = count // 2

    def paired(value):
        return jnp.concatenate([value[:half], value[half:]], axis=1)

    for part in range(rows // group):
        grad = jnp.concatenate(
            [held[step, :, part * group + i, :] for i in range(group)], axis=1
        )
        high, middle, low = three_parts(grad)
        stacked = jnp.concatenate([high, middle, low, high, middle], axis=0)
        grad_normal = paired(dot(stacked, parts, TN))
        value = cond[part * group : (part + 1) * group].reshape(count, lanes)
        centred = dot(paired(value), centre)
        scale = lax.rsqrt(lane_mean(centred * centred, ones) + epsilon)
        normal = centred * scale
        result = ((grad_normal - normal * lane_mean(grad_normal * normal, ones)) * scale).astype(BF)
        result = jnp.concatenate([result[:, :lanes], result[:, lanes:]], axis=0)
        out[part * group : (part + 1) * group] = result.reshape(group, cols, lanes)


def params(**more):
    return pltpu.CompilerParams(vmem_limit_bytes=56 * 1024 * 1024, **more)


VMEM = pl.BlockSpec(memory_space=pltpu.VMEM)
SMEM = pl.BlockSpec(memory_space=pltpu.SMEM)
ANY = pl.BlockSpec(memory_space=pl.ANY)


def on_device(
    pair_rep,
    single,
    atom_feat,
    coords,
    levels,
    window_offset,
    atom_token,
    trans_in,
    trans_out,
    bias_weight,
    single_weight,
    coord_weight,
    atom_weight,
    agg_weight,
    token_weight,
    noise_weight,
    cotangent,
):
    tile_index = lax.axis_index(TILE).astype(jnp.int32)
    core_index = lax.axis_index("core").astype(jnp.int32)
    copies, tok_rows, width = cotangent.shape
    atom_rows, atom_width = atom_feat.shape
    cols = pair_rep.shape[1]
    rim = K_WIN // 2
    atoms, normed, first, last = pl.pallas_call(
        start_kernel,
        out_shape=(
            jax.ShapeDtypeStruct((copies, atom_rows, atom_width), F32),
            jax.ShapeDtypeStruct((copies, atom_rows, atom_width), BF),
            jax.ShapeDtypeStruct((copies, rim, atom_width), BF),
            jax.ShapeDtypeStruct((copies, rim, atom_width), BF),
        ),
        in_specs=[SMEM] + [VMEM] * 3,
        out_specs=(VMEM,) * 4,
        compiler_params=params(),
        cost_estimate=pl.CostEstimate(flops=1_000_000, bytes_accessed=500_000, transcendentals=0),
        name="atom_start",
    )(levels, atom_feat, coords, coord_weight)
    forward = [(i, i + 1) for i in range(63)]
    backward = [(i + 1, i) for i in range(63)]
    low = lax.ppermute(last, TILE, forward)
    high = lax.ppermute(first, TILE, backward)
    bias_t = bias_weight.T
    inputs = (pair_rep, trans_in, trans_out, bias_t)
    step = 8
    part_bias = jax.ShapeDtypeStruct((H, step, cols), F32)
    cond, bias_first = pair_call(pair_first_kernel, 0, inputs, [], last, None, part_bias)
    low, high, bias_first = lax.optimization_barrier((low, high, bias_first))
    packed = pl.pallas_call(
        atom_kernel,
        out_shape=jax.ShapeDtypeStruct((H, copies * tok_rows, 256), jnp.int16),
        in_specs=[SMEM] * 3 + [VMEM] * 10 + [ANY, VMEM],
        out_specs=VMEM,
        scratch_shapes=[pltpu.VMEM(token_weight.shape, BF), pltpu.SemaphoreType.DMA],
        compiler_params=params(),
        cost_estimate=pl.CostEstimate(flops=3_000_000_000, bytes_accessed=6_000_000, transcendentals=0),
        name="atom_stage",
    )(
        tile_index[None], window_offset, levels, low, high, normed, atoms, atom_weight, agg_weight,
        atom_token, single, single_weight, noise_weight, token_weight, cotangent,
    )
    cond, bias_second = pair_call(
        pair_next_kernel, 1, inputs, [], packed, cond, part_bias
    )
    packed = lax.all_to_all(packed, PLANE, 0, 0, tiled=True)
    packed, bias_second = lax.optimization_barrier((packed, bias_second))
    own = packed[:, :, 128:]
    ahead = [(i, (i + 1) % 8) for i in range(8)]
    behind = [(i, (i + 7) % 8) for i in range(8)]
    rising = [own, lax.ppermute(own, "z", ahead)]
    falling = [own, lax.ppermute(own, "z", behind)]
    cond, bias = pair_call(
        pair_last_kernel, 2, inputs, [bias_first, bias_second], own, cond,
        jax.ShapeDtypeStruct((H, tok_rows, cols), jnp.int16), [pltpu.VMEM((H, step, cols), F32)],
    )
    rising[1], falling[1], bias = lax.optimization_barrier((rising[1], falling[1], bias))
    rising.append(lax.ppermute(rising[1], "z", ahead))
    falling.append(lax.ppermute(falling[1], "z", behind))
    rising.append(lax.ppermute(rising[2], "z", ahead))
    falling.append(lax.ppermute(falling[2], "z", behind))
    rising.append(lax.ppermute(rising[3], "z", ahead))
    every = rising + [falling[3], falling[2], falling[1]]
    steps = tok_rows // step
    bias_mine = lax.all_to_all(bias, PLANE, 0, 0, tiled=True)
    swap = [(0, 1), (1, 0)]
    bias_other = lax.ppermute(bias_mine, "core", swap)

    head_index = lax.axis_index(PLANE).astype(jnp.int32)
    z_index = lax.axis_index("z").astype(jnp.int32)
    grad_mine, grad_other = pl.pallas_call(
        attend_kernel,
        out_shape=(
            jax.ShapeDtypeStruct((H, tok_rows, cols + 128), F32),
            jax.ShapeDtypeStruct((H, tok_rows, cols), F32),
        ),
        in_specs=[SMEM] * 3 + [VMEM] * 12,
        out_specs=(VMEM, VMEM),
        scratch_shapes=[pltpu.VMEM((8,) + own.shape, jnp.int16)],
        compiler_params=params(),
        cost_estimate=pl.CostEstimate(flops=4_000_000_000, bytes_accessed=8_000_000, transcendentals=1_200_000),
        name="token_attention",
    )(
        core_index[None], head_index[None], z_index[None], packed, *every, bias_mine, bias_other, bias_t
    )
    merged = pl.pallas_call(
        merge_kernel,
        out_shape=jax.ShapeDtypeStruct((H, 2 * tok_rows, 256), jnp.int16),
        in_specs=[VMEM] * 2,
        out_specs=VMEM,
        compiler_params=params(),
        cost_estimate=pl.CostEstimate(flops=2_000_000, bytes_accessed=2_000_000, transcendentals=0),
        name="gradient_merge",
    )(grad_mine, lax.ppermute(grad_other, "core", swap))
    merged = lax.all_to_all(merged, PLANE, 0, 0, tiled=True)
    gradient, update = pl.pallas_call(
        grad_kernel,
        grid=(steps,),
        out_shape=(
            jax.ShapeDtypeStruct(pair_rep.shape, BF),
            jax.ShapeDtypeStruct(cotangent.shape, BF),
        ),
        in_specs=[
            pl.BlockSpec(merged.shape, lambda i: (0, 0, 0)),
            pl.BlockSpec((step, cols, 128), lambda i: (i, 0, 0)),
            pl.BlockSpec(bias_t.shape, lambda i: (0, 0)),
        ],
        out_specs=(
            pl.BlockSpec((step, cols, 128), lambda i: (i, 0, 0)),
            pl.BlockSpec(cotangent.shape, lambda i: (0, 0, 0)),
        ),
        scratch_shapes=[pltpu.VMEM((steps, H, step, cols), F32)],
        compiler_params=params(),
        cost_estimate=pl.CostEstimate(flops=400_000_000, bytes_accessed=6_000_000, transcendentals=0),
        name="pair_gradient",
    )(merged, cond, bias_t)
    return (update, gradient)


def solution(mesh):
    fine = Mesh(mesh.devices.reshape(8, 8, 2, 2), ("z", "g", "ylo", "core"))
    placed = (
        P(TILE, COPY, None),
        P(TILE, None),
        P(TILE, None),
        P(COPY, None, TILE),
        P(COPY),
        P(TILE),
        P(TILE),
        P(),
        P(),
        P(),
        P(),
        P(),
        P(),
        P(),
        P(),
        P(),
        P(COPY, TILE, None),
    )
    return jax.shard_map(
        on_device,
        mesh=fine,
        in_specs=placed,
        out_specs=(P(COPY, TILE, None), P(TILE, COPY, None)),
        check_vma=False,
    )
```

```python
import math

import jax
import jax.numpy as jnp
from jax import lax
from jax.experimental import pallas as pl
from jax.experimental.pallas import tpu as pltpu
from jax.sharding import Mesh, PartitionSpec as P

A_HEAD = 32
A_HEADS = 4
Q_BLOCK = 32
K_WIN = 128
LEVELS = 200
HEAD = 48
H = 16

epsilon = 1e-05
sigma_data = 16.0
sigma_top = 160.0
sigma_low = 0.0004
rho_power = 7.0
excluded = -1e30
TILE = ("z", "g")
COPY = ("ylo", "core")
PLANE = ("g", "ylo")
BF = jnp.bfloat16
F32 = jnp.float32
NT = (((1,), (1,)), ((), ()))
NN = (((1,), (0,)), ((), ()))
TN = (((0,), (0,)), ((), ()))


def norm_parts(value):
    average = jnp.mean(value, axis=-1, keepdims=True)
    centred = value - average
    spread = jnp.mean(centred * centred, axis=-1, keepdims=True)
    scale = lax.rsqrt(spread + epsilon)
    return (centred * scale, scale)


def noise_parts(level):
    fraction = jnp.full((1, 128), level, jnp.int32).astype(F32) / LEVELS
    highest = sigma_top ** (1.0 / rho_power)
    lowest = sigma_low ** (1.0 / rho_power)
    root = highest + fraction * (lowest - highest)
    square = root * root
    sigma = sigma_data * (square * square * square * root)
    input_scale = lax.rsqrt(sigma * sigma + sigma_data * sigma_data)
    noise_code = 0.25 * jnp.log(sigma / sigma_data)
    return (input_scale, noise_code)


def dot(a, b, dims=NN):
    return lax.dot_general(a, b, dims, preferred_element_type=F32)


def two_parts(value):
    high = value.astype(BF)
    low = (value - high.astype(F32)).astype(BF)
    return high, low


def three_parts(value):
    high = value.astype(BF)
    rest = value - high.astype(F32)
    middle = rest.astype(BF)
    low = (rest - middle.astype(F32)).astype(BF)
    return high, middle, low


def grid_scale(top):
    top = jnp.maximum(top, 1e-30)
    power = jnp.ceil(jnp.log2(top))
    steps = jnp.ceil(top * jnp.exp2(13.0 - power)) + 1.0
    return steps, power


def scale_value(steps, power):
    return steps * jnp.exp2(power - 13.0) * (1.0 / 32767.0)


def whole(value):
    return jnp.round(value).astype(jnp.int32)


def start_kernel(levels, feat, coords, coord_weight, atoms_out, normed_out, first_out, last_out):
    rows = feat.shape[0]
    rim = K_WIN // 2
    for n in range(coords.shape[0]):
        input_scale, _ = noise_parts(levels[n])
        scaled = coords[n] * input_scale[:, :1]
        atoms = feat[...].astype(F32) + lax.dot_general(
            scaled, coord_weight[...], TN, precision=lax.Precision.HIGHEST, preferred_element_type=F32
        )
        normal, _ = norm_parts(atoms)
        normal = normal.astype(BF)
        atoms_out[n] = atoms
        normed_out[n] = normal
        first_out[n] = normal[:rim]
        last_out[n] = normal[rows - rim :]


def atom_kernel(
    place, offsets, levels, low, high, normed, atoms, atom_weight, agg_weight, atom_token,
    single, single_weight, noise_weight, token_weight, cotangent, out, weight_held, arrival
):
    tile = place[0]
    fetch = pltpu.make_async_copy(token_weight, weight_held, arrival)
    fetch.start()
    copies, rows, width = normed.shape
    blocks = rows // Q_BLOCK
    span = K_WIN + Q_BLOCK
    rim = K_WIN // 2
    total = 64 * rows
    tok_rows = single.shape[0]
    head_of = lax.broadcasted_iota(jnp.int32, (Q_BLOCK, width), 1) // A_HEAD
    twice_head = lax.broadcasted_iota(jnp.int32, (Q_BLOCK, 2 * width), 1) % width // A_HEAD
    reach = lax.broadcasted_iota(jnp.int32, (1, span), 1)
    local_token = atom_token[...].reshape(1, rows) - tile * tok_rows
    member = (lax.broadcasted_iota(jnp.int32, (tok_rows, rows), 0) == local_token).astype(F32)
    counts = jnp.sum(member, axis=1, keepdims=True)
    member = member.astype(BF)
    single_term = dot(single[...], single_weight[...])
    noise_row = noise_weight[...].reshape(1, noise_weight.shape[0])
    scores = []
    vals = []
    for n in range(copies):
        ext = jnp.concatenate([low[n], normed[n], high[n]], axis=0)
        proj = dot(ext, atom_weight[...])
        queries = proj[rim : rim + rows, :width] * (1.0 / math.sqrt(A_HEAD))
        q_high, q_low = two_parts(queries)
        key_high, key_low = two_parts(proj[:, width : 2 * width])
        keys = jnp.concatenate([key_high, key_low], axis=1)
        vals.append(jnp.concatenate(two_parts(proj[:, 2 * width :]), axis=1))
        twice = jnp.concatenate([q_high, q_high], axis=1)
        once = jnp.concatenate([q_low, jnp.zeros_like(q_low)], axis=1)
        blank = jnp.zeros((Q_BLOCK, 2 * width), BF)
        for b in range(blocks):
            first = b * Q_BLOCK
            stacked = jnp.concatenate(
                [
                    jnp.where(twice_head == h, part[first : first + Q_BLOCK], blank)
                    for part in (twice, once)
                    for h in range(A_HEADS)
                ],
                axis=0,
            )
            both = dot(stacked, keys[first : first + span], NT)
            offset = offsets[b]
            position = tile * rows + first - rim + reach
            inside = (
                (reach >= offset)
                & (reach < offset + K_WIN)
                & (position >= 0)
                & (position < total)
            )
            half = A_HEADS * Q_BLOCK
            scores.append(jnp.where(inside, both[:half] + both[half:], excluded))
    scores = jnp.concatenate(scores, axis=0)
    weights = jnp.exp(scores - jnp.max(scores, axis=-1, keepdims=True))
    weights = weights * (1.0 / jnp.sum(weights, axis=-1, keepdims=True))
    weights = weights.astype(BF)
    token_in = []
    for n in range(copies):
        parts = []
        for b in range(blocks):
            first = b * Q_BLOCK
            at = (n * blocks + b) * A_HEADS * Q_BLOCK
            mixed = dot(weights[at : at + A_HEADS * Q_BLOCK], vals[n][first : first + span])
            mixed = mixed[:, :width] + mixed[:, width:]
            gathered = jnp.where(head_of == 0, mixed[:Q_BLOCK], 0.0)
            for h in range(1, A_HEADS):
                gathered += jnp.where(
                    head_of == h, mixed[h * Q_BLOCK : (h + 1) * Q_BLOCK], 0.0
                )
            parts.append(gathered)
        atom_out = (atoms[n] + jnp.concatenate(parts, axis=0)).astype(BF)
        hidden = jnp.maximum(dot(atom_out, agg_weight[...]), 0.0)
        sums = 0.0
        for part in two_parts(hidden):
            sums = sums + dot(member, part)
        token_normal, _ = norm_parts(sums / counts)
        _, noise_code = noise_parts(levels[n])
        token_in.append(token_normal + single_term + noise_code[:, :1] * noise_row)
    token_in = jnp.concatenate(token_in, axis=0)
    count = token_in.shape[0]
    stacked = jnp.concatenate(two_parts(token_in), axis=0)
    fetch.wait()
    proj = dot(stacked, weight_held[...])
    proj = proj[:count] + proj[count:]
    wide = H * HEAD
    cot = jnp.concatenate([cotangent[n].astype(F32) for n in range(copies)], axis=0)
    head_at = lax.broadcasted_iota(jnp.int32, (H, wide), 1) // HEAD
    mine = head_at == lax.broadcasted_iota(jnp.int32, (H, wide), 0)
    lane = lax.broadcasted_iota(jnp.int32, (H, 128 - 2 * HEAD), 1)
    codes = [jnp.zeros(lane.shape, F32)] * 2
    coded = []
    sources = [
        proj[:, :wide] * (1.0 / math.sqrt(HEAD)), cot, proj[:, wide : 2 * wide], proj[:, 2 * wide :]
    ]
    for index, source in enumerate(sources):
        top = jnp.max(jnp.abs(source), axis=0, keepdims=True)
        steps, power = grid_scale(jnp.max(jnp.where(mine, top, 0.0), axis=1, keepdims=True))
        inverse = 1.0 / scale_value(steps, power)
        inverse = jnp.max(jnp.where(mine, inverse, 0.0), axis=0, keepdims=True)
        coded.append(jnp.round(source * inverse))
        half, at = index // 2, 2 * (index % 2)
        codes[half] = jnp.where(
            lane == at, steps, jnp.where(lane == at + 1, power, codes[half])
        )
    for h in range(H):
        at = h * HEAD
        for half in range(2):
            row = [coded[2 * half + k][:, at : at + HEAD] for k in range(2)]
            row.append(jnp.broadcast_to(codes[half][h : h + 1], (count, 128 - 2 * HEAD)))
            out[h, :, half * 128 : (half + 1) * 128] = (
                jnp.concatenate(row, axis=1).astype(jnp.int32).astype(jnp.int16)
            )


def head_unit(weight):
    weight = weight.astype(F32)
    reach = jnp.sqrt(jnp.sum(weight * weight, axis=-1, keepdims=True))
    return reach * (math.sqrt(128.0) * 1.01 / 32767.0) + 1e-30


def lane_matrices(lanes):
    row_at = lax.broadcasted_iota(jnp.int32, (2 * lanes, 2 * lanes), 0)
    col_at = lax.broadcasted_iota(jnp.int32, (2 * lanes, 2 * lanes), 1)
    same = (row_at // lanes) == (col_at // lanes)
    ones = jnp.where(same, 1.0 / lanes, 0.0).astype(BF)
    centre = jnp.where(
        same, jnp.where(row_at == col_at, 1.0 - 1.0 / lanes, -1.0 / lanes), 0.0
    ).astype(BF)
    return jnp.concatenate([ones, ones], axis=0), centre


def lane_mean(value, ones):
    return dot(jnp.concatenate(two_parts(value), axis=1), ones)


def pair_block(pair, trans_in, trans_out, bias_weight_t, cond_out, store):
    inner = trans_out.shape[0]
    cols = pair.shape[1]
    lanes = 128
    ones, centre = lane_matrices(lanes)
    unit = head_unit(bias_weight_t[...])

    def normalise(value):
        half = value.shape[0] // 2
        centred = dot(jnp.concatenate([value[:half], value[half:]], axis=1), centre)
        normal = (centred * lax.rsqrt(lane_mean(centred * centred, ones) + epsilon)).astype(BF)
        return jnp.concatenate([normal[:, :lanes], normal[:, lanes:]], axis=0)

    group = 2
    chunk = 128
    weights = [
        jnp.concatenate(
            [
                trans_in[:, f : f + chunk] * 0.5,
                trans_in[:, inner + f : inner + f + chunk],
            ],
            axis=1,
        )
        for f in range(0, inner, chunk)
    ]
    count = pair.shape[0] // group
    normed, hidden, cond = {}, {}, {}

    def value_of(k):
        return pair[k * group : (k + 1) * group].reshape(group * cols, lanes)

    def gate(k, f):
        if 0 <= k < count:
            both = dot(normed[k], weights[f])
            half = both[:, :chunk]
            hidden[k, f] = ((half + half * jnp.tanh(half)) * both[:, chunk:]).astype(BF)

    def down(k):
        if 0 <= k < count:
            joined = jnp.concatenate([hidden[k, f] for f in range(len(weights))], axis=1)
            cond[k] = (value_of(k).astype(F32) + dot(joined, trans_out[...])).astype(BF)
            cond_out[k * group : (k + 1) * group] = cond[k].reshape(group, cols, lanes)

    def project(k):
        if 0 <= k < count:
            bias = dot(bias_weight_t[...], normalise(cond[k]), NT) * (1.0 / unit)
            for i in range(group):
                store(k * group + i, bias[:, i * cols : (i + 1) * cols])

    for t in range(count + 3):
        gate(t - 1, 0)
        project(t - 3)
        gate(t - 1, 1)
        down(t - 2)
        gate(t - 1, 2)
        if t < count:
            normed[t] = normalise(value_of(t))
        gate(t - 1, 3)


def pair_first_kernel(pair, trans_in, trans_out, bias_weight_t, anchor, cond_out, bias_out):
    def store(i, value):
        bias_out[:, i, :] = value

    pair_block(pair, trans_in, trans_out, bias_weight_t, cond_out, store)


def pair_next_kernel(pair, trans_in, trans_out, bias_weight_t, anchor, cond, cond_out, bias_out):
    pair_first_kernel(pair, trans_in, trans_out, bias_weight_t, anchor, cond_out, bias_out)


def pair_last_kernel(
    pair, trans_in, trans_out, bias_weight_t, anchor, cond, first, second, third, cond_out, bias_out,
    held
):
    def store(i, value):
        held[:, i, :] = value

    pair_block(pair, trans_in, trans_out, bias_weight_t, cond_out, store)
    for h in range(bias_out.shape[0]):
        parts = [first[h], second[h], third[h], held[h]]
        bias_out[h] = whole(jnp.concatenate(parts, axis=0)).astype(jnp.int16)


def pair_call(kernel, step, index, inputs, extra, anchor, cond, bias_shape, scratch=()):
    pair_rep, trans_in, trans_out, bias_t = inputs
    cols = pair_rep.shape[1]
    block = pl.BlockSpec((step, cols, 128), lambda i: (index, 0, 0))
    operands = [pair_rep, trans_in, trans_out, bias_t, anchor]
    if cond is not None:
        operands.append(cond)
    count = len(operands)
    specs = [block] + [pl.BlockSpec(x.shape, lambda i: (0, 0)) for x in operands[1:4]]
    specs += [ANY] * (count - 4)
    specs += [pl.BlockSpec(x.shape, lambda i: (0, 0, 0)) for x in extra]
    return pl.pallas_call(
        kernel,
        grid=(1,),
        out_shape=(jax.ShapeDtypeStruct(pair_rep.shape, BF), bias_shape),
        in_specs=specs,
        out_specs=(block, pl.BlockSpec(bias_shape.shape, lambda i: (0, 0, 0))),
        scratch_shapes=list(scratch),
        input_output_aliases={} if cond is None else {5: 0},
        compiler_params=params(),
        cost_estimate=pl.CostEstimate(
            flops=step * 750_000_000, bytes_accessed=step * 1_000_000, transcendentals=0
        ),
        name="pair_part",
    )(*operands, *extra)


def attend_kernel(
    core_at, head_at, z_at, queries, kv0, kv1, kv2, kv3, kv4, kv5, kv6, kv7, bias_mine, bias_other, bias_weight_t,
    update_mine, grad_other, kv
):
    core = core_at[0]
    unit = head_unit(bias_weight_t[...])
    this = lax.broadcasted_iota(jnp.int32, unit.shape, 0) == head_at[0]
    unit = jnp.sum(jnp.where(this, unit, 0.0), axis=0, keepdims=True)
    for back, block in enumerate((kv0, kv1, kv2, kv3, kv4, kv5, kv6, kv7)):
        kv[lax.rem(z_at[0] + 8 - back, 8)] = block[...]
    blocks = [core, 2 + core, 1 - core, 3 - core]
    cols = 384
    tok = 24
    rows = 8 * tok
    lane = lax.broadcasted_iota(jnp.int32, (1, 128), 1)
    is_key = lane < HEAD
    is_value = (lane >= HEAD) & (lane < 2 * HEAD)

    def decode(block):
        block = block.astype(jnp.int32).astype(F32)
        codes = block[0:1]
        at = 2 * HEAD
        first = scale_value(codes[:, at : at + 1], codes[:, at + 1 : at + 2])
        second = scale_value(codes[:, at + 2 : at + 3], codes[:, at + 3 : at + 4])
        return block * jnp.where(is_key, first, jnp.where(is_value, second, 0.0))

    bias = jnp.concatenate(
        [
            jnp.concatenate(
                [
                    (bias_mine if c < 2 else bias_other)[2 * g + c % 2].astype(jnp.int32).astype(F32)
                    for c in range(4)
                ],
                axis=1,
            )
            for g in range(8)
        ],
        axis=0,
    ) * unit
    def products_of(y, p, query_blocks, token_blocks):
        query = jnp.concatenate([b[p * tok : (p + 1) * tok] for b in query_blocks], axis=0)
        q_high, q_low = two_parts(jnp.where(is_key, query, 0.0))
        c_high, c_low = two_parts(jnp.where(is_value, query, 0.0))
        high, low = two_parts(
            jnp.concatenate([b[p * tok : (p + 1) * tok] for b in token_blocks], axis=0)
        )
        both = jnp.concatenate([high, low], axis=1)
        none = jnp.zeros_like(q_low)
        stacked = jnp.concatenate(
            [
                jnp.concatenate([q_high, q_high], axis=1),
                jnp.concatenate([q_low, none], axis=1),
                jnp.concatenate([c_high, c_high], axis=1),
                jnp.concatenate([c_low, none], axis=1),
            ],
            axis=0,
        )
        return both, dot(stacked, both, NT)

    def products_at(index):
        y, p = index // 2, index % 2
        if p == 0:
            blocks_of[y] = (
                [decode(queries[2 * g + y, :, :128]) for g in range(8)],
                [decode(kv[2 * c + z, 2 * g + y]) for c in blocks for z in range(2) for g in range(8)],
            )
        return products_of(y, p, *blocks_of[y])

    blocks_of = {}
    grad = None
    coming = products_at(0)
    for index in range(4):
        y, p = index // 2, index % 2
        both, products = coming
        if index < 3:
            coming = products_at(index + 1)
        scores = products[:rows] + products[rows : 2 * rows] + bias
        prob_grad = products[2 * rows : 3 * rows] + products[3 * rows :]
        top = jnp.max(scores, axis=-1, keepdims=True)
        weights = jnp.exp(scores - top)
        weights = weights * (1.0 / jnp.sum(weights, axis=-1, keepdims=True))
        mixed = dot(weights.astype(BF), both)
        mixed = mixed[:, :128] + mixed[:, 128:]
        for g in range(8):
            update_mine[2 * g + y, :, cols + p * HEAD : cols + (p + 1) * HEAD] = mixed[
                g * tok : (g + 1) * tok, HEAD : 2 * HEAD
            ]
        term = weights * prob_grad
        term = term - weights * jnp.sum(term, axis=-1, keepdims=True)
        grad = term if grad is None else grad + term
    for g in range(8):
        for c in range(4):
            (update_mine if c < 2 else grad_other)[2 * g + c % 2, :, :cols] = grad[
                g * tok : (g + 1) * tok, c * cols : (c + 1) * cols
            ]


def merge_kernel(mine, other, out):
    cols = other.shape[2]
    used = 2 * HEAD
    lane = lax.broadcasted_iota(jnp.int32, (1, 128), 1)
    for h in range(mine.shape[0]):
        grad = mine[h, :, :cols] + other[h]
        update = jnp.where(lane < used, mine[h, :, cols:], 0.0)
        codes = update
        scaled = []
        for at, part in ((0, grad), (2, update)):
            steps, power = grid_scale(jnp.max(jnp.abs(part), axis=-1, keepdims=True))
            scaled.append(part * (1.0 / scale_value(steps, power)))
            codes = jnp.where(lane == used + at, steps, codes)
            codes = jnp.where(lane == used + at + 1, power, codes)
        last = jnp.where(lane < used, scaled[1], codes)
        out[h] = jnp.concatenate(
            [
                whole(scaled[0][:, :256]),
                whole(jnp.concatenate([scaled[0][:, 256:], last], axis=1)),
            ],
            axis=0,
        ).astype(jnp.int16)


def grad_kernel(packed, cond, bias_weight, out, update_out, held):
    step = pl.program_id(0)
    lanes = 128
    heads, _, rows, cols = held.shape[1], 0, held.shape[2], held.shape[3]
    tok = packed.shape[1] // 2

    @pl.when(step == 0)
    def _():
        pieces = [[], []]
        for h in range(heads):
            block = packed[h].astype(jnp.int32).astype(F32)
            low, high = block[:tok], block[tok:]
            at = lanes + 2 * HEAD
            grad_scale = scale_value(high[:, at : at + 1], high[:, at + 1 : at + 2])
            update_scale = scale_value(high[:, at + 2 : at + 3], high[:, at + 3 : at + 4])
            grad = jnp.concatenate([low, high[:, :lanes]], axis=1) * grad_scale
            for s in range(held.shape[0]):
                held[s, h] = grad[s * rows : (s + 1) * rows]
            for p in range(2):
                pieces[p].append(
                    high[:, lanes + p * HEAD : lanes + (p + 1) * HEAD] * update_scale
                )
        for p in range(2):
            update_out[p] = jnp.concatenate(pieces[p], axis=1).astype(BF)

    ones, centre = lane_matrices(lanes)
    weight = bias_weight[...].astype(F32)
    w_high, w_low = two_parts(weight - jnp.mean(weight, axis=-1, keepdims=True))
    parts = jnp.concatenate([w_high, w_high, w_high, w_low, w_low], axis=0)
    group = 4
    count = group * cols
    half = count // 2

    def paired(value):
        return jnp.concatenate([value[:half], value[half:]], axis=1)

    for part in range(rows // group):
        grad = jnp.concatenate(
            [held[step, :, part * group + i, :] for i in range(group)], axis=1
        )
        high, middle, low = three_parts(grad)
        stacked = jnp.concatenate([high, middle, low, high, middle], axis=0)
        grad_normal = paired(dot(stacked, parts, TN))
        value = cond[part * group : (part + 1) * group].reshape(count, lanes)
        centred = dot(paired(value), centre)
        scale = lax.rsqrt(lane_mean(centred * centred, ones) + epsilon)
        normal = centred * scale
        result = ((grad_normal - normal * lane_mean(grad_normal * normal, ones)) * scale).astype(BF)
        result = jnp.concatenate([result[:, :lanes], result[:, lanes:]], axis=0)
        out[part * group : (part + 1) * group] = result.reshape(group, cols, lanes)


def params(**more):
    return pltpu.CompilerParams(vmem_limit_bytes=56 * 1024 * 1024, **more)


VMEM = pl.BlockSpec(memory_space=pltpu.VMEM)
SMEM = pl.BlockSpec(memory_space=pltpu.SMEM)
ANY = pl.BlockSpec(memory_space=pl.ANY)


def on_device(
    pair_rep,
    single,
    atom_feat,
    coords,
    levels,
    window_offset,
    atom_token,
    trans_in,
    trans_out,
    bias_weight,
    single_weight,
    coord_weight,
    atom_weight,
    agg_weight,
    token_weight,
    noise_weight,
    cotangent,
):
    tile_index = lax.axis_index(TILE).astype(jnp.int32)
    core_index = lax.axis_index("core").astype(jnp.int32)
    copies, tok_rows, width = cotangent.shape
    atom_rows, atom_width = atom_feat.shape
    cols = pair_rep.shape[1]
    rim = K_WIN // 2
    atoms, normed, first, last = pl.pallas_call(
        start_kernel,
        out_shape=(
            jax.ShapeDtypeStruct((copies, atom_rows, atom_width), F32),
            jax.ShapeDtypeStruct((copies, atom_rows, atom_width), BF),
            jax.ShapeDtypeStruct((copies, rim, atom_width), BF),
            jax.ShapeDtypeStruct((copies, rim, atom_width), BF),
        ),
        in_specs=[SMEM] + [VMEM] * 3,
        out_specs=(VMEM,) * 4,
        compiler_params=params(),
        cost_estimate=pl.CostEstimate(flops=1_000_000, bytes_accessed=500_000, transcendentals=0),
        name="atom_start",
    )(levels, atom_feat, coords, coord_weight)
    forward = [(i, i + 1) for i in range(63)]
    backward = [(i + 1, i) for i in range(63)]
    low = lax.ppermute(last, TILE, forward)
    high = lax.ppermute(first, TILE, backward)
    bias_t = bias_weight.T
    inputs = (pair_rep, trans_in, trans_out, bias_t)
    step = 8
    part_bias = jax.ShapeDtypeStruct((H, step, cols), F32)
    cond, bias_first = pair_call(pair_first_kernel, step, 0, inputs, [], last, None, part_bias)
    low, high, bias_first = lax.optimization_barrier((low, high, bias_first))
    packed = pl.pallas_call(
        atom_kernel,
        out_shape=jax.ShapeDtypeStruct((H, copies * tok_rows, 256), jnp.int16),
        in_specs=[SMEM] * 3 + [VMEM] * 10 + [ANY, VMEM],
        out_specs=VMEM,
        scratch_shapes=[pltpu.VMEM(token_weight.shape, BF), pltpu.SemaphoreType.DMA],
        compiler_params=params(),
        cost_estimate=pl.CostEstimate(flops=3_000_000_000, bytes_accessed=6_000_000, transcendentals=0),
        name="atom_stage",
    )(
        tile_index[None], window_offset, levels, low, high, normed, atoms, atom_weight, agg_weight,
        atom_token, single, single_weight, noise_weight, token_weight, cotangent,
    )
    cond, bias_second = pair_call(
        pair_next_kernel, step, 1, inputs, [], packed, cond, part_bias
    )
    packed = lax.all_to_all(packed, PLANE, 0, 0, tiled=True)
    packed, bias_second = lax.optimization_barrier((packed, bias_second))
    own = packed[:, :, 128:]
    ahead = [(i, (i + 1) % 8) for i in range(8)]
    behind = [(i, (i + 7) % 8) for i in range(8)]
    rising = [own, lax.ppermute(own, "z", ahead)]
    falling = [own, lax.ppermute(own, "z", behind)]
    small = step // 2
    small_bias = jax.ShapeDtypeStruct((H, small, cols), F32)
    cond, bias_third = pair_call(
        pair_next_kernel, small, 4, inputs, [], own, cond, small_bias
    )
    rising[1], falling[1], bias_third = lax.optimization_barrier(
        (rising[1], falling[1], bias_third)
    )
    rising.append(lax.ppermute(rising[1], "z", ahead))
    falling.append(lax.ppermute(falling[1], "z", behind))
    cond, bias = pair_call(
        pair_last_kernel, small, 5, inputs, [bias_first, bias_second, bias_third], rising[1], cond,
        jax.ShapeDtypeStruct((H, tok_rows, cols), jnp.int16), [pltpu.VMEM((H, small, cols), F32)],
    )
    rising[2], falling[2], bias = lax.optimization_barrier((rising[2], falling[2], bias))
    rising.append(lax.ppermute(rising[2], "z", ahead))
    falling.append(lax.ppermute(falling[2], "z", behind))
    rising.append(lax.ppermute(rising[3], "z", ahead))
    every = rising + [falling[3], falling[2], falling[1]]
    steps = tok_rows // step
    bias_mine = lax.all_to_all(bias, PLANE, 0, 0, tiled=True)
    swap = [(0, 1), (1, 0)]
    bias_other = lax.ppermute(bias_mine, "core", swap)

    head_index = lax.axis_index(PLANE).astype(jnp.int32)
    z_index = lax.axis_index("z").astype(jnp.int32)
    grad_mine, grad_other = pl.pallas_call(
        attend_kernel,
        out_shape=(
            jax.ShapeDtypeStruct((H, tok_rows, cols + 128), F32),
            jax.ShapeDtypeStruct((H, tok_rows, cols), F32),
        ),
        in_specs=[SMEM] * 3 + [VMEM] * 12,
        out_specs=(VMEM, VMEM),
        scratch_shapes=[pltpu.VMEM((8,) + own.shape, jnp.int16)],
        compiler_params=params(),
        cost_estimate=pl.CostEstimate(flops=4_000_000_000, bytes_accessed=8_000_000, transcendentals=1_200_000),
        name="token_attention",
    )(
        core_index[None], head_index[None], z_index[None], packed, *every, bias_mine, bias_other, bias_t
    )
    merged = pl.pallas_call(
        merge_kernel,
        out_shape=jax.ShapeDtypeStruct((H, 2 * tok_rows, 256), jnp.int16),
        in_specs=[VMEM] * 2,
        out_specs=VMEM,
        compiler_params=params(),
        cost_estimate=pl.CostEstimate(flops=2_000_000, bytes_accessed=2_000_000, transcendentals=0),
        name="gradient_merge",
    )(grad_mine, lax.ppermute(grad_other, "core", swap))
    merged = lax.all_to_all(merged, PLANE, 0, 0, tiled=True)
    gradient, update = pl.pallas_call(
        grad_kernel,
        grid=(steps,),
        out_shape=(
            jax.ShapeDtypeStruct(pair_rep.shape, BF),
            jax.ShapeDtypeStruct(cotangent.shape, BF),
        ),
        in_specs=[
            pl.BlockSpec(merged.shape, lambda i: (0, 0, 0)),
            pl.BlockSpec((step, cols, 128), lambda i: (i, 0, 0)),
            pl.BlockSpec(bias_t.shape, lambda i: (0, 0)),
        ],
        out_specs=(
            pl.BlockSpec((step, cols, 128), lambda i: (i, 0, 0)),
            pl.BlockSpec(cotangent.shape, lambda i: (0, 0, 0)),
        ),
        scratch_shapes=[pltpu.VMEM((steps, H, step, cols), F32)],
        compiler_params=params(),
        cost_estimate=pl.CostEstimate(flops=400_000_000, bytes_accessed=6_000_000, transcendentals=0),
        name="pair_gradient",
    )(merged, cond, bias_t)
    return (update, gradient)


def solution(mesh):
    fine = Mesh(mesh.devices.reshape(8, 8, 2, 2), ("z", "g", "ylo", "core"))
    placed = (
        P(TILE, COPY, None),
        P(TILE, None),
        P(TILE, None),
        P(COPY, None, TILE),
        P(COPY),
        P(TILE),
        P(TILE),
        P(),
        P(),
        P(),
        P(),
        P(),
        P(),
        P(),
        P(),
        P(),
        P(COPY, TILE, None),
    )
    return jax.shard_map(
        on_device,
        mesh=fine,
        in_specs=placed,
        out_specs=(P(COPY, TILE, None), P(TILE, COPY, None)),
        check_vma=False,
    )
```

```python
import math

import jax
import jax.numpy as jnp
from jax import lax
from jax.experimental import pallas as pl
from jax.experimental.pallas import tpu as pltpu
from jax.sharding import Mesh, PartitionSpec as P

A_HEAD = 32
A_HEADS = 4
Q_BLOCK = 32
K_WIN = 128
LEVELS = 200
HEAD = 48
H = 16

epsilon = 1e-05
sigma_data = 16.0
sigma_top = 160.0
sigma_low = 0.0004
rho_power = 7.0
excluded = -1e30
TILE = ("z", "g")
COPY = ("ylo", "core")
PLANE = ("g", "ylo")
BF = jnp.bfloat16
F32 = jnp.float32
NT = (((1,), (1,)), ((), ()))
NN = (((1,), (0,)), ((), ()))
TN = (((0,), (0,)), ((), ()))


def norm_parts(value):
    average = jnp.mean(value, axis=-1, keepdims=True)
    centred = value - average
    spread = jnp.mean(centred * centred, axis=-1, keepdims=True)
    scale = lax.rsqrt(spread + epsilon)
    return (centred * scale, scale)


def noise_parts(level):
    fraction = jnp.full((1, 128), level, jnp.int32).astype(F32) / LEVELS
    highest = sigma_top ** (1.0 / rho_power)
    lowest = sigma_low ** (1.0 / rho_power)
    root = highest + fraction * (lowest - highest)
    square = root * root
    sigma = sigma_data * (square * square * square * root)
    input_scale = lax.rsqrt(sigma * sigma + sigma_data * sigma_data)
    noise_code = 0.25 * jnp.log(sigma / sigma_data)
    return (input_scale, noise_code)


def dot(a, b, dims=NN):
    return lax.dot_general(a, b, dims, preferred_element_type=F32)


def two_parts(value):
    high = value.astype(BF)
    low = (value - high.astype(F32)).astype(BF)
    return high, low


def three_parts(value):
    high = value.astype(BF)
    rest = value - high.astype(F32)
    middle = rest.astype(BF)
    low = (rest - middle.astype(F32)).astype(BF)
    return high, middle, low


def grid_scale(top):
    top = jnp.maximum(top, 1e-30)
    power = jnp.ceil(jnp.log2(top))
    steps = jnp.ceil(top * jnp.exp2(13.0 - power)) + 1.0
    return steps, power


def scale_value(steps, power):
    return steps * jnp.exp2(power - 13.0) * (1.0 / 32767.0)


def whole(value):
    return jnp.round(value).astype(jnp.int32)


def start_kernel(levels, feat, coords, coord_weight, atoms_out, normed_out, first_out, last_out):
    rows = feat.shape[0]
    rim = K_WIN // 2
    for n in range(coords.shape[0]):
        input_scale, _ = noise_parts(levels[n])
        scaled = coords[n] * input_scale[:, :1]
        atoms = feat[...].astype(F32) + lax.dot_general(
            scaled, coord_weight[...], TN, precision=lax.Precision.HIGHEST, preferred_element_type=F32
        )
        normal, _ = norm_parts(atoms)
        normal = normal.astype(BF)
        atoms_out[n] = atoms
        normed_out[n] = normal
        first_out[n] = normal[:rim]
        last_out[n] = normal[rows - rim :]


def atom_kernel(
    place, offsets, levels, low, high, normed, atoms, atom_weight, agg_weight, atom_token,
    single, single_weight, noise_weight, token_weight, cotangent, out, weight_held, arrival
):
    tile = place[0]
    fetch = pltpu.make_async_copy(token_weight, weight_held, arrival)
    fetch.start()
    copies, rows, width = normed.shape
    blocks = rows // Q_BLOCK
    span = K_WIN + Q_BLOCK
    rim = K_WIN // 2
    total = 64 * rows
    tok_rows = single.shape[0]
    head_of = lax.broadcasted_iota(jnp.int32, (Q_BLOCK, width), 1) // A_HEAD
    twice_head = lax.broadcasted_iota(jnp.int32, (Q_BLOCK, 2 * width), 1) % width // A_HEAD
    reach = lax.broadcasted_iota(jnp.int32, (1, span), 1)
    local_token = atom_token[...].reshape(1, rows) - tile * tok_rows
    member = (lax.broadcasted_iota(jnp.int32, (tok_rows, rows), 0) == local_token).astype(F32)
    counts = jnp.sum(member, axis=1, keepdims=True)
    member = member.astype(BF)
    single_term = dot(single[...], single_weight[...])
    noise_row = noise_weight[...].reshape(1, noise_weight.shape[0])
    scores = []
    vals = []
    for n in range(copies):
        ext = jnp.concatenate([low[n], normed[n], high[n]], axis=0)
        proj = dot(ext, atom_weight[...])
        queries = proj[rim : rim + rows, :width] * (1.0 / math.sqrt(A_HEAD))
        q_high, q_low = two_parts(queries)
        key_high, key_low = two_parts(proj[:, width : 2 * width])
        keys = jnp.concatenate([key_high, key_low], axis=1)
        vals.append(jnp.concatenate(two_parts(proj[:, 2 * width :]), axis=1))
        twice = jnp.concatenate([q_high, q_high], axis=1)
        once = jnp.concatenate([q_low, jnp.zeros_like(q_low)], axis=1)
        blank = jnp.zeros((Q_BLOCK, 2 * width), BF)
        for b in range(blocks):
            first = b * Q_BLOCK
            stacked = jnp.concatenate(
                [
                    jnp.where(twice_head == h, part[first : first + Q_BLOCK], blank)
                    for part in (twice, once)
                    for h in range(A_HEADS)
                ],
                axis=0,
            )
            both = dot(stacked, keys[first : first + span], NT)
            offset = offsets[b]
            position = tile * rows + first - rim + reach
            inside = (
                (reach >= offset)
                & (reach < offset + K_WIN)
                & (position >= 0)
                & (position < total)
            )
            half = A_HEADS * Q_BLOCK
            scores.append(jnp.where(inside, both[:half] + both[half:], excluded))
    scores = jnp.concatenate(scores, axis=0)
    weights = jnp.exp(scores - jnp.max(scores, axis=-1, keepdims=True))
    weights = weights * (1.0 / jnp.sum(weights, axis=-1, keepdims=True))
    weights = weights.astype(BF)
    token_in = []
    for n in range(copies):
        parts = []
        for b in range(blocks):
            first = b * Q_BLOCK
            at = (n * blocks + b) * A_HEADS * Q_BLOCK
            mixed = dot(weights[at : at + A_HEADS * Q_BLOCK], vals[n][first : first + span])
            mixed = mixed[:, :width] + mixed[:, width:]
            gathered = jnp.where(head_of == 0, mixed[:Q_BLOCK], 0.0)
            for h in range(1, A_HEADS):
                gathered += jnp.where(
                    head_of == h, mixed[h * Q_BLOCK : (h + 1) * Q_BLOCK], 0.0
                )
            parts.append(gathered)
        atom_out = (atoms[n] + jnp.concatenate(parts, axis=0)).astype(BF)
        hidden = jnp.maximum(dot(atom_out, agg_weight[...]), 0.0)
        sums = 0.0
        for part in two_parts(hidden):
            sums = sums + dot(member, part)
        token_normal, _ = norm_parts(sums / counts)
        _, noise_code = noise_parts(levels[n])
        token_in.append(token_normal + single_term + noise_code[:, :1] * noise_row)
    token_in = jnp.concatenate(token_in, axis=0)
    count = token_in.shape[0]
    stacked = jnp.concatenate(two_parts(token_in), axis=0)
    fetch.wait()
    proj = dot(stacked, weight_held[...])
    proj = proj[:count] + proj[count:]
    wide = H * HEAD
    cot = jnp.concatenate([cotangent[n].astype(F32) for n in range(copies)], axis=0)
    head_at = lax.broadcasted_iota(jnp.int32, (H, wide), 1) // HEAD
    mine = head_at == lax.broadcasted_iota(jnp.int32, (H, wide), 0)
    lane = lax.broadcasted_iota(jnp.int32, (H, 128 - 2 * HEAD), 1)
    codes = [jnp.zeros(lane.shape, F32)] * 2
    coded = []
    sources = [
        proj[:, :wide] * (1.0 / math.sqrt(HEAD)), cot, proj[:, wide : 2 * wide], proj[:, 2 * wide :]
    ]
    for index, source in enumerate(sources):
        top = jnp.max(jnp.abs(source), axis=0, keepdims=True)
        steps, power = grid_scale(jnp.max(jnp.where(mine, top, 0.0), axis=1, keepdims=True))
        inverse = 1.0 / scale_value(steps, power)
        inverse = jnp.max(jnp.where(mine, inverse, 0.0), axis=0, keepdims=True)
        coded.append(jnp.round(source * inverse))
        half, at = index // 2, 2 * (index % 2)
        codes[half] = jnp.where(
            lane == at, steps, jnp.where(lane == at + 1, power, codes[half])
        )
    for h in range(H):
        at = h * HEAD
        for half in range(2):
            row = [coded[2 * half + k][:, at : at + HEAD] for k in range(2)]
            row.append(jnp.broadcast_to(codes[half][h : h + 1], (count, 128 - 2 * HEAD)))
            out[h, :, half * 128 : (half + 1) * 128] = (
                jnp.concatenate(row, axis=1).astype(jnp.int32).astype(jnp.int16)
            )


def head_unit(weight):
    weight = weight.astype(F32)
    reach = jnp.sqrt(jnp.sum(weight * weight, axis=-1, keepdims=True))
    return reach * (math.sqrt(128.0) * 1.01 / 32767.0) + 1e-30


def lane_matrices(lanes):
    row_at = lax.broadcasted_iota(jnp.int32, (2 * lanes, 2 * lanes), 0)
    col_at = lax.broadcasted_iota(jnp.int32, (2 * lanes, 2 * lanes), 1)
    same = (row_at // lanes) == (col_at // lanes)
    ones = jnp.where(same, 1.0 / lanes, 0.0).astype(BF)
    centre = jnp.where(
        same, jnp.where(row_at == col_at, 1.0 - 1.0 / lanes, -1.0 / lanes), 0.0
    ).astype(BF)
    return jnp.concatenate([ones, ones], axis=0), centre


def lane_mean(value, ones):
    return dot(jnp.concatenate(two_parts(value), axis=1), ones)


def pair_block(pair, trans_in, trans_out, bias_weight_t, cond_out, store):
    inner = trans_out.shape[0]
    cols = pair.shape[1]
    lanes = 128
    ones, centre = lane_matrices(lanes)
    unit = head_unit(bias_weight_t[...])

    def normalise(value):
        half = value.shape[0] // 2
        centred = dot(jnp.concatenate([value[:half], value[half:]], axis=1), centre)
        normal = (centred * lax.rsqrt(lane_mean(centred * centred, ones) + epsilon)).astype(BF)
        return jnp.concatenate([normal[:, :lanes], normal[:, lanes:]], axis=0)

    group = 2
    chunk = 128
    weights = [
        jnp.concatenate(
            [
                trans_in[:, f : f + chunk] * 0.5,
                trans_in[:, inner + f : inner + f + chunk],
            ],
            axis=1,
        )
        for f in range(0, inner, chunk)
    ]
    count = pair.shape[0] // group
    normed, hidden, cond = {}, {}, {}

    def value_of(k):
        return pair[k * group : (k + 1) * group].reshape(group * cols, lanes)

    def gate(k, f):
        if 0 <= k < count:
            both = dot(normed[k], weights[f])
            half = both[:, :chunk]
            hidden[k, f] = ((half + half * jnp.tanh(half)) * both[:, chunk:]).astype(BF)

    def down(k):
        if 0 <= k < count:
            joined = jnp.concatenate([hidden[k, f] for f in range(len(weights))], axis=1)
            cond[k] = (value_of(k).astype(F32) + dot(joined, trans_out[...])).astype(BF)
            cond_out[k * group : (k + 1) * group] = cond[k].reshape(group, cols, lanes)

    def project(k):
        if 0 <= k < count:
            bias = dot(bias_weight_t[...], normalise(cond[k]), NT) * (1.0 / unit)
            for i in range(group):
                store(k * group + i, bias[:, i * cols : (i + 1) * cols])

    for t in range(count + 3):
        gate(t - 1, 0)
        project(t - 3)
        gate(t - 1, 1)
        down(t - 2)
        gate(t - 1, 2)
        if t < count:
            normed[t] = normalise(value_of(t))
        gate(t - 1, 3)


def pair_first_kernel(pair, trans_in, trans_out, bias_weight_t, anchor, cond_out, bias_out):
    def store(i, value):
        bias_out[:, i, :] = value

    pair_block(pair, trans_in, trans_out, bias_weight_t, cond_out, store)


def pair_next_kernel(pair, trans_in, trans_out, bias_weight_t, anchor, cond, cond_out, bias_out):
    pair_first_kernel(pair, trans_in, trans_out, bias_weight_t, anchor, cond_out, bias_out)


def pair_last_kernel(
    pair, trans_in, trans_out, bias_weight_t, anchor, cond, first, second, cond_out, bias_out, held
):
    def store(i, value):
        held[:, i, :] = value

    pair_block(pair, trans_in, trans_out, bias_weight_t, cond_out, store)
    for h in range(bias_out.shape[0]):
        parts = [first[h], second[h], held[h]]
        bias_out[h] = whole(jnp.concatenate(parts, axis=0)).astype(jnp.int16)


def pair_call(kernel, step, index, inputs, extra, anchor, cond, bias_shape, scratch=(), room=56):
    pair_rep, trans_in, trans_out, bias_t = inputs
    cols = pair_rep.shape[1]
    block = pl.BlockSpec((step, cols, 128), lambda i: (index, 0, 0))
    operands = [pair_rep, trans_in, trans_out, bias_t, anchor]
    if cond is not None:
        operands.append(cond)
    count = len(operands)
    specs = [block] + [pl.BlockSpec(x.shape, lambda i: (0, 0)) for x in operands[1:4]]
    specs += [ANY] * (count - 4)
    specs += [pl.BlockSpec(x.shape, lambda i: (0, 0, 0)) for x in extra]
    return pl.pallas_call(
        kernel,
        grid=(1,),
        out_shape=(jax.ShapeDtypeStruct(pair_rep.shape, BF), bias_shape),
        in_specs=specs,
        out_specs=(block, pl.BlockSpec(bias_shape.shape, lambda i: (0, 0, 0))),
        scratch_shapes=list(scratch),
        input_output_aliases={} if cond is None else {5: 0},
        compiler_params=params(room),
        cost_estimate=pl.CostEstimate(
            flops=step * 750_000_000, bytes_accessed=step * 1_000_000, transcendentals=0
        ),
        name="pair_part",
    )(*operands, *extra)


def attend_kernel(
    core_at, head_at, z_at, queries, kv0, kv1, kv2, kv3, kv4, kv5, kv6, kv7, bias_mine, bias_other, bias_weight_t,
    update_mine, grad_other, kv
):
    core = core_at[0]
    unit = head_unit(bias_weight_t[...])
    this = lax.broadcasted_iota(jnp.int32, unit.shape, 0) == head_at[0]
    unit = jnp.sum(jnp.where(this, unit, 0.0), axis=0, keepdims=True)
    for back, block in enumerate((kv0, kv1, kv2, kv3, kv4, kv5, kv6, kv7)):
        kv[lax.rem(z_at[0] + 8 - back, 8)] = block[...]
    blocks = [core, 2 + core, 1 - core, 3 - core]
    cols = 384
    tok = 24
    rows = 8 * tok
    lane = lax.broadcasted_iota(jnp.int32, (1, 128), 1)
    is_key = lane < HEAD
    is_value = (lane >= HEAD) & (lane < 2 * HEAD)

    def decode(block):
        block = block.astype(jnp.int32).astype(F32)
        codes = block[0:1]
        at = 2 * HEAD
        first = scale_value(codes[:, at : at + 1], codes[:, at + 1 : at + 2])
        second = scale_value(codes[:, at + 2 : at + 3], codes[:, at + 3 : at + 4])
        return block * jnp.where(is_key, first, jnp.where(is_value, second, 0.0))

    bias = jnp.concatenate(
        [
            jnp.concatenate(
                [
                    (bias_mine if c < 2 else bias_other)[2 * g + c % 2].astype(jnp.int32).astype(F32)
                    for c in range(4)
                ],
                axis=1,
            )
            for g in range(8)
        ],
        axis=0,
    ) * unit
    def products_of(y, p, query_blocks, token_blocks):
        query = jnp.concatenate([b[p * tok : (p + 1) * tok] for b in query_blocks], axis=0)
        q_high, q_low = two_parts(jnp.where(is_key, query, 0.0))
        c_high, c_low = two_parts(jnp.where(is_value, query, 0.0))
        high, low = two_parts(
            jnp.concatenate([b[p * tok : (p + 1) * tok] for b in token_blocks], axis=0)
        )
        both = jnp.concatenate([high, low], axis=1)
        none = jnp.zeros_like(q_low)
        stacked = jnp.concatenate(
            [
                jnp.concatenate([q_high, q_high], axis=1),
                jnp.concatenate([q_low, none], axis=1),
                jnp.concatenate([c_high, c_high], axis=1),
                jnp.concatenate([c_low, none], axis=1),
            ],
            axis=0,
        )
        return both, dot(stacked, both, NT)

    def products_at(index):
        y, p = index // 2, index % 2
        if p == 0:
            blocks_of[y] = (
                [decode(queries[2 * g + y, :, :128]) for g in range(8)],
                [decode(kv[2 * c + z, 2 * g + y]) for c in blocks for z in range(2) for g in range(8)],
            )
        return products_of(y, p, *blocks_of[y])

    blocks_of = {}
    grad = None
    coming = products_at(0)
    for index in range(4):
        y, p = index // 2, index % 2
        both, products = coming
        if index < 3:
            coming = products_at(index + 1)
        scores = products[:rows] + products[rows : 2 * rows] + bias
        prob_grad = products[2 * rows : 3 * rows] + products[3 * rows :]
        top = jnp.max(scores, axis=-1, keepdims=True)
        weights = jnp.exp(scores - top)
        weights = weights * (1.0 / jnp.sum(weights, axis=-1, keepdims=True))
        mixed = dot(weights.astype(BF), both)
        mixed = mixed[:, :128] + mixed[:, 128:]
        for g in range(8):
            update_mine[2 * g + y, :, cols + p * HEAD : cols + (p + 1) * HEAD] = mixed[
                g * tok : (g + 1) * tok, HEAD : 2 * HEAD
            ]
        term = weights * prob_grad
        term = term - weights * jnp.sum(term, axis=-1, keepdims=True)
        grad = term if grad is None else grad + term
    for g in range(8):
        for c in range(4):
            (update_mine if c < 2 else grad_other)[2 * g + c % 2, :, :cols] = grad[
                g * tok : (g + 1) * tok, c * cols : (c + 1) * cols
            ]


def merge_kernel(mine, other, out):
    cols = other.shape[2]
    used = 2 * HEAD
    lane = lax.broadcasted_iota(jnp.int32, (1, 128), 1)
    for h in range(mine.shape[0]):
        grad = mine[h, :, :cols] + other[h]
        update = jnp.where(lane < used, mine[h, :, cols:], 0.0)
        codes = update
        scaled = []
        for at, part in ((0, grad), (2, update)):
            steps, power = grid_scale(jnp.max(jnp.abs(part), axis=-1, keepdims=True))
            scaled.append(part * (1.0 / scale_value(steps, power)))
            codes = jnp.where(lane == used + at, steps, codes)
            codes = jnp.where(lane == used + at + 1, power, codes)
        last = jnp.where(lane < used, scaled[1], codes)
        out[h] = jnp.concatenate(
            [
                whole(scaled[0][:, :256]),
                whole(jnp.concatenate([scaled[0][:, 256:], last], axis=1)),
            ],
            axis=0,
        ).astype(jnp.int16)


def normal_kernel(cond, anchor, normal_out, scale_out):
    rows, cols, lanes = cond.shape
    ones, centre = lane_matrices(lanes)
    group = 4
    for part in range(rows // group):
        value = cond[part * group : (part + 1) * group].reshape(group * cols, lanes)
        half = group * cols // 2
        centred = dot(jnp.concatenate([value[:half], value[half:]], axis=1), centre)
        scale = lax.rsqrt(lane_mean(centred * centred, ones) + epsilon)
        normal_out[part] = centred * scale
        scale_out[part] = scale


def grad_kernel(packed, normals, scales, bias_weight, out, update_out, held):
    step = pl.program_id(0)
    lanes = 128
    heads, _, rows, cols = held.shape[1], 0, held.shape[2], held.shape[3]
    tok = packed.shape[1] // 2

    @pl.when(step == 0)
    def _():
        pieces = [[], []]
        for h in range(heads):
            block = packed[h].astype(jnp.int32).astype(F32)
            low, high = block[:tok], block[tok:]
            at = lanes + 2 * HEAD
            grad_scale = scale_value(high[:, at : at + 1], high[:, at + 1 : at + 2])
            update_scale = scale_value(high[:, at + 2 : at + 3], high[:, at + 3 : at + 4])
            grad = jnp.concatenate([low, high[:, :lanes]], axis=1) * grad_scale
            for s in range(held.shape[0]):
                held[s, h] = grad[s * rows : (s + 1) * rows]
            for p in range(2):
                pieces[p].append(
                    high[:, lanes + p * HEAD : lanes + (p + 1) * HEAD] * update_scale
                )
        for p in range(2):
            update_out[p] = jnp.concatenate(pieces[p], axis=1).astype(BF)

    ones, _ = lane_matrices(lanes)
    weight = bias_weight[...].astype(F32)
    w_high, w_low = two_parts(weight - jnp.mean(weight, axis=-1, keepdims=True))
    parts = jnp.concatenate([w_high, w_high, w_high, w_low, w_low], axis=0)
    group = 4
    count = group * cols
    half = count // 2

    def paired(value):
        return jnp.concatenate([value[:half], value[half:]], axis=1)

    for part in range(rows // group):
        grad = jnp.concatenate(
            [held[step, :, part * group + i, :] for i in range(group)], axis=1
        )
        high, middle, low = three_parts(grad)
        stacked = jnp.concatenate([high, middle, low, high, middle], axis=0)
        grad_normal = paired(dot(stacked, parts, TN))
        normal = normals[step * (rows // group) + part]
        scale = scales[step * (rows // group) + part]
        result = ((grad_normal - normal * lane_mean(grad_normal * normal, ones)) * scale).astype(BF)
        result = jnp.concatenate([result[:, :lanes], result[:, lanes:]], axis=0)
        out[part * group : (part + 1) * group] = result.reshape(group, cols, lanes)


def params(mebibytes):
    return pltpu.CompilerParams(vmem_limit_bytes=mebibytes * 1024 * 1024)


VMEM = pl.BlockSpec(memory_space=pltpu.VMEM)
SMEM = pl.BlockSpec(memory_space=pltpu.SMEM)
ANY = pl.BlockSpec(memory_space=pl.ANY)


def on_device(
    pair_rep,
    single,
    atom_feat,
    coords,
    levels,
    window_offset,
    atom_token,
    trans_in,
    trans_out,
    bias_weight,
    single_weight,
    coord_weight,
    atom_weight,
    agg_weight,
    token_weight,
    noise_weight,
    cotangent,
):
    tile_index = lax.axis_index(TILE).astype(jnp.int32)
    core_index = lax.axis_index("core").astype(jnp.int32)
    copies, tok_rows, width = cotangent.shape
    atom_rows, atom_width = atom_feat.shape
    cols = pair_rep.shape[1]
    rim = K_WIN // 2
    atoms, normed, first, last = pl.pallas_call(
        start_kernel,
        out_shape=(
            jax.ShapeDtypeStruct((copies, atom_rows, atom_width), F32),
            jax.ShapeDtypeStruct((copies, atom_rows, atom_width), BF),
            jax.ShapeDtypeStruct((copies, rim, atom_width), BF),
            jax.ShapeDtypeStruct((copies, rim, atom_width), BF),
        ),
        in_specs=[SMEM] + [VMEM] * 3,
        out_specs=(VMEM,) * 4,
        compiler_params=params(56),
        cost_estimate=pl.CostEstimate(flops=1_000_000, bytes_accessed=500_000, transcendentals=0),
        name="atom_start",
    )(levels, atom_feat, coords, coord_weight)
    forward = [(i, i + 1) for i in range(63)]
    backward = [(i + 1, i) for i in range(63)]
    low = lax.ppermute(last, TILE, forward)
    high = lax.ppermute(first, TILE, backward)
    bias_t = bias_weight.T
    inputs = (pair_rep, trans_in, trans_out, bias_t)
    step = 8
    part_bias = jax.ShapeDtypeStruct((H, step, cols), F32)
    cond, bias_first = pair_call(
        pair_first_kernel, step, 0, inputs, [], last, None, part_bias
    )
    low, high, bias_first = lax.optimization_barrier((low, high, bias_first))
    packed = pl.pallas_call(
        atom_kernel,
        out_shape=jax.ShapeDtypeStruct((H, copies * tok_rows, 256), jnp.int16),
        in_specs=[SMEM] * 3 + [VMEM] * 10 + [ANY, VMEM],
        out_specs=VMEM,
        scratch_shapes=[pltpu.VMEM(token_weight.shape, BF), pltpu.SemaphoreType.DMA],
        compiler_params=params(56),
        cost_estimate=pl.CostEstimate(flops=3_000_000_000, bytes_accessed=6_000_000, transcendentals=0),
        name="atom_stage",
    )(
        tile_index[None], window_offset, levels, low, high, normed, atoms, atom_weight, agg_weight,
        atom_token, single, single_weight, noise_weight, token_weight, cotangent,
    )
    cond, bias_second = pair_call(
        pair_next_kernel, step, 1, inputs, [], packed, cond, part_bias
    )
    packed = lax.all_to_all(packed, PLANE, 0, 0, tiled=True)
    packed, bias_second = lax.optimization_barrier((packed, bias_second))
    own = packed[:, :, 128:]
    ahead = [(i, (i + 1) % 8) for i in range(8)]
    behind = [(i, (i + 7) % 8) for i in range(8)]
    rising = [own, lax.ppermute(own, "z", ahead)]
    falling = [own, lax.ppermute(own, "z", behind)]
    cond, bias = pair_call(
        pair_last_kernel, step, 2, inputs, [bias_first, bias_second], own, cond,
        jax.ShapeDtypeStruct((H, tok_rows, cols), jnp.int16), [pltpu.VMEM((H, step, cols), F32)],
    )
    rising[1], falling[1], bias = lax.optimization_barrier((rising[1], falling[1], bias))
    rising.append(lax.ppermute(rising[1], "z", ahead))
    falling.append(lax.ppermute(falling[1], "z", behind))
    rising.append(lax.ppermute(rising[2], "z", ahead))
    falling.append(lax.ppermute(falling[2], "z", behind))
    rising.append(lax.ppermute(rising[3], "z", ahead))
    steps = tok_rows // step
    bias_mine = lax.all_to_all(bias, PLANE, 0, 0, tiled=True)
    swap = [(0, 1), (1, 0)]
    bias_other = lax.ppermute(bias_mine, "core", swap)

    pieces = (tok_rows // 4, 2 * cols, 256)
    normals, scales = pl.pallas_call(
        normal_kernel,
        out_shape=(jax.ShapeDtypeStruct(pieces, F32),) * 2,
        in_specs=[VMEM, ANY],
        out_specs=(VMEM, VMEM),
        compiler_params=params(20),
        cost_estimate=pl.CostEstimate(flops=1_500_000_000, bytes_accessed=12_000_000, transcendentals=0),
        name="pair_normal",
    )(cond, rising[3])
    rising[4], normals, scales = lax.optimization_barrier((rising[4], normals, scales))
    every = rising + [falling[3], falling[2], falling[1]]
    head_index = lax.axis_index(PLANE).astype(jnp.int32)
    z_index = lax.axis_index("z").astype(jnp.int32)
    grad_mine, grad_other = pl.pallas_call(
        attend_kernel,
        out_shape=(
            jax.ShapeDtypeStruct((H, tok_rows, cols + 128), F32),
            jax.ShapeDtypeStruct((H, tok_rows, cols), F32),
        ),
        in_specs=[SMEM] * 3 + [VMEM] * 12,
        out_specs=(VMEM, VMEM),
        scratch_shapes=[pltpu.VMEM((8,) + own.shape, jnp.int16)],
        compiler_params=params(24),
        cost_estimate=pl.CostEstimate(flops=4_000_000_000, bytes_accessed=8_000_000, transcendentals=1_200_000),
        name="token_attention",
    )(
        core_index[None], head_index[None], z_index[None], packed, *every, bias_mine, bias_other, bias_t
    )
    merged = pl.pallas_call(
        merge_kernel,
        out_shape=jax.ShapeDtypeStruct((H, 2 * tok_rows, 256), jnp.int16),
        in_specs=[VMEM] * 2,
        out_specs=VMEM,
        compiler_params=params(6),
        cost_estimate=pl.CostEstimate(flops=2_000_000, bytes_accessed=2_000_000, transcendentals=0),
        name="gradient_merge",
    )(grad_mine, lax.ppermute(grad_other, "core", swap))
    merged = lax.all_to_all(merged, PLANE, 0, 0, tiled=True)
    gradient, update = pl.pallas_call(
        grad_kernel,
        grid=(steps,),
        out_shape=(
            jax.ShapeDtypeStruct(pair_rep.shape, BF),
            jax.ShapeDtypeStruct(cotangent.shape, BF),
        ),
        in_specs=[
            pl.BlockSpec(merged.shape, lambda i: (0, 0, 0)),
            VMEM,
            VMEM,
            pl.BlockSpec(bias_t.shape, lambda i: (0, 0)),
        ],
        out_specs=(
            pl.BlockSpec((step, cols, 128), lambda i: (i, 0, 0)),
            pl.BlockSpec(cotangent.shape, lambda i: (0, 0, 0)),
        ),
        scratch_shapes=[pltpu.VMEM((steps, H, step, cols), F32)],
        compiler_params=params(24),
        cost_estimate=pl.CostEstimate(flops=400_000_000, bytes_accessed=6_000_000, transcendentals=0),
        name="pair_gradient",
    )(merged, normals, scales, bias_t)
    return (update, gradient)


def solution(mesh):
    fine = Mesh(mesh.devices.reshape(8, 8, 2, 2), ("z", "g", "ylo", "core"))
    placed = (
        P(TILE, COPY, None),
        P(TILE, None),
        P(TILE, None),
        P(COPY, None, TILE),
        P(COPY),
        P(TILE),
        P(TILE),
        P(),
        P(),
        P(),
        P(),
        P(),
        P(),
        P(),
        P(),
        P(),
        P(COPY, TILE, None),
    )
    return jax.shard_map(
        on_device,
        mesh=fine,
        in_specs=placed,
        out_specs=(P(COPY, TILE, None), P(TILE, COPY, None)),
        check_vma=False,
    )
```

```python
import math

import jax
import jax.numpy as jnp
from jax import lax
from jax.experimental import pallas as pl
from jax.experimental.pallas import tpu as pltpu
from jax.sharding import Mesh, PartitionSpec as P

A_HEAD = 32
A_HEADS = 4
Q_BLOCK = 32
K_WIN = 128
LEVELS = 200
HEAD = 48
H = 16

epsilon = 1e-05
sigma_data = 16.0
sigma_top = 160.0
sigma_low = 0.0004
rho_power = 7.0
excluded = -1e30
TILE = ("z", "g")
COPY = ("ylo", "core")
PLANE = ("g", "ylo")
BF = jnp.bfloat16
F32 = jnp.float32
NT = (((1,), (1,)), ((), ()))
NN = (((1,), (0,)), ((), ()))
TN = (((0,), (0,)), ((), ()))


def norm_parts(value):
    average = jnp.mean(value, axis=-1, keepdims=True)
    centred = value - average
    spread = jnp.mean(centred * centred, axis=-1, keepdims=True)
    scale = lax.rsqrt(spread + epsilon)
    return (centred * scale, scale)


def noise_parts(level):
    fraction = jnp.full((1, 128), level, jnp.int32).astype(F32) / LEVELS
    highest = sigma_top ** (1.0 / rho_power)
    lowest = sigma_low ** (1.0 / rho_power)
    root = highest + fraction * (lowest - highest)
    square = root * root
    sigma = sigma_data * (square * square * square * root)
    input_scale = lax.rsqrt(sigma * sigma + sigma_data * sigma_data)
    noise_code = 0.25 * jnp.log(sigma / sigma_data)
    return (input_scale, noise_code)


def dot(a, b, dims=NN):
    return lax.dot_general(a, b, dims, preferred_element_type=F32)


def two_parts(value):
    high = value.astype(BF)
    low = (value - high.astype(F32)).astype(BF)
    return high, low


def three_parts(value):
    high = value.astype(BF)
    rest = value - high.astype(F32)
    middle = rest.astype(BF)
    low = (rest - middle.astype(F32)).astype(BF)
    return high, middle, low


def grid_scale(top):
    top = jnp.maximum(top, 1e-30)
    power = jnp.ceil(jnp.log2(top))
    steps = jnp.ceil(top * jnp.exp2(13.0 - power)) + 1.0
    return steps, power


def scale_value(steps, power):
    return steps * jnp.exp2(power - 13.0) * (1.0 / 32767.0)


def whole(value):
    return jnp.round(value).astype(jnp.int32)


def start_kernel(levels, feat, coords, coord_weight, atoms_out, normed_out, first_out, last_out):
    rows = feat.shape[0]
    rim = K_WIN // 2
    for n in range(coords.shape[0]):
        input_scale, _ = noise_parts(levels[n])
        scaled = coords[n] * input_scale[:, :1]
        atoms = feat[...].astype(F32) + lax.dot_general(
            scaled, coord_weight[...], TN, precision=lax.Precision.HIGHEST, preferred_element_type=F32
        )
        normal, _ = norm_parts(atoms)
        normal = normal.astype(BF)
        atoms_out[n] = atoms
        normed_out[n] = normal
        first_out[n] = normal[:rim]
        last_out[n] = normal[rows - rim :]


def atom_kernel(
    place, offsets, levels, low, high, normed, atoms, atom_weight, agg_weight, atom_token,
    single, single_weight, noise_weight, token_weight, cotangent, out, weight_held, arrival
):
    tile = place[0]
    fetch = pltpu.make_async_copy(token_weight, weight_held, arrival)
    fetch.start()
    copies, rows, width = normed.shape
    blocks = rows // Q_BLOCK
    span = K_WIN + Q_BLOCK
    rim = K_WIN // 2
    total = 64 * rows
    tok_rows = single.shape[0]
    head_of = lax.broadcasted_iota(jnp.int32, (Q_BLOCK, width), 1) // A_HEAD
    twice_head = lax.broadcasted_iota(jnp.int32, (Q_BLOCK, 2 * width), 1) % width // A_HEAD
    reach = lax.broadcasted_iota(jnp.int32, (1, span), 1)
    local_token = atom_token[...].reshape(1, rows) - tile * tok_rows
    member = (lax.broadcasted_iota(jnp.int32, (tok_rows, rows), 0) == local_token).astype(F32)
    counts = jnp.sum(member, axis=1, keepdims=True)
    member = member.astype(BF)
    single_term = dot(single[...], single_weight[...])
    noise_row = noise_weight[...].reshape(1, noise_weight.shape[0])
    scores = []
    vals = []
    for n in range(copies):
        ext = jnp.concatenate([low[n], normed[n], high[n]], axis=0)
        proj = dot(ext, atom_weight[...])
        queries = proj[rim : rim + rows, :width] * (1.0 / math.sqrt(A_HEAD))
        q_high, q_low = two_parts(queries)
        key_high, key_low = two_parts(proj[:, width : 2 * width])
        keys = jnp.concatenate([key_high, key_low], axis=1)
        vals.append(jnp.concatenate(two_parts(proj[:, 2 * width :]), axis=1))
        twice = jnp.concatenate([q_high, q_high], axis=1)
        once = jnp.concatenate([q_low, jnp.zeros_like(q_low)], axis=1)
        blank = jnp.zeros((Q_BLOCK, 2 * width), BF)
        for b in range(blocks):
            first = b * Q_BLOCK
            stacked = jnp.concatenate(
                [
                    jnp.where(twice_head == h, part[first : first + Q_BLOCK], blank)
                    for part in (twice, once)
                    for h in range(A_HEADS)
                ],
                axis=0,
            )
            both = dot(stacked, keys[first : first + span], NT)
            offset = offsets[b]
            position = tile * rows + first - rim + reach
            inside = (
                (reach >= offset)
                & (reach < offset + K_WIN)
                & (position >= 0)
                & (position < total)
            )
            half = A_HEADS * Q_BLOCK
            scores.append(jnp.where(inside, both[:half] + both[half:], excluded))
    scores = jnp.concatenate(scores, axis=0)
    weights = jnp.exp(scores - jnp.max(scores, axis=-1, keepdims=True))
    weights = weights * (1.0 / jnp.sum(weights, axis=-1, keepdims=True))
    weights = weights.astype(BF)
    token_in = []
    for n in range(copies):
        parts = []
        for b in range(blocks):
            first = b * Q_BLOCK
            at = (n * blocks + b) * A_HEADS * Q_BLOCK
            mixed = dot(weights[at : at + A_HEADS * Q_BLOCK], vals[n][first : first + span])
            mixed = mixed[:, :width] + mixed[:, width:]
            gathered = jnp.where(head_of == 0, mixed[:Q_BLOCK], 0.0)
            for h in range(1, A_HEADS):
                gathered += jnp.where(
                    head_of == h, mixed[h * Q_BLOCK : (h + 1) * Q_BLOCK], 0.0
                )
            parts.append(gathered)
        atom_out = (atoms[n] + jnp.concatenate(parts, axis=0)).astype(BF)
        hidden = jnp.maximum(dot(atom_out, agg_weight[...]), 0.0)
        sums = 0.0
        for part in two_parts(hidden):
            sums = sums + dot(member, part)
        token_normal, _ = norm_parts(sums / counts)
        _, noise_code = noise_parts(levels[n])
        token_in.append(token_normal + single_term + noise_code[:, :1] * noise_row)
    token_in = jnp.concatenate(token_in, axis=0)
    count = token_in.shape[0]
    stacked = jnp.concatenate(two_parts(token_in), axis=0)
    fetch.wait()
    proj = dot(stacked, weight_held[...])
    proj = proj[:count] + proj[count:]
    wide = H * HEAD
    cot = jnp.concatenate([cotangent[n].astype(F32) for n in range(copies)], axis=0)
    head_at = lax.broadcasted_iota(jnp.int32, (H, wide), 1) // HEAD
    mine = head_at == lax.broadcasted_iota(jnp.int32, (H, wide), 0)
    lane = lax.broadcasted_iota(jnp.int32, (H, 128 - 2 * HEAD), 1)
    codes = [jnp.zeros(lane.shape, F32)] * 2
    coded = []
    sources = [
        proj[:, :wide] * (1.0 / math.sqrt(HEAD)), cot, proj[:, wide : 2 * wide], proj[:, 2 * wide :]
    ]
    for index, source in enumerate(sources):
        top = jnp.max(jnp.abs(source), axis=0, keepdims=True)
        steps, power = grid_scale(jnp.max(jnp.where(mine, top, 0.0), axis=1, keepdims=True))
        inverse = 1.0 / scale_value(steps, power)
        inverse = jnp.max(jnp.where(mine, inverse, 0.0), axis=0, keepdims=True)
        coded.append(jnp.round(source * inverse))
        half, at = index // 2, 2 * (index % 2)
        codes[half] = jnp.where(
            lane == at, steps, jnp.where(lane == at + 1, power, codes[half])
        )
    for h in range(H):
        at = h * HEAD
        for half in range(2):
            row = [coded[2 * half + k][:, at : at + HEAD] for k in range(2)]
            row.append(jnp.broadcast_to(codes[half][h : h + 1], (count, 128 - 2 * HEAD)))
            out[h, :, half * 128 : (half + 1) * 128] = (
                jnp.concatenate(row, axis=1).astype(jnp.int32).astype(jnp.int16)
            )


def head_unit(weight):
    weight = weight.astype(F32)
    reach = jnp.sqrt(jnp.sum(weight * weight, axis=-1, keepdims=True))
    return reach * (math.sqrt(128.0) * 1.01 / 32767.0) + 1e-30


def lane_matrices(lanes):
    row_at = lax.broadcasted_iota(jnp.int32, (2 * lanes, 2 * lanes), 0)
    col_at = lax.broadcasted_iota(jnp.int32, (2 * lanes, 2 * lanes), 1)
    same = (row_at // lanes) == (col_at // lanes)
    ones = jnp.where(same, 1.0 / lanes, 0.0).astype(BF)
    centre = jnp.where(
        same, jnp.where(row_at == col_at, 1.0 - 1.0 / lanes, -1.0 / lanes), 0.0
    ).astype(BF)
    return jnp.concatenate([ones, ones], axis=0), centre


def lane_mean(value, ones):
    return dot(jnp.concatenate(two_parts(value), axis=1), ones)


def pair_block(pair, trans_in, trans_out, bias_weight_t, cond_out, store):
    inner = trans_out.shape[0]
    cols = pair.shape[1]
    lanes = 128
    ones, centre = lane_matrices(lanes)
    unit = head_unit(bias_weight_t[...])

    def half_mean(value):
        return jnp.concatenate(
            [
                jnp.broadcast_to(
                    jnp.mean(value[:, at : at + lanes], axis=-1, keepdims=True),
                    (value.shape[0], lanes),
                )
                for at in (0, lanes)
            ],
            axis=1,
        )

    def normalise(value, by_product):
        half = value.shape[0] // 2
        centred = dot(jnp.concatenate([value[:half], value[half:]], axis=1), centre)
        square = centred * centred
        spread = lane_mean(square, ones) if by_product else half_mean(square)
        normal = (centred * lax.rsqrt(spread + epsilon)).astype(BF)
        return jnp.concatenate([normal[:, :lanes], normal[:, lanes:]], axis=0)

    group = 2
    chunk = 128
    weights = [
        jnp.concatenate(
            [
                trans_in[:, f : f + chunk] * 0.5,
                trans_in[:, inner + f : inner + f + chunk],
            ],
            axis=1,
        )
        for f in range(0, inner, chunk)
    ]
    count = pair.shape[0] // group
    normed, hidden, cond = {}, {}, {}

    def value_of(k):
        return pair[k * group : (k + 1) * group].reshape(group * cols, lanes)

    def gate(k, f):
        if 0 <= k < count:
            both = dot(normed[k], weights[f])
            half = both[:, :chunk]
            hidden[k, f] = ((half + half * jnp.tanh(half)) * both[:, chunk:]).astype(BF)

    def down(k):
        if 0 <= k < count:
            joined = jnp.concatenate([hidden[k, f] for f in range(len(weights))], axis=1)
            cond[k] = (value_of(k).astype(F32) + dot(joined, trans_out[...])).astype(BF)
            cond_out[k * group : (k + 1) * group] = cond[k].reshape(group, cols, lanes)

    def project(k):
        if 0 <= k < count:
            bias = dot(bias_weight_t[...], normalise(cond[k], True), NT) * (1.0 / unit)
            for i in range(group):
                store(k * group + i, bias[:, i * cols : (i + 1) * cols])

    for t in range(count + 3):
        gate(t - 1, 0)
        project(t - 3)
        gate(t - 1, 1)
        down(t - 2)
        gate(t - 1, 2)
        if t < count:
            normed[t] = normalise(value_of(t), False)
        gate(t - 1, 3)


def pair_first_kernel(pair, trans_in, trans_out, bias_weight_t, anchor, cond_out, bias_out):
    def store(i, value):
        bias_out[0, :, i, :] = value

    pair_block(pair, trans_in, trans_out, bias_weight_t, cond_out, store)


def pair_next_kernel(pair, trans_in, trans_out, bias_weight_t, anchor, cond, cond_out, bias_out):
    pair_first_kernel(pair, trans_in, trans_out, bias_weight_t, anchor, cond_out, bias_out)


def pair_last_kernel(
    pair, trans_in, trans_out, bias_weight_t, anchor, cond, first, second, cond_out, bias_out, held
):
    step = pl.program_id(0)

    def store(i, value):
        held[step, :, i, :] = value

    pair_block(pair, trans_in, trans_out, bias_weight_t, cond_out, store)

    @pl.when(step == pl.num_programs(0) - 1)
    def _():
        for h in range(bias_out.shape[0]):
            parts = [ref[s, h] for ref in (first, second, held) for s in range(held.shape[0])]
            bias_out[h] = whole(jnp.concatenate(parts, axis=0)).astype(jnp.int16)


def pair_call(kernel, index, inputs, extra, anchor, cond, bias_shape, bias_block, scratch=()):
    pair_rep, trans_in, trans_out, bias_t = inputs
    cols = pair_rep.shape[1]
    rows, steps = 4, 2
    block = pl.BlockSpec((rows, cols, 128), lambda i: (steps * index + i, 0, 0))
    operands = [pair_rep, trans_in, trans_out, bias_t, anchor]
    if cond is not None:
        operands.append(cond)
    count = len(operands)
    specs = [block] + [pl.BlockSpec(x.shape, lambda i: (0, 0)) for x in operands[1:4]]
    specs += [ANY] * (count - 4)
    specs += [pl.BlockSpec(x.shape, lambda i: (0, 0, 0, 0)) for x in extra]
    return pl.pallas_call(
        kernel,
        grid=(steps,),
        out_shape=(jax.ShapeDtypeStruct(pair_rep.shape, BF), bias_shape),
        in_specs=specs,
        out_specs=(block, bias_block),
        scratch_shapes=list(scratch),
        input_output_aliases={} if cond is None else {5: 0},
        compiler_params=params(56),
        cost_estimate=pl.CostEstimate(
            flops=6_000_000_000, bytes_accessed=8_000_000, transcendentals=0
        ),
        name="pair_part",
    )(*operands, *extra)


def attend_kernel(
    core_at, head_at, z_at, queries, kv0, kv1, kv2, kv3, kv4, kv5, kv6, kv7, bias_mine, bias_other, bias_weight_t,
    update_mine, grad_other, kv
):
    core = core_at[0]
    unit = head_unit(bias_weight_t[...])
    this = lax.broadcasted_iota(jnp.int32, unit.shape, 0) == head_at[0]
    unit = jnp.sum(jnp.where(this, unit, 0.0), axis=0, keepdims=True)
    for back, block in enumerate((kv0, kv1, kv2, kv3, kv4, kv5, kv6, kv7)):
        kv[lax.rem(z_at[0] + 8 - back, 8)] = block[...]
    blocks = [core, 2 + core, 1 - core, 3 - core]
    cols = 384
    tok = 24
    rows = 8 * tok
    lane = lax.broadcasted_iota(jnp.int32, (1, 128), 1)
    is_key = lane < HEAD
    is_value = (lane >= HEAD) & (lane < 2 * HEAD)

    def decode(block):
        block = block.astype(jnp.int32).astype(F32)
        codes = block[0:1]
        at = 2 * HEAD
        first = scale_value(codes[:, at : at + 1], codes[:, at + 1 : at + 2])
        second = scale_value(codes[:, at + 2 : at + 3], codes[:, at + 3 : at + 4])
        return block * jnp.where(is_key, first, jnp.where(is_value, second, 0.0))

    bias = jnp.concatenate(
        [
            jnp.concatenate(
                [
                    (bias_mine if c < 2 else bias_other)[2 * g + c % 2].astype(jnp.int32).astype(F32)
                    for c in range(4)
                ],
                axis=1,
            )
            for g in range(8)
        ],
        axis=0,
    ) * unit
    def products_of(y, p, query_blocks, token_blocks):
        query = jnp.concatenate([b[p * tok : (p + 1) * tok] for b in query_blocks], axis=0)
        q_high, q_low = two_parts(jnp.where(is_key, query, 0.0))
        c_high, c_low = two_parts(jnp.where(is_value, query, 0.0))
        high, low = two_parts(
            jnp.concatenate([b[p * tok : (p + 1) * tok] for b in token_blocks], axis=0)
        )
        both = jnp.concatenate([high, low], axis=1)
        none = jnp.zeros_like(q_low)
        stacked = jnp.concatenate(
            [
                jnp.concatenate([q_high, q_high], axis=1),
                jnp.concatenate([q_low, none], axis=1),
                jnp.concatenate([c_high, c_high], axis=1),
                jnp.concatenate([c_low, none], axis=1),
            ],
            axis=0,
        )
        return both, dot(stacked, both, NT)

    def products_at(index):
        y, p = index // 2, index % 2
        if p == 0:
            blocks_of[y] = (
                [decode(queries[2 * g + y, :, :128]) for g in range(8)],
                [decode(kv[2 * c + z, 2 * g + y]) for c in blocks for z in range(2) for g in range(8)],
            )
        return products_of(y, p, *blocks_of[y])

    blocks_of = {}
    grad = None
    coming = products_at(0)
    for index in range(4):
        y, p = index // 2, index % 2
        both, products = coming
        if index < 3:
            coming = products_at(index + 1)
        scores = products[:rows] + products[rows : 2 * rows] + bias
        prob_grad = products[2 * rows : 3 * rows] + products[3 * rows :]
        top = jnp.max(scores, axis=-1, keepdims=True)
        weights = jnp.exp(scores - top)
        weights = weights * (1.0 / jnp.sum(weights, axis=-1, keepdims=True))
        mixed = dot(weights.astype(BF), both)
        mixed = mixed[:, :128] + mixed[:, 128:]
        for g in range(8):
            update_mine[2 * g + y, :, cols + p * HEAD : cols + (p + 1) * HEAD] = mixed[
                g * tok : (g + 1) * tok, HEAD : 2 * HEAD
            ]
        term = weights * prob_grad
        term = term - weights * jnp.sum(term, axis=-1, keepdims=True)
        grad = term if grad is None else grad + term
    for g in range(8):
        for c in range(4):
            (update_mine if c < 2 else grad_other)[2 * g + c % 2, :, :cols] = grad[
                g * tok : (g + 1) * tok, c * cols : (c + 1) * cols
            ]


def merge_kernel(mine, other, out):
    cols = other.shape[2]
    used = 2 * HEAD
    lane = lax.broadcasted_iota(jnp.int32, (1, 128), 1)
    for h in range(mine.shape[0]):
        grad = mine[h, :, :cols] + other[h]
        update = jnp.where(lane < used, mine[h, :, cols:], 0.0)
        codes = update
        scaled = []
        for at, part in ((0, grad), (2, update)):
            steps, power = grid_scale(jnp.max(jnp.abs(part), axis=-1, keepdims=True))
            scaled.append(part * (1.0 / scale_value(steps, power)))
            codes = jnp.where(lane == used + at, steps, codes)
            codes = jnp.where(lane == used + at + 1, power, codes)
        last = jnp.where(lane < used, scaled[1], codes)
        out[h] = jnp.concatenate(
            [
                whole(scaled[0][:, :256]),
                whole(jnp.concatenate([scaled[0][:, 256:], last], axis=1)),
            ],
            axis=0,
        ).astype(jnp.int16)


def normal_kernel(cond, anchor, normal_out, scale_out):
    rows, cols, lanes = cond.shape
    ones, centre = lane_matrices(lanes)
    group = 4
    for part in range(rows // group):
        value = cond[part * group : (part + 1) * group].reshape(group * cols, lanes)
        half = group * cols // 2
        centred = dot(jnp.concatenate([value[:half], value[half:]], axis=1), centre)
        scale = lax.rsqrt(lane_mean(centred * centred, ones) + epsilon)
        normal_out[part] = centred * scale
        scale_out[part] = scale


def grad_kernel(packed, normals, scales, bias_weight, out, update_out, held):
    step = pl.program_id(0)
    lanes = 128
    heads, _, rows, cols = held.shape[1], 0, held.shape[2], held.shape[3]
    tok = packed.shape[1] // 2

    @pl.when(step == 0)
    def _():
        pieces = [[], []]
        for h in range(heads):
            block = packed[h].astype(jnp.int32).astype(F32)
            low, high = block[:tok], block[tok:]
            at = lanes + 2 * HEAD
            grad_scale = scale_value(high[:, at : at + 1], high[:, at + 1 : at + 2])
            update_scale = scale_value(high[:, at + 2 : at + 3], high[:, at + 3 : at + 4])
            grad = jnp.concatenate([low, high[:, :lanes]], axis=1) * grad_scale
            for s in range(held.shape[0]):
                held[s, h] = grad[s * rows : (s + 1) * rows]
            for p in range(2):
                pieces[p].append(
                    high[:, lanes + p * HEAD : lanes + (p + 1) * HEAD] * update_scale
                )
        for p in range(2):
            update_out[p] = jnp.concatenate(pieces[p], axis=1).astype(BF)

    ones, _ = lane_matrices(lanes)
    weight = bias_weight[...].astype(F32)
    w_high, w_low = two_parts(weight - jnp.mean(weight, axis=-1, keepdims=True))
    parts = jnp.concatenate([w_high, w_high, w_high, w_low, w_low], axis=0)
    group = 4
    count = group * cols
    half = count // 2

    def paired(value):
        return jnp.concatenate([value[:half], value[half:]], axis=1)

    for part in range(rows // group):
        grad = jnp.concatenate(
            [held[step, :, part * group + i, :] for i in range(group)], axis=1
        )
        high, middle, low = three_parts(grad)
        stacked = jnp.concatenate([high, middle, low, high, middle], axis=0)
        grad_normal = paired(dot(stacked, parts, TN))
        normal = normals[step * (rows // group) + part]
        scale = scales[step * (rows // group) + part]
        result = ((grad_normal - normal * lane_mean(grad_normal * normal, ones)) * scale).astype(BF)
        result = jnp.concatenate([result[:, :lanes], result[:, lanes:]], axis=0)
        out[part * group : (part + 1) * group] = result.reshape(group, cols, lanes)


def params(mebibytes):
    return pltpu.CompilerParams(vmem_limit_bytes=mebibytes * 1024 * 1024)


VMEM = pl.BlockSpec(memory_space=pltpu.VMEM)
SMEM = pl.BlockSpec(memory_space=pltpu.SMEM)
ANY = pl.BlockSpec(memory_space=pl.ANY)


def on_device(
    pair_rep,
    single,
    atom_feat,
    coords,
    levels,
    window_offset,
    atom_token,
    trans_in,
    trans_out,
    bias_weight,
    single_weight,
    coord_weight,
    atom_weight,
    agg_weight,
    token_weight,
    noise_weight,
    cotangent,
):
    tile_index = lax.axis_index(TILE).astype(jnp.int32)
    core_index = lax.axis_index("core").astype(jnp.int32)
    copies, tok_rows, width = cotangent.shape
    atom_rows, atom_width = atom_feat.shape
    cols = pair_rep.shape[1]
    rim = K_WIN // 2
    atoms, normed, first, last = pl.pallas_call(
        start_kernel,
        out_shape=(
            jax.ShapeDtypeStruct((copies, atom_rows, atom_width), F32),
            jax.ShapeDtypeStruct((copies, atom_rows, atom_width), BF),
            jax.ShapeDtypeStruct((copies, rim, atom_width), BF),
            jax.ShapeDtypeStruct((copies, rim, atom_width), BF),
        ),
        in_specs=[SMEM] + [VMEM] * 3,
        out_specs=(VMEM,) * 4,
        compiler_params=params(56),
        cost_estimate=pl.CostEstimate(flops=1_000_000, bytes_accessed=500_000, transcendentals=0),
        name="atom_start",
    )(levels, atom_feat, coords, coord_weight)
    forward = [(i, i + 1) for i in range(63)]
    backward = [(i + 1, i) for i in range(63)]
    low = lax.ppermute(last, TILE, forward)
    high = lax.ppermute(first, TILE, backward)
    bias_t = bias_weight.T
    inputs = (pair_rep, trans_in, trans_out, bias_t)
    step = 8
    part_bias = jax.ShapeDtypeStruct((2, H, step // 2, cols), F32)
    part_block = pl.BlockSpec((1, H, step // 2, cols), lambda i: (i, 0, 0, 0))
    cond, bias_first = pair_call(pair_first_kernel, 0, inputs, [], last, None, part_bias, part_block)
    low, high, bias_first = lax.optimization_barrier((low, high, bias_first))
    packed = pl.pallas_call(
        atom_kernel,
        out_shape=jax.ShapeDtypeStruct((H, copies * tok_rows, 256), jnp.int16),
        in_specs=[SMEM] * 3 + [VMEM] * 10 + [ANY, VMEM],
        out_specs=VMEM,
        scratch_shapes=[pltpu.VMEM(token_weight.shape, BF), pltpu.SemaphoreType.DMA],
        compiler_params=params(56),
        cost_estimate=pl.CostEstimate(flops=3_000_000_000, bytes_accessed=6_000_000, transcendentals=0),
        name="atom_stage",
    )(
        tile_index[None], window_offset, levels, low, high, normed, atoms, atom_weight, agg_weight,
        atom_token, single, single_weight, noise_weight, token_weight, cotangent,
    )
    cond, bias_second = pair_call(
        pair_next_kernel, 1, inputs, [], packed, cond, part_bias, part_block
    )
    packed = lax.all_to_all(packed, PLANE, 0, 0, tiled=True)
    packed, bias_second = lax.optimization_barrier((packed, bias_second))
    own = packed[:, :, 128:]
    ahead = [(i, (i + 1) % 8) for i in range(8)]
    behind = [(i, (i + 7) % 8) for i in range(8)]
    rising = [own, lax.ppermute(own, "z", ahead)]
    falling = [own, lax.ppermute(own, "z", behind)]
    cond, bias = pair_call(
        pair_last_kernel, 2, inputs, [bias_first, bias_second], own, cond,
        jax.ShapeDtypeStruct((H, tok_rows, cols), jnp.int16),
        pl.BlockSpec((H, tok_rows, cols), lambda i: (0, 0, 0)),
        [pltpu.VMEM(part_bias.shape, F32)],
    )
    rising[1], falling[1], bias = lax.optimization_barrier((rising[1], falling[1], bias))
    rising.append(lax.ppermute(rising[1], "z", ahead))
    falling.append(lax.ppermute(falling[1], "z", behind))
    rising.append(lax.ppermute(rising[2], "z", ahead))
    falling.append(lax.ppermute(falling[2], "z", behind))
    rising.append(lax.ppermute(rising[3], "z", ahead))
    steps = tok_rows // step
    bias_mine = lax.all_to_all(bias, PLANE, 0, 0, tiled=True)
    swap = [(0, 1), (1, 0)]
    bias_other = lax.ppermute(bias_mine, "core", swap)

    pieces = (tok_rows // 4, 2 * cols, 256)
    normals, scales = pl.pallas_call(
        normal_kernel,
        out_shape=(jax.ShapeDtypeStruct(pieces, F32),) * 2,
        in_specs=[VMEM, ANY],
        out_specs=(VMEM, VMEM),
        compiler_params=params(20),
        cost_estimate=pl.CostEstimate(flops=1_500_000_000, bytes_accessed=12_000_000, transcendentals=0),
        name="pair_normal",
    )(cond, rising[3])
    rising[4], normals, scales = lax.optimization_barrier((rising[4], normals, scales))
    every = rising + [falling[3], falling[2], falling[1]]
    head_index = lax.axis_index(PLANE).astype(jnp.int32)
    z_index = lax.axis_index("z").astype(jnp.int32)
    grad_mine, grad_other = pl.pallas_call(
        attend_kernel,
        out_shape=(
            jax.ShapeDtypeStruct((H, tok_rows, cols + 128), F32),
            jax.ShapeDtypeStruct((H, tok_rows, cols), F32),
        ),
        in_specs=[SMEM] * 3 + [VMEM] * 12,
        out_specs=(VMEM, VMEM),
        scratch_shapes=[pltpu.VMEM((8,) + own.shape, jnp.int16)],
        compiler_params=params(24),
        cost_estimate=pl.CostEstimate(flops=4_000_000_000, bytes_accessed=8_000_000, transcendentals=1_200_000),
        name="token_attention",
    )(
        core_index[None], head_index[None], z_index[None], packed, *every, bias_mine, bias_other, bias_t
    )
    merged = pl.pallas_call(
        merge_kernel,
        out_shape=jax.ShapeDtypeStruct((H, 2 * tok_rows, 256), jnp.int16),
        in_specs=[VMEM] * 2,
        out_specs=VMEM,
        compiler_params=params(6),
        cost_estimate=pl.CostEstimate(flops=2_000_000, bytes_accessed=2_000_000, transcendentals=0),
        name="gradient_merge",
    )(grad_mine, lax.ppermute(grad_other, "core", swap))
    merged = lax.all_to_all(merged, PLANE, 0, 0, tiled=True)
    gradient, update = pl.pallas_call(
        grad_kernel,
        grid=(steps,),
        out_shape=(
            jax.ShapeDtypeStruct(pair_rep.shape, BF),
            jax.ShapeDtypeStruct(cotangent.shape, BF),
        ),
        in_specs=[
            pl.BlockSpec(merged.shape, lambda i: (0, 0, 0)),
            VMEM,
            VMEM,
            pl.BlockSpec(bias_t.shape, lambda i: (0, 0)),
        ],
        out_specs=(
            pl.BlockSpec((step, cols, 128), lambda i: (i, 0, 0)),
            pl.BlockSpec(cotangent.shape, lambda i: (0, 0, 0)),
        ),
        scratch_shapes=[pltpu.VMEM((steps, H, step, cols), F32)],
        compiler_params=params(24),
        cost_estimate=pl.CostEstimate(flops=400_000_000, bytes_accessed=6_000_000, transcendentals=0),
        name="pair_gradient",
    )(merged, normals, scales, bias_t)
    return (update, gradient)


def solution(mesh):
    fine = Mesh(mesh.devices.reshape(8, 8, 2, 2), ("z", "g", "ylo", "core"))
    placed = (
        P(TILE, COPY, None),
        P(TILE, None),
        P(TILE, None),
        P(COPY, None, TILE),
        P(COPY),
        P(TILE),
        P(TILE),
        P(),
        P(),
        P(),
        P(),
        P(),
        P(),
        P(),
        P(),
        P(),
        P(COPY, TILE, None),
    )
    return jax.shard_map(
        on_device,
        mesh=fine,
        in_specs=placed,
        out_specs=(P(COPY, TILE, None), P(TILE, COPY, None)),
        check_vma=False,
    )
```

```python
import math

import jax
import jax.numpy as jnp
from jax import lax
from jax.experimental import pallas as pl
from jax.experimental.pallas import tpu as pltpu
from jax.sharding import Mesh, PartitionSpec as P

A_HEAD = 32
A_HEADS = 4
Q_BLOCK = 32
K_WIN = 128
LEVELS = 200
HEAD = 48
H = 16

epsilon = 1e-05
sigma_data = 16.0
sigma_top = 160.0
sigma_low = 0.0004
rho_power = 7.0
excluded = -1e30
TILE = ("z", "g")
COPY = ("ylo", "core")
PLANE = ("g", "ylo")
BF = jnp.bfloat16
F32 = jnp.float32
NT = (((1,), (1,)), ((), ()))
NN = (((1,), (0,)), ((), ()))
TN = (((0,), (0,)), ((), ()))


def norm_parts(value):
    average = jnp.mean(value, axis=-1, keepdims=True)
    centred = value - average
    spread = jnp.mean(centred * centred, axis=-1, keepdims=True)
    scale = lax.rsqrt(spread + epsilon)
    return (centred * scale, scale)


def noise_parts(level):
    fraction = jnp.full((1, 128), level, jnp.int32).astype(F32) / LEVELS
    highest = sigma_top ** (1.0 / rho_power)
    lowest = sigma_low ** (1.0 / rho_power)
    root = highest + fraction * (lowest - highest)
    square = root * root
    sigma = sigma_data * (square * square * square * root)
    input_scale = lax.rsqrt(sigma * sigma + sigma_data * sigma_data)
    noise_code = 0.25 * jnp.log(sigma / sigma_data)
    return (input_scale, noise_code)


def dot(a, b, dims=NN):
    return lax.dot_general(a, b, dims, preferred_element_type=F32)


def two_parts(value):
    high = value.astype(BF)
    low = (value - high.astype(F32)).astype(BF)
    return high, low


def three_parts(value):
    high = value.astype(BF)
    rest = value - high.astype(F32)
    middle = rest.astype(BF)
    low = (rest - middle.astype(F32)).astype(BF)
    return high, middle, low


def grid_scale(top):
    top = jnp.maximum(top, 1e-30)
    power = jnp.ceil(jnp.log2(top))
    steps = jnp.ceil(top * jnp.exp2(13.0 - power)) + 1.0
    return steps, power


def scale_value(steps, power):
    return steps * jnp.exp2(power - 13.0) * (1.0 / 32767.0)


def whole(value):
    return jnp.round(value).astype(jnp.int32)


def start_kernel(levels, feat, coords, coord_weight, atoms_out, normed_out, first_out, last_out):
    rows = feat.shape[0]
    rim = K_WIN // 2
    for n in range(coords.shape[1]):
        input_scale, _ = noise_parts(levels[n])
        scaled = jnp.concatenate(
            [coords[x, n : n + 1] for x in range(coords.shape[0])], axis=0
        ) * input_scale[:, :1]
        atoms = feat[...].astype(F32) + lax.dot_general(
            scaled, coord_weight[...], TN, precision=lax.Precision.HIGHEST, preferred_element_type=F32
        )
        normal, _ = norm_parts(atoms)
        normal = normal.astype(BF)
        atoms_out[n] = atoms
        normed_out[n] = normal
        first_out[n] = normal[:rim]
        last_out[n] = normal[rows - rim :]


def atom_kernel(
    place, offsets, levels, low, high, normed, atoms, atom_weight, agg_weight, atom_token,
    single, single_weight, noise_weight, token_weight, cotangent, out, weight_held, arrival
):
    tile = place[0]
    fetch = pltpu.make_async_copy(token_weight, weight_held, arrival)
    fetch.start()
    copies, rows, width = normed.shape
    blocks = rows // Q_BLOCK
    span = K_WIN + Q_BLOCK
    rim = K_WIN // 2
    total = 64 * rows
    tok_rows = single.shape[0]
    head_of = lax.broadcasted_iota(jnp.int32, (Q_BLOCK, width), 1) // A_HEAD
    twice_head = lax.broadcasted_iota(jnp.int32, (Q_BLOCK, 2 * width), 1) % width // A_HEAD
    reach = lax.broadcasted_iota(jnp.int32, (1, span), 1)
    local_token = atom_token[...].reshape(1, rows) - tile * tok_rows
    member = (lax.broadcasted_iota(jnp.int32, (tok_rows, rows), 0) == local_token).astype(F32)
    counts = jnp.sum(member, axis=1, keepdims=True)
    member = member.astype(BF)
    single_term = dot(single[...], single_weight[...])
    noise_row = noise_weight[...].reshape(1, noise_weight.shape[0])
    scores = []
    vals = []
    for n in range(copies):
        ext = jnp.concatenate([low[n], normed[n], high[n]], axis=0)
        proj = dot(ext, atom_weight[...])
        queries = proj[rim : rim + rows, :width] * (1.0 / math.sqrt(A_HEAD))
        q_high, q_low = two_parts(queries)
        key_high, key_low = two_parts(proj[:, width : 2 * width])
        keys = jnp.concatenate([key_high, key_low], axis=1)
        vals.append(jnp.concatenate(two_parts(proj[:, 2 * width :]), axis=1))
        twice = jnp.concatenate([q_high, q_high], axis=1)
        once = jnp.concatenate([q_low, jnp.zeros_like(q_low)], axis=1)
        blank = jnp.zeros((Q_BLOCK, 2 * width), BF)
        for b in range(blocks):
            first = b * Q_BLOCK
            stacked = jnp.concatenate(
                [
                    jnp.where(twice_head == h, part[first : first + Q_BLOCK], blank)
                    for part in (twice, once)
                    for h in range(A_HEADS)
                ],
                axis=0,
            )
            both = dot(stacked, keys[first : first + span], NT)
            offset = offsets[b]
            position = tile * rows + first - rim + reach
            inside = (
                (reach >= offset)
                & (reach < offset + K_WIN)
                & (position >= 0)
                & (position < total)
            )
            half = A_HEADS * Q_BLOCK
            scores.append(jnp.where(inside, both[:half] + both[half:], excluded))
    scores = jnp.concatenate(scores, axis=0)
    weights = jnp.exp(scores - jnp.max(scores, axis=-1, keepdims=True))
    weights = weights * (1.0 / jnp.sum(weights, axis=-1, keepdims=True))
    weights = weights.astype(BF)
    token_in = []
    for n in range(copies):
        parts = []
        for b in range(blocks):
            first = b * Q_BLOCK
            at = (n * blocks + b) * A_HEADS * Q_BLOCK
            mixed = dot(weights[at : at + A_HEADS * Q_BLOCK], vals[n][first : first + span])
            mixed = mixed[:, :width] + mixed[:, width:]
            gathered = jnp.where(head_of == 0, mixed[:Q_BLOCK], 0.0)
            for h in range(1, A_HEADS):
                gathered += jnp.where(
                    head_of == h, mixed[h * Q_BLOCK : (h + 1) * Q_BLOCK], 0.0
                )
            parts.append(gathered)
        atom_out = (atoms[n] + jnp.concatenate(parts, axis=0)).astype(BF)
        hidden = jnp.maximum(dot(atom_out, agg_weight[...]), 0.0)
        sums = 0.0
        for part in two_parts(hidden):
            sums = sums + dot(member, part)
        token_normal, _ = norm_parts(sums / counts)
        _, noise_code = noise_parts(levels[n])
        token_in.append(token_normal + single_term + noise_code[:, :1] * noise_row)
    token_in = jnp.concatenate(token_in, axis=0)
    count = token_in.shape[0]
    stacked = jnp.concatenate(two_parts(token_in), axis=0)
    fetch.wait()
    proj = dot(stacked, weight_held[...])
    proj = proj[:count] + proj[count:]
    wide = H * HEAD
    cot = jnp.concatenate([cotangent[n].astype(F32) for n in range(copies)], axis=0)
    head_at = lax.broadcasted_iota(jnp.int32, (H, wide), 1) // HEAD
    mine = head_at == lax.broadcasted_iota(jnp.int32, (H, wide), 0)
    lane = lax.broadcasted_iota(jnp.int32, (H, 128 - 2 * HEAD), 1)
    codes = [jnp.zeros(lane.shape, F32)] * 2
    coded = []
    sources = [
        proj[:, :wide] * (1.0 / math.sqrt(HEAD)), cot, proj[:, wide : 2 * wide], proj[:, 2 * wide :]
    ]
    for index, source in enumerate(sources):
        top = jnp.max(jnp.abs(source), axis=0, keepdims=True)
        steps, power = grid_scale(jnp.max(jnp.where(mine, top, 0.0), axis=1, keepdims=True))
        inverse = 1.0 / scale_value(steps, power)
        inverse = jnp.max(jnp.where(mine, inverse, 0.0), axis=0, keepdims=True)
        coded.append(jnp.round(source * inverse))
        half, at = index // 2, 2 * (index % 2)
        codes[half] = jnp.where(
            lane == at, steps, jnp.where(lane == at + 1, power, codes[half])
        )
    for h in range(H):
        at = h * HEAD
        for half in range(2):
            row = [coded[2 * half + k][:, at : at + HEAD] for k in range(2)]
            row.append(jnp.broadcast_to(codes[half][h : h + 1], (count, 128 - 2 * HEAD)))
            out[h, :, half * 128 : (half + 1) * 128] = (
                jnp.concatenate(row, axis=1).astype(jnp.int32).astype(jnp.int16)
            )


def head_unit(weight):
    weight = weight.astype(F32)
    reach = jnp.sqrt(jnp.sum(weight * weight, axis=-1, keepdims=True))
    return reach * (math.sqrt(128.0) * 1.01 / 32767.0) + 1e-30


def lane_matrices(lanes):
    row_at = lax.broadcasted_iota(jnp.int32, (2 * lanes, 2 * lanes), 0)
    col_at = lax.broadcasted_iota(jnp.int32, (2 * lanes, 2 * lanes), 1)
    same = (row_at // lanes) == (col_at // lanes)
    ones = jnp.where(same, 1.0 / lanes, 0.0).astype(BF)
    centre = jnp.where(
        same, jnp.where(row_at == col_at, 1.0 - 1.0 / lanes, -1.0 / lanes), 0.0
    ).astype(BF)
    return jnp.concatenate([ones, ones], axis=0), centre


def lane_mean(value, ones):
    return dot(jnp.concatenate(two_parts(value), axis=1), ones)


def pair_block(pair, trans_in, trans_out, bias_weight_t, cond_out, store):
    inner = trans_out.shape[0]
    cols = pair.shape[1]
    lanes = 128
    ones, centre = lane_matrices(lanes)
    unit = head_unit(bias_weight_t[...])

    def normalise(value):
        half = value.shape[0] // 2
        centred = dot(jnp.concatenate([value[:half], value[half:]], axis=1), centre)
        normal = (centred * lax.rsqrt(lane_mean(centred * centred, ones) + epsilon)).astype(BF)
        return jnp.concatenate([normal[:, :lanes], normal[:, lanes:]], axis=0)

    group = 2
    chunk = 128
    weights = [
        jnp.concatenate(
            [
                trans_in[:, f : f + chunk] * 0.5,
                trans_in[:, inner + f : inner + f + chunk],
            ],
            axis=1,
        )
        for f in range(0, inner, chunk)
    ]
    count = pair.shape[0] // group
    normed, hidden, cond = {}, {}, {}

    def value_of(k):
        return pair[k * group : (k + 1) * group].reshape(group * cols, lanes)

    def gate(k, f):
        if 0 <= k < count:
            both = dot(normed[k], weights[f])
            half = both[:, :chunk]
            hidden[k, f] = ((half + half * jnp.tanh(half)) * both[:, chunk:]).astype(BF)

    def down(k):
        if 0 <= k < count:
            joined = jnp.concatenate([hidden[k, f] for f in range(len(weights))], axis=1)
            cond[k] = (value_of(k).astype(F32) + dot(joined, trans_out[...])).astype(BF)
            cond_out[k * group : (k + 1) * group] = cond[k].reshape(group, cols, lanes)

    def project(k):
        if 0 <= k < count:
            bias = dot(bias_weight_t[...], normalise(cond[k]), NT) * (1.0 / unit)
            for i in range(group):
                store(k * group + i, bias[:, i * cols : (i + 1) * cols])

    for t in range(count + 3):
        gate(t - 1, 0)
        project(t - 3)
        gate(t - 1, 1)
        down(t - 2)
        gate(t - 1, 2)
        if t < count:
            normed[t] = normalise(value_of(t))
        gate(t - 1, 3)


def pair_first_kernel(pair, trans_in, trans_out, bias_weight_t, anchor, cond_out, bias_out):
    def store(i, value):
        bias_out[:, i, :] = value

    pair_block(pair, trans_in, trans_out, bias_weight_t, cond_out, store)


def pair_next_kernel(pair, trans_in, trans_out, bias_weight_t, anchor, cond, cond_out, bias_out):
    pair_first_kernel(pair, trans_in, trans_out, bias_weight_t, anchor, cond_out, bias_out)


def pair_last_kernel(
    pair, trans_in, trans_out, bias_weight_t, anchor, cond, first, second, cond_out, bias_out, held
):
    def store(i, value):
        held[:, i, :] = value

    pair_block(pair, trans_in, trans_out, bias_weight_t, cond_out, store)
    for h in range(bias_out.shape[0]):
        parts = [first[h], second[h], held[h]]
        bias_out[h] = whole(jnp.concatenate(parts, axis=0)).astype(jnp.int16)


def pair_call(kernel, step, index, inputs, extra, anchor, cond, bias_shape, scratch=(), room=56):
    pair_rep, trans_in, trans_out, bias_t = inputs
    cols = pair_rep.shape[1]
    block = pl.BlockSpec((step, cols, 128), lambda i: (index, 0, 0))
    operands = [pair_rep, trans_in, trans_out, bias_t, anchor]
    if cond is not None:
        operands.append(cond)
    count = len(operands)
    specs = [block] + [pl.BlockSpec(x.shape, lambda i: (0, 0)) for x in operands[1:4]]
    specs += [ANY] * (count - 4)
    specs += [pl.BlockSpec(x.shape, lambda i: (0, 0, 0)) for x in extra]
    return pl.pallas_call(
        kernel,
        grid=(1,),
        out_shape=(jax.ShapeDtypeStruct(pair_rep.shape, BF), bias_shape),
        in_specs=specs,
        out_specs=(block, pl.BlockSpec(bias_shape.shape, lambda i: (0, 0, 0))),
        scratch_shapes=list(scratch),
        input_output_aliases={} if cond is None else {5: 0},
        compiler_params=params(room),
        cost_estimate=pl.CostEstimate(
            flops=step * 750_000_000, bytes_accessed=step * 1_000_000, transcendentals=0
        ),
        name="pair_part",
    )(*operands, *extra)


def attend_kernel(
    core_at, head_at, z_at, queries, kv0, kv1, kv2, kv3, kv4, kv5, kv6, kv7, bias_mine, bias_other, bias_weight_t,
    update_mine, grad_other, kv
):
    core = core_at[0]
    unit = head_unit(bias_weight_t[...])
    this = lax.broadcasted_iota(jnp.int32, unit.shape, 0) == head_at[0]
    unit = jnp.sum(jnp.where(this, unit, 0.0), axis=0, keepdims=True)
    for back, block in enumerate((kv0, kv1, kv2, kv3, kv4, kv5, kv6, kv7)):
        kv[lax.rem(z_at[0] + 8 - back, 8)] = block[...]
    blocks = [core, 2 + core, 1 - core, 3 - core]
    cols = 384
    tok = 24
    rows = 8 * tok
    lane = lax.broadcasted_iota(jnp.int32, (1, 128), 1)
    is_key = lane < HEAD
    is_value = (lane >= HEAD) & (lane < 2 * HEAD)

    def decode(block):
        block = block.astype(jnp.int32).astype(F32)
        codes = block[0:1]
        at = 2 * HEAD
        first = scale_value(codes[:, at : at + 1], codes[:, at + 1 : at + 2])
        second = scale_value(codes[:, at + 2 : at + 3], codes[:, at + 3 : at + 4])
        return block * jnp.where(is_key, first, jnp.where(is_value, second, 0.0))

    bias = jnp.concatenate(
        [
            jnp.concatenate(
                [
                    (bias_mine if c < 2 else bias_other)[2 * g + c % 2].astype(jnp.int32).astype(F32)
                    for c in range(4)
                ],
                axis=1,
            )
            for g in range(8)
        ],
        axis=0,
    ) * unit
    def products_of(y, p, query_blocks, token_blocks):
        query = jnp.concatenate([b[p * tok : (p + 1) * tok] for b in query_blocks], axis=0)
        q_high, q_low = two_parts(jnp.where(is_key, query, 0.0))
        c_high, c_low = two_parts(jnp.where(is_value, query, 0.0))
        high, low = two_parts(
            jnp.concatenate([b[p * tok : (p + 1) * tok] for b in token_blocks], axis=0)
        )
        both = jnp.concatenate([high, low], axis=1)
        none = jnp.zeros_like(q_low)
        stacked = jnp.concatenate(
            [
                jnp.concatenate([q_high, q_high], axis=1),
                jnp.concatenate([q_low, none], axis=1),
                jnp.concatenate([c_high, c_high], axis=1),
                jnp.concatenate([c_low, none], axis=1),
            ],
            axis=0,
        )
        return both, dot(stacked, both, NT)

    def products_at(index):
        y, p = index // 2, index % 2
        if p == 0:
            blocks_of[y] = (
                [decode(queries[2 * g + y, :, :128]) for g in range(8)],
                [decode(kv[2 * c + z, 2 * g + y]) for c in blocks for z in range(2) for g in range(8)],
            )
        return products_of(y, p, *blocks_of[y])

    blocks_of = {}
    grad = None
    coming = products_at(0)
    for index in range(4):
        y, p = index // 2, index % 2
        both, products = coming
        if index < 3:
            coming = products_at(index + 1)
        scores = products[:rows] + products[rows : 2 * rows] + bias
        prob_grad = products[2 * rows : 3 * rows] + products[3 * rows :]
        top = jnp.max(scores, axis=-1, keepdims=True)
        weights = jnp.exp(scores - top)
        weights = weights * (1.0 / jnp.sum(weights, axis=-1, keepdims=True))
        mixed = dot(weights.astype(BF), both)
        mixed = mixed[:, :128] + mixed[:, 128:]
        for g in range(8):
            update_mine[2 * g + y, :, cols + p * HEAD : cols + (p + 1) * HEAD] = mixed[
                g * tok : (g + 1) * tok, HEAD : 2 * HEAD
            ]
        term = weights * prob_grad
        term = term - weights * jnp.sum(term, axis=-1, keepdims=True)
        grad = term if grad is None else grad + term
    for g in range(8):
        for c in range(4):
            (update_mine if c < 2 else grad_other)[2 * g + c % 2, :, :cols] = grad[
                g * tok : (g + 1) * tok, c * cols : (c + 1) * cols
            ]


def merge_kernel(mine, other, out):
    cols = other.shape[2]
    used = 2 * HEAD
    lane = lax.broadcasted_iota(jnp.int32, (1, 128), 1)
    for h in range(mine.shape[0]):
        grad = mine[h, :, :cols] + other[h]
        update = jnp.where(lane < used, mine[h, :, cols:], 0.0)
        codes = update
        scaled = []
        for at, part in ((0, grad), (2, update)):
            steps, power = grid_scale(jnp.max(jnp.abs(part), axis=-1, keepdims=True))
            scaled.append(part * (1.0 / scale_value(steps, power)))
            codes = jnp.where(lane == used + at, steps, codes)
            codes = jnp.where(lane == used + at + 1, power, codes)
        last = jnp.where(lane < used, scaled[1], codes)
        out[h] = jnp.concatenate(
            [
                whole(scaled[0][:, :256]),
                whole(jnp.concatenate([scaled[0][:, 256:], last], axis=1)),
            ],
            axis=0,
        ).astype(jnp.int16)


def normal_kernel(cond, anchor, normal_out, scale_out):
    rows, cols, lanes = cond.shape
    ones, centre = lane_matrices(lanes)
    group = 4
    for part in range(rows // group):
        value = cond[part * group : (part + 1) * group].reshape(group * cols, lanes)
        half = group * cols // 2
        centred = dot(jnp.concatenate([value[:half], value[half:]], axis=1), centre)
        scale = lax.rsqrt(lane_mean(centred * centred, ones) + epsilon)
        normal_out[part] = centred * scale
        scale_out[part] = scale


def grad_kernel(packed, normals, scales, bias_weight, out, update_out, held):
    step = pl.program_id(0)
    lanes = 128
    heads, _, rows, cols = held.shape[1], 0, held.shape[2], held.shape[3]
    tok = packed.shape[1] // 2

    @pl.when(step == 0)
    def _():
        pieces = [[], []]
        for h in range(heads):
            block = packed[h].astype(jnp.int32).astype(F32)
            low, high = block[:tok], block[tok:]
            at = lanes + 2 * HEAD
            grad_scale = scale_value(high[:, at : at + 1], high[:, at + 1 : at + 2])
            update_scale = scale_value(high[:, at + 2 : at + 3], high[:, at + 3 : at + 4])
            grad = jnp.concatenate([low, high[:, :lanes]], axis=1) * grad_scale
            for s in range(held.shape[0]):
                held[s, h] = grad[s * rows : (s + 1) * rows]
            for p in range(2):
                pieces[p].append(
                    high[:, lanes + p * HEAD : lanes + (p + 1) * HEAD] * update_scale
                )
        for p in range(2):
            update_out[p] = jnp.concatenate(pieces[p], axis=1).astype(BF)

    ones, _ = lane_matrices(lanes)
    weight = bias_weight[...].astype(F32)
    w_high, w_low = two_parts(weight - jnp.mean(weight, axis=-1, keepdims=True))
    parts = jnp.concatenate([w_high, w_high, w_high, w_low, w_low], axis=0)
    group = 4
    count = group * cols
    half = count // 2

    def paired(value):
        return jnp.concatenate([value[:half], value[half:]], axis=1)

    for part in range(rows // group):
        grad = jnp.concatenate(
            [held[step, :, part * group + i, :] for i in range(group)], axis=1
        )
        high, middle, low = three_parts(grad)
        stacked = jnp.concatenate([high, middle, low, high, middle], axis=0)
        grad_normal = paired(dot(stacked, parts, TN))
        normal = normals[step * (rows // group) + part]
        scale = scales[step * (rows // group) + part]
        result = ((grad_normal - normal * lane_mean(grad_normal * normal, ones)) * scale).astype(BF)
        result = jnp.concatenate([result[:, :lanes], result[:, lanes:]], axis=0)
        out[part * group : (part + 1) * group] = result.reshape(group, cols, lanes)


def params(mebibytes):
    return pltpu.CompilerParams(vmem_limit_bytes=mebibytes * 1024 * 1024)


VMEM = pl.BlockSpec(memory_space=pltpu.VMEM)
SMEM = pl.BlockSpec(memory_space=pltpu.SMEM)
ANY = pl.BlockSpec(memory_space=pl.ANY)


def on_device(
    pair_rep,
    single,
    atom_feat,
    coords,
    levels,
    window_offset,
    atom_token,
    trans_in,
    trans_out,
    bias_weight,
    single_weight,
    coord_weight,
    atom_weight,
    agg_weight,
    token_weight,
    noise_weight,
    cotangent,
):
    tile_index = lax.axis_index(TILE).astype(jnp.int32)
    core_index = lax.axis_index("core").astype(jnp.int32)
    copies, tok_rows, width = cotangent.shape
    atom_rows, atom_width = atom_feat.shape
    cols = pair_rep.shape[1]
    rim = K_WIN // 2
    atoms, normed, first, last = pl.pallas_call(
        start_kernel,
        out_shape=(
            jax.ShapeDtypeStruct((copies, atom_rows, atom_width), F32),
            jax.ShapeDtypeStruct((copies, atom_rows, atom_width), BF),
            jax.ShapeDtypeStruct((copies, rim, atom_width), BF),
            jax.ShapeDtypeStruct((copies, rim, atom_width), BF),
        ),
        in_specs=[SMEM] + [VMEM] * 3,
        out_specs=(VMEM,) * 4,
        compiler_params=params(56),
        cost_estimate=pl.CostEstimate(flops=1_000_000, bytes_accessed=500_000, transcendentals=0),
        name="atom_start",
    )(levels, atom_feat, coords.transpose(1, 0, 2), coord_weight)
    forward = [(i, i + 1) for i in range(63)]
    backward = [(i + 1, i) for i in range(63)]
    low = lax.ppermute(last, TILE, forward)
    high = lax.ppermute(first, TILE, backward)
    bias_t = bias_weight.T
    inputs = (pair_rep, trans_in, trans_out, bias_t)
    step = 8
    part_bias = jax.ShapeDtypeStruct((H, step, cols), F32)
    cond, bias_first = pair_call(
        pair_first_kernel, step, 0, inputs, [], last, None, part_bias
    )
    low, high, bias_first = lax.optimization_barrier((low, high, bias_first))
    packed = pl.pallas_call(
        atom_kernel,
        out_shape=jax.ShapeDtypeStruct((H, copies * tok_rows, 256), jnp.int16),
        in_specs=[SMEM] * 3 + [VMEM] * 10 + [ANY, VMEM],
        out_specs=VMEM,
        scratch_shapes=[pltpu.VMEM(token_weight.shape, BF), pltpu.SemaphoreType.DMA],
        compiler_params=params(56),
        cost_estimate=pl.CostEstimate(flops=3_000_000_000, bytes_accessed=6_000_000, transcendentals=0),
        name="atom_stage",
    )(
        tile_index[None], window_offset, levels, low, high, normed, atoms, atom_weight, agg_weight,
        atom_token, single, single_weight, noise_weight, token_weight, cotangent,
    )
    cond, bias_second = pair_call(
        pair_next_kernel, step, 1, inputs, [], packed, cond, part_bias
    )
    packed = lax.all_to_all(packed, PLANE, 0, 0, tiled=True)
    packed, bias_second = lax.optimization_barrier((packed, bias_second))
    own = packed[:, :, 128:]
    ahead = [(i, (i + 1) % 8) for i in range(8)]
    behind = [(i, (i + 7) % 8) for i in range(8)]
    rising = [own, lax.ppermute(own, "z", ahead)]
    falling = [own, lax.ppermute(own, "z", behind)]
    cond, bias = pair_call(
        pair_last_kernel, step, 2, inputs, [bias_first, bias_second], own, cond,
        jax.ShapeDtypeStruct((H, tok_rows, cols), jnp.int16), [pltpu.VMEM((H, step, cols), F32)],
    )
    rising[1], falling[1], bias = lax.optimization_barrier((rising[1], falling[1], bias))
    rising.append(lax.ppermute(rising[1], "z", ahead))
    falling.append(lax.ppermute(falling[1], "z", behind))
    rising.append(lax.ppermute(rising[2], "z", ahead))
    falling.append(lax.ppermute(falling[2], "z", behind))
    rising.append(lax.ppermute(rising[3], "z", ahead))
    steps = tok_rows // step
    bias_mine = lax.all_to_all(bias, PLANE, 0, 0, tiled=True)
    swap = [(0, 1), (1, 0)]
    bias_other = lax.ppermute(bias_mine, "core", swap)

    pieces = (tok_rows // 4, 2 * cols, 256)
    normals, scales = pl.pallas_call(
        normal_kernel,
        out_shape=(jax.ShapeDtypeStruct(pieces, F32),) * 2,
        in_specs=[VMEM, ANY],
        out_specs=(VMEM, VMEM),
        compiler_params=params(20),
        cost_estimate=pl.CostEstimate(flops=1_500_000_000, bytes_accessed=12_000_000, transcendentals=0),
        name="pair_normal",
    )(cond, rising[3])
    rising[4], normals, scales = lax.optimization_barrier((rising[4], normals, scales))
    every = rising + [falling[3], falling[2], falling[1]]
    head_index = lax.axis_index(PLANE).astype(jnp.int32)
    z_index = lax.axis_index("z").astype(jnp.int32)
    grad_mine, grad_other = pl.pallas_call(
        attend_kernel,
        out_shape=(
            jax.ShapeDtypeStruct((H, tok_rows, cols + 128), F32),
            jax.ShapeDtypeStruct((H, tok_rows, cols), F32),
        ),
        in_specs=[SMEM] * 3 + [VMEM] * 12,
        out_specs=(VMEM, VMEM),
        scratch_shapes=[pltpu.VMEM((8,) + own.shape, jnp.int16)],
        compiler_params=params(24),
        cost_estimate=pl.CostEstimate(flops=4_000_000_000, bytes_accessed=8_000_000, transcendentals=1_200_000),
        name="token_attention",
    )(
        core_index[None], head_index[None], z_index[None], packed, *every, bias_mine, bias_other, bias_t
    )
    merged = pl.pallas_call(
        merge_kernel,
        out_shape=jax.ShapeDtypeStruct((H, 2 * tok_rows, 256), jnp.int16),
        in_specs=[VMEM] * 2,
        out_specs=VMEM,
        compiler_params=params(6),
        cost_estimate=pl.CostEstimate(flops=2_000_000, bytes_accessed=2_000_000, transcendentals=0),
        name="gradient_merge",
    )(grad_mine, lax.ppermute(grad_other, "core", swap))
    merged = lax.all_to_all(merged, PLANE, 0, 0, tiled=True)
    gradient, update = pl.pallas_call(
        grad_kernel,
        grid=(steps,),
        out_shape=(
            jax.ShapeDtypeStruct(pair_rep.shape, BF),
            jax.ShapeDtypeStruct(cotangent.shape, BF),
        ),
        in_specs=[
            pl.BlockSpec(merged.shape, lambda i: (0, 0, 0)),
            VMEM,
            VMEM,
            pl.BlockSpec(bias_t.shape, lambda i: (0, 0)),
        ],
        out_specs=(
            pl.BlockSpec((step, cols, 128), lambda i: (i, 0, 0)),
            pl.BlockSpec(cotangent.shape, lambda i: (0, 0, 0)),
        ),
        scratch_shapes=[pltpu.VMEM((steps, H, step, cols), F32)],
        compiler_params=params(24),
        cost_estimate=pl.CostEstimate(flops=400_000_000, bytes_accessed=6_000_000, transcendentals=0),
        name="pair_gradient",
    )(merged, normals, scales, bias_t)
    return (update, gradient)


def solution(mesh):
    fine = Mesh(mesh.devices.reshape(8, 8, 2, 2), ("z", "g", "ylo", "core"))
    placed = (
        P(TILE, COPY, None),
        P(TILE, None),
        P(TILE, None),
        P(COPY, None, TILE),
        P(COPY),
        P(TILE),
        P(TILE),
        P(),
        P(),
        P(),
        P(),
        P(),
        P(),
        P(),
        P(),
        P(),
        P(COPY, TILE, None),
    )
    return jax.shard_map(
        on_device,
        mesh=fine,
        in_specs=placed,
        out_specs=(P(COPY, TILE, None), P(TILE, COPY, None)),
        check_vma=False,
    )
```
